256 devices in a mesh: seq: 64 (over x, z, core), head: 4 (over y).
Axes of the slice: x: 4, y: 4, z: 8, core: 2. Of those that a mesh axis runs over, the one named last changes fastest.
Arguments:
- query: bfloat16 [32768, 16, 128], P('seq', 'head'), may hold values from -6 to 6
- key: bfloat16 [32768, 16, 128], P('seq', 'head'), may hold values from -6 to 6
- value: bfloat16 [32768, 16, 128], P('seq', 'head'), may hold values from -0.5 to 0.5
- beta: float32 [16, 32768], P('head', 'seq'), may hold values from 0.1 to 2
- log_decay: float32 [16, 32768], P('head', 'seq')
- out_weight: bfloat16 [2048, 2048], P('head'), may hold values from -0.125 to 0.125
Outputs:
- mixed: bfloat16 [32768, 2048], P(('seq', 'head'))
The draws below stay inside these ranges and needn't reach their ends.
All inputs are finite; a program needn't handle non-finite values.
Results may differ from the reference program's by a relative error of at most 0.0075.
Values may be sent and summed in bfloat16 or wider, within the bound.
A program may use at most 128 MiB of HBM per device.

```python
import math
import jax
import jax.numpy as jnp
from jax import lax

HEAD_TOTAL = 16
DK = 128
DV = 128
D = 2048
TOK_DEV = 512
SEQUENCE_TOKENS = 32768


def lasting_heads(key, lasting_count):
    order = jax.random.permutation(jax.random.fold_in(key, 7), HEAD_TOTAL)
    return order < lasting_count


def draw_beta(key, part):
    lasting = lasting_heads(key, HEAD_TOTAL // 2)
    key = jax.random.fold_in(key, 1)
    key_quick, key_lasting = jax.random.split(key)
    quick = jax.random.uniform(key_quick, (HEAD_TOTAL, SEQUENCE_TOKENS), jnp.float32, 0.1, 2.0)
    kept = 2.0 - jax.random.uniform(key_lasting, (HEAD_TOTAL, SEQUENCE_TOKENS), jnp.float32) * (32.0 / SEQUENCE_TOKENS)
    return jnp.where(lasting[:, None], kept, quick)


def draw_log_decay(key, part):
    lasting = lasting_heads(key, HEAD_TOTAL // 2)
    key = jax.random.fold_in(key, 2)
    random_subkeys = jax.random.split(key, 6)
    quick_rate = jnp.exp(jax.random.uniform(random_subkeys[0], (HEAD_TOTAL,), jnp.float32, math.log(1.0 / 50.0), math.log(1.0 / 30.0)))
    lasting_rate = jax.random.uniform(random_subkeys[1], (HEAD_TOTAL,), jnp.float32, 0.25, 0.5) / SEQUENCE_TOKENS
    baseline_rate = jnp.where(lasting, lasting_rate, quick_rate)
    jitter_level = jax.random.uniform(random_subkeys[2], (HEAD_TOTAL, SEQUENCE_TOKENS), jnp.float32, 0.5, 1.5)
    processor_factor = jnp.exp(jax.random.uniform(random_subkeys[3], (HEAD_TOTAL, SEQUENCE_TOKENS // TOK_DEV, 1), jnp.float32, math.log(0.5), math.log(2.0)))
    processor_factor = jnp.broadcast_to(processor_factor, (HEAD_TOTAL, SEQUENCE_TOKENS // TOK_DEV, TOK_DEV)).reshape(HEAD_TOTAL, SEQUENCE_TOKENS)
    spike_position = jax.random.randint(random_subkeys[4], (HEAD_TOTAL, 1, 2), 0, SEQUENCE_TOKENS)
    falloff_amount = jax.random.uniform(random_subkeys[5], (HEAD_TOTAL, 1, 2), jnp.float32, math.log(0.5), math.log(0.8))
    token_position = jnp.arange(SEQUENCE_TOKENS)[None, :, None]
    spike_events = jnp.sum(jnp.where(token_position == spike_position, falloff_amount, 0.0), axis=-1)
    return spike_events - baseline_rate[:, None] * jitter_level * processor_factor


def block_scale(stream_key, extent, cuts, least, high):
    factor_of = 1.0
    for dim, shards_of in cuts:
        steps = jax.random.uniform(jax.random.fold_in(jax.random.fold_in(stream_key, 6), dim), (shards_of,), jnp.float32, least / len(cuts), high / len(cuts))
        factor_of = factor_of * jnp.repeat(jnp.exp(steps), extent[dim] // shards_of).reshape((-1,) + (1,) * (len(extent) - 1 - dim))
    return factor_of


def bell_draw(rng, extent, spread, most, pieces=(), held_as=jnp.bfloat16):
    result = spread * jax.random.normal(rng, extent, jnp.float32)
    if pieces:
        result = result * block_scale(rng, extent, pieces, -0.22, 0.18)
    return jnp.clip(result, -most, most).astype(held_as)


def setup_inputs(seed: int = 0) -> dict:
    seeds = jax.random.split(jax.random.key(seed), 7)
    query = bell_draw(seeds[0], (SEQUENCE_TOKENS, HEAD_TOTAL, DK), 1.0, 6.0, ((0, 64), (1, 4)))
    key = bell_draw(seeds[1], (SEQUENCE_TOKENS, HEAD_TOTAL, DK), 1.0, 6.0, ((0, 64), (1, 4)))
    value = bell_draw(seeds[2], (SEQUENCE_TOKENS, HEAD_TOTAL, DV), (16.0 * SEQUENCE_TOKENS ** -0.5), 0.5, ((0, 64), (1, 4)))
    beta = draw_beta(jax.random.fold_in(seeds[6], 71), 0)
    log_decay = draw_log_decay(jax.random.fold_in(seeds[6], 71), 0)
    out_weight = bell_draw(seeds[5], (HEAD_TOTAL * DV, D), (HEAD_TOTAL * DV) ** -0.5, 0.125, ((0, 4),))
    return dict(query=query, key=key, value=value, beta=beta, log_decay=log_decay, out_weight=out_weight)


def unit_rows(tensor):
    widened = tensor.astype(jnp.float32)
    return widened * lax.rsqrt(lax.optimization_barrier(jnp.sum(widened * widened, axis=-1, keepdims=True)) + 1e-06)

def reference(query, key, value, beta, log_decay, out_weight):
    queries = unit_rows(query)
    keys_all = unit_rows(key)
    values_all = value.astype(jnp.float32)
    decays = jnp.exp(log_decay).T
    strengths = beta.T

    def advance_token(running_state, token_slice):
        query_current, key_current, value_t, strength_t, decay_t = token_slice
        retrieved_values = jnp.einsum('in,inc->ic', key_current, running_state, precision=lax.Precision.HIGHEST)
        erased = running_state - strength_t[:, None, None] * key_current[:, :, None] * retrieved_values[:, None, :]
        running_state = decay_t[:, None, None] * erased + strength_t[:, None, None] * key_current[:, :, None] * value_t[:, None, :]
        output_current = jnp.einsum('in,inc->ic', query_current, running_state, precision=lax.Precision.HIGHEST)
        return (running_state, output_current)
    initial = jnp.zeros((HEAD_TOTAL, DK, DV), jnp.float32)
    final_state, per_token = lax.scan(advance_token, initial, (queries, keys_all, values_all, strengths, decays))
    attended = per_token.reshape(SEQUENCE_TOKENS, HEAD_TOTAL * DV).astype(jnp.bfloat16)
    return jnp.dot(attended, out_weight, preferred_element_type=jnp.float32).astype(jnp.bfloat16)
```

```python
import jax
import jax.numpy as jnp
from jax import lax
from jax.experimental import pallas as pl
from jax.experimental.pallas import tpu as pltpu
from jax.sharding import PartitionSpec as P

C = 128
LEVELS = (2, 4, 8, 16, 32, 64)
F32, BF16 = jnp.float32, jnp.bfloat16


def dot(a, b):
    return jnp.dot(a, b, preferred_element_type=F32)


def dot_nt(a, b, precision=None):
    return lax.dot_general(a, b, (((1,), (1,)), ((), ())), precision=precision, preferred_element_type=F32)


def halves(a):
    hi = a.astype(BF16)
    return hi, (a - hi.astype(F32)).astype(BF16)


def wide(a, b):
    return jnp.concatenate([a, b], axis=1)


def tall(a, b):
    return jnp.concatenate([a, b], axis=0)


def exact_square(a_halves, b_halves):
    row = wide(*b_halves)
    both = dot(wide(*a_halves), tall(row, row))
    return both[:, :C] + both[:, C:]


def exact_apply(a_halves, b_hi, b_lo):
    return dot(wide(*a_halves), tall(b_hi, b_hi)) + dot(a_halves[0], b_lo)


def fill_masks(masks):
    row = lax.broadcasted_iota(jnp.int32, (C, C), 0)
    col = lax.broadcasted_iota(jnp.int32, (C, C), 1)
    for i, s in enumerate((1,) + LEVELS):
        same = (row // (2 * s)) == (col // (2 * s))
        low = ((row // s) % 2 == 1) & ((col // s) % 2 == 0)
        masks[i] = jnp.where(same & low, 1.0, 0.0).astype(BF16)


def chunk_start(q, k, b_col, g_row, g_col):
    row = lax.broadcasted_iota(jnp.int32, (C, C), 0)
    col = lax.broadcasted_iota(jnp.int32, (C, C), 1)
    eye = row == col
    both = dot_nt(tall(k, q), k)
    gram, query_key = both[:C], both[C:]
    diagonal = jnp.where(eye, gram, 0.0)
    rk_row = lax.rsqrt(jnp.sum(diagonal, axis=0, keepdims=True) + 1e-06)
    rk_col = lax.rsqrt(jnp.sum(diagonal, axis=1, keepdims=True) + 1e-06)
    decay = jnp.exp(jnp.where(row >= col, g_col - g_row, -1e30)) * rk_row
    lower = jnp.where(row > col, decay * gram, 0.0) * (b_col * rk_col)
    return lower, (decay * query_key).astype(BF16), rk_row, rk_col


def invert(lowers, masks):
    row = lax.broadcasted_iota(jnp.int32, (C, C), 0)
    col = lax.broadcasted_iota(jnp.int32, (C, C), 1)
    split = [halves(a) for a in lowers]
    first = masks[0].astype(F32)
    xs = [jnp.where(row == col, 1.0, 0.0) - a * first for a in lowers]
    for i in range(len(LEVELS)):
        mask = masks[i + 1]
        xh = [halves(x) for x in xs]
        ys = [exact_square((hi * mask, lo * mask), x) for (hi, lo), x in zip(split, xh)]
        yh = [halves(y) for y in ys]
        zs = [exact_square(x, y) for x, y in zip(xh, yh)]
        xs = [x - z for x, z in zip(xs, zs)]
    return xs


def chunk_end(x, qkd, q, k, v, b_row, g_row, g_col, rk_row, rk_col):
    row = lax.broadcasted_iota(jnp.int32, (C, C), 0)
    col = lax.broadcasted_iota(jnp.int32, (C, C), 1)
    carried = dot(wide(*halves(x * b_row)), tall(v, v))
    key_factor = dot(wide(*halves(x * (b_row * jnp.exp(g_row) * rk_row))), tall(k, k))
    pair = wide(-key_factor, carried)
    g_end = g_col[C - 1 :, :]
    pair_hi, pair_lo = halves(pair * (jnp.exp(g_end - g_col) * rk_col))
    kt = k.T
    ab = dot(wide(kt, kt), tall(pair_hi, pair_lo))
    step = ab[:, :C] + jnp.where(row == col, jnp.exp(g_end), 0.0)
    added = ab[:, C:]
    qf = q.astype(F32)
    rq_col = lax.rsqrt(jnp.sum(qf * qf, axis=1, keepdims=True) + 1e-06)
    qo = dot(qkd, pair.astype(BF16))
    rows_q = (qo[:, :C] + jnp.exp(g_col) * qf) * rq_col
    rows_o = qo[:, C:] * rq_col
    return step, added, rows_q, rows_o


def head_parts(q_of, k_of, v_of, beta, decay_log, masks, put):
    row = lax.broadcasted_iota(jnp.int32, (C, C), 0)
    col = lax.broadcasted_iota(jnp.int32, (C, C), 1)
    sums = jnp.where(row <= col, 1.0, 0.0)
    logs = jnp.maximum(decay_log, -110.0)
    logs = tall(logs, logs)
    g = jnp.dot(logs, sums, precision=lax.Precision.HIGHEST, preferred_element_type=F32)
    stacked = tall(beta, g[:4])
    turned = stacked.T
    b_row = [beta[c : c + 1] for c in range(4)]
    b_col = [turned[:, c : c + 1] for c in range(4)]
    g_row = [g[c : c + 1] for c in range(4)]
    g_col = [turned[:, 4 + c : 5 + c] for c in range(4)]
    starts = [chunk_start(q_of(c), k_of(c), b_col[c], g_row[c], g_col[c]) for c in range(4)]
    xs = invert([s[0] for s in starts], masks)
    ends = [chunk_end(xs[c], starts[c][1], q_of(c), k_of(c), v_of(c), b_row[c], g_row[c], g_col[c], *starts[c][2:])
            for c in range(4)]
    state = None
    for c in range(4):
        step, added, rows_q, rows_o = ends[c]
        if state is None:
            state = wide(step, added)
        else:
            s_hi, s_lo = halves(state)
            moved = dot(rows_q.astype(BF16), s_hi)
            rows_q = moved[:, :C]
            rows_o = rows_o + moved[:, C:]
            state = exact_apply(halves(step), s_hi, s_lo) + wide(jnp.zeros((C, C), F32), added)
        put(c, rows_q, rows_o)
    return state


def k1_kernel(q_ref, k_ref, v_ref, b_ref, d_ref, qe_ref, o_ref, item_ref, masks):
    h = pl.program_id(0)

    @pl.when(h == 0)
    def _():
        fill_masks(masks)

    def four(ref):
        lines = lax.broadcasted_iota(jnp.int32, (4, 512), 0)
        mine = jnp.sum(jnp.where(lines == h, ref[...], 0.0), axis=0, keepdims=True)
        return jnp.concatenate([mine[:, c * C : (c + 1) * C] for c in range(4)], axis=0)

    def at(ref):
        return lambda c: ref[0, c * C : (c + 1) * C, :]

    def put(c, rows_q, rows_o):
        qe_ref[0, c * C : (c + 1) * C, :] = rows_q.astype(BF16)
        o_ref[0, c * C : (c + 1) * C, :] = rows_o

    state = head_parts(at(q_ref), at(k_ref), at(v_ref), four(b_ref), four(d_ref), masks, put)
    hi, lo = halves(state[:, :C])
    item_ref[0, :, :C] = hi
    item_ref[0, :, C : 2 * C] = lo
    item_ref[0, :, 2 * C :] = state[:, C:].astype(BF16)


def k1(q, k, v, b, d):
    spec = pl.BlockSpec((1, 512, 128), lambda h: (h, 0, 0))
    small = pl.BlockSpec((4, 512), lambda h: (0, 0))
    return pl.pallas_call(
        k1_kernel,
        grid=(4,),
        in_specs=[spec, spec, spec, small, small],
        out_specs=[spec, spec, pl.BlockSpec((1, 128, 384), lambda h: (h, 0, 0))],
        out_shape=[jax.ShapeDtypeStruct((4, 512, 128), BF16), jax.ShapeDtypeStruct((4, 512, 128), F32),
                   jax.ShapeDtypeStruct((4, 128, 384), BF16)],
        scratch_shapes=[pltpu.VMEM((7, C, C), BF16)],
        compiler_params=pltpu.CompilerParams(vmem_limit_bytes=48 * 2**20),
    )(q, k, v, b, d)


MESH = pl.DeviceIdType.MESH


def wide3(hi, lo, u):
    return jnp.concatenate([hi, lo, u], axis=1)


def as_item(state):
    hi, lo = halves(state[:, :C])
    return wide3(hi, lo, state[:, C:].astype(BF16))


def from_item(item):
    return wide(item[:, :C].astype(F32) + item[:, C : 2 * C].astype(F32), item[:, 2 * C :].astype(F32))


def join(later, earlier):
    hi, lo = halves(earlier)
    item_halves = (later[:, :C], later[:, C : 2 * C])
    return exact_apply(item_halves, hi, lo) + wide(jnp.zeros((C, C), F32), later[:, 2 * C :].astype(F32))


def pass_state(item, state):
    s = state.astype(BF16)
    return dot(item[:, : 2 * C], tall(s, s)) + item[:, 2 * C :].astype(F32)


def mix_kernel(item_ref, qe_ref, o_ref, w_ref, out_ref, group, pairs, rows, enters, entering, att, arrived, weight,
               total, state, w_sem, g_send, g_recv, p_send, p_recv, x_send, x_recv, e_send, e_recv, y_send, y_recv):
    seq, head = lax.axis_index("seq"), lax.axis_index("head")
    member, pair, line = seq % 4, (seq // 4) % 4, seq // 16
    base = seq - member

    def in_pairs(step):
        return line * 16 + ((pair + step + 4) % 4) * 4 + member

    barrier = pltpu.get_barrier_semaphore()
    friends = [{"seq": base + (member ^ j)} for j in (1, 2, 3)]
    friends += [{"seq": in_pairs(1)}, {"seq": in_pairs(-1)}]
    friends += [{"seq": (seq + 16 * j) % 64} for j in (1, 2, 3)]
    friends += [{"head": (head + j) % 4} for j in (1, 2, 3)]
    for friend in friends:
        pl.semaphore_signal(barrier, inc=1, device_id=friend, device_id_type=MESH)
    load = pltpu.make_async_copy(w_ref, weight, w_sem)
    load.start()
    pl.semaphore_wait(barrier, len(friends))

    def send(source, target, send_sem, recv_sem, to):
        copy = pltpu.make_async_remote_copy(source, target, send_sem, recv_sem, device_id=to, device_id_type=MESH)
        copy.start()
        return copy

    to_group = []
    for j in (1, 2, 3):
        other = member ^ j
        to_group.append(send(item_ref.at[other], group.at[member], g_send.at[j], g_recv.at[j], {"seq": base + other}))
    group[pl.ds(member, 1)] = item_ref[pl.ds(member, 1)]
    for copy in to_group:
        copy.wait()
    early = join(group[1], from_item(group[0]))
    late = as_item(join(group[3], from_item(group[2])))
    pairs[0] = as_item(join(late, early))

    up = send(pairs.at[0], pairs.at[3], p_send.at[0], p_recv.at[0], {"seq": in_pairs(1)})
    down = send(pairs.at[0], pairs.at[1], p_send.at[1], p_recv.at[1], {"seq": in_pairs(-1)})
    up.wait_recv()
    up2 = send(pairs.at[3, :64], pairs.at[2, :64], p_send.at[2], p_recv.at[2], {"seq": in_pairs(1)})
    down.wait_recv()
    down2 = send(pairs.at[1, 64:], pairs.at[2, 64:], p_send.at[3], p_recv.at[3], {"seq": in_pairs(-1)})
    up.wait_send()
    down.wait_send()
    up2.wait()
    down2.wait()
    eye = jnp.where(
        lax.broadcasted_iota(jnp.int32, (C, 2 * C), 0) == lax.broadcasted_iota(jnp.int32, (C, 2 * C), 1), 1.0, 0.0)
    run = from_item(pairs[(4 - pair) % 4])
    before = jnp.where(pair == 0, eye, run)
    for j in (1, 2, 3):
        run = join(pairs[(j + 4 - pair) % 4], run)
        if j < 3:
            before = jnp.where(pair > j, run, before)

    rows[pl.ds(line, 1)] = run.astype(BF16)[None]
    for j in (1, 2, 3):
        @pl.when(line + j < 4)
        def _():
            send(rows.at[line], rows.at[line], x_send.at[j], x_recv.at[j], {"seq": seq + 16 * j})

    def line_copy(j):
        return pltpu.make_async_remote_copy(rows.at[line], rows.at[line], x_send.at[j], x_recv.at[j],
                                            device_id={"seq": (seq + 16 * j) % 64}, device_id_type=MESH)

    state[...] = jnp.zeros((C, C), F32)
    for j in (3, 2, 1):
        @pl.when(line - j >= 0)
        def _():
            line_copy(j).wait_recv()
            there = rows[line - j]
            state[...] = dot(there[:, :C], state[...].astype(BF16)) + there[:, C:].astype(F32)

    entry = dot(wide(*halves(before[:, :C])), tall(state[...].astype(BF16), state[...].astype(BF16))) + before[:, C:]
    for i in range(4):
        enters[i] = entry.astype(BF16)
        if i < 3:
            entry = pass_state(group[i], entry)
    to_members = []
    for j in (1, 2, 3):
        other = member ^ j
        to_members.append(
            send(enters.at[other], entering.at[member], e_send.at[j], e_recv.at[j], {"seq": base + other}))
    entering[pl.ds(member, 1)] = enters[pl.ds(member, 1)]
    for j in (1, 2, 3):
        @pl.when(line + j < 4)
        def _():
            line_copy(j).wait_send()
    for copy in to_members:
        copy.wait()

    for h in range(4):
        mine = dot(qe_ref[h], entering[h]) + o_ref[h]
        for t in range(4):
            att[t, :, h * C : (h + 1) * C] = mine[t * C : (t + 1) * C].astype(BF16)
    over = []
    for j in (1, 2, 3):
        other = (head + j) % 4
        over.append(send(att.at[other], arrived.at[j], y_send.at[j], y_recv.at[j], {"head": other}))
    load.wait()
    for n in range(4):
        cols = slice(n * 512, (n + 1) * 512)
        total[:, cols] = dot(att[head], weight[head, :, cols])
    for j in (1, 3, 2):
        over[j - 1].wait()
        for n in range(4):
            cols = slice(n * 512, (n + 1) * 512)
            more = total[:, cols] + dot(arrived[j], weight[(head + 4 - j) % 4, :, cols])
            if j == 2:
                out_ref[:, cols] = more.astype(BF16)
            else:
                total[:, cols] = more


def mix(item, qe, o, w):
    vmem = pl.BlockSpec(memory_space=pltpu.VMEM)
    dma = pltpu.SemaphoreType.DMA((4,))
    return pl.pallas_call(
        mix_kernel,
        out_shape=jax.ShapeDtypeStruct((128, 2048), BF16),
        in_specs=[vmem, vmem, vmem, pl.BlockSpec(memory_space=pl.ANY)],
        out_specs=vmem,
        scratch_shapes=[
            pltpu.VMEM((4, C, 3 * C), BF16),
            pltpu.VMEM((4, C, 3 * C), BF16),
            pltpu.VMEM((4, C, 2 * C), BF16),
            pltpu.VMEM((4, C, C), BF16),
            pltpu.VMEM((4, C, C), BF16),
            pltpu.VMEM((4, C, 512), BF16),
            pltpu.VMEM((4, C, 512), BF16),
            pltpu.VMEM((4, 512, 2048), BF16),
            pltpu.VMEM((C, 2048), F32),
            pltpu.VMEM((C, C), F32),
            pltpu.SemaphoreType.DMA,
        ] + [dma] * 10,
        compiler_params=pltpu.CompilerParams(
            collective_id=0, has_side_effects=True, vmem_limit_bytes=48 * 2**20),
    )(item, qe, o, w)


def body(query, key, value, beta, log_decay, out_weight):
    weight = lax.all_gather(out_weight, "head")
    turn = lambda a: a.transpose(1, 0, 2)
    qe, o, item = k1(turn(query), turn(key), turn(value), beta, log_decay)
    return mix(item, qe, o, weight)


def solution(mesh):
    in_specs = (
        P("seq", "head", None),
        P("seq", "head", None),
        P("seq", "head", None),
        P("head", "seq"),
        P("head", "seq"),
        P("head", None),
    )
    out_specs = P(("seq", "head"), None)
    return jax.shard_map(body, mesh=mesh, in_specs=in_specs, out_specs=out_specs, check_vma=False)
```

```python
import jax
import jax.numpy as jnp
from jax import lax
from jax.experimental import pallas as pl
from jax.experimental.pallas import tpu as pltpu
from jax.sharding import PartitionSpec as P

C = 128
LEVELS = (2, 4, 8, 16, 32, 64)
F32, BF16 = jnp.float32, jnp.bfloat16


def dot(a, b):
    return jnp.dot(a, b, preferred_element_type=F32)


def dot_nt(a, b, precision=None):
    return lax.dot_general(a, b, (((1,), (1,)), ((), ())), precision=precision, preferred_element_type=F32)


def halves(a):
    hi = a.astype(BF16)
    return hi, (a - hi.astype(F32)).astype(BF16)


def wide(a, b):
    return jnp.concatenate([a, b], axis=1)


def tall(a, b):
    return jnp.concatenate([a, b], axis=0)


def exact_square(a_halves, b_halves):
    row = wide(*b_halves)
    both = dot(wide(*a_halves), tall(row, row))
    return both[:, :C] + both[:, C:]


def exact_apply(a_halves, b_hi, b_lo):
    return dot(wide(*a_halves), tall(b_hi, b_hi)) + dot(a_halves[0], b_lo)


def fill_masks(masks):
    row = lax.broadcasted_iota(jnp.int32, (C, C), 0)
    col = lax.broadcasted_iota(jnp.int32, (C, C), 1)
    for i, s in enumerate((1,) + LEVELS):
        same = (row // (2 * s)) == (col // (2 * s))
        low = ((row // s) % 2 == 1) & ((col // s) % 2 == 0)
        masks[i] = jnp.where(same & low, 1.0, 0.0).astype(BF16)


def chunk_start(q, k, b_col, g_row, g_col):
    row = lax.broadcasted_iota(jnp.int32, (C, C), 0)
    col = lax.broadcasted_iota(jnp.int32, (C, C), 1)
    eye = row == col
    both = dot_nt(tall(k, q), k)
    gram, query_key = both[:C], both[C:]
    diagonal = jnp.where(eye, gram, 0.0)
    rk_row = lax.rsqrt(jnp.sum(diagonal, axis=0, keepdims=True) + 1e-06)
    rk_col = lax.rsqrt(jnp.sum(diagonal, axis=1, keepdims=True) + 1e-06)
    decay = jnp.exp(jnp.where(row >= col, g_col - g_row, -1e30)) * rk_row
    lower = jnp.where(row > col, decay * gram, 0.0) * (b_col * rk_col)
    return lower, (decay * query_key).astype(BF16), rk_row, rk_col


def invert(lowers, masks):
    row = lax.broadcasted_iota(jnp.int32, (C, C), 0)
    col = lax.broadcasted_iota(jnp.int32, (C, C), 1)
    split = [halves(a) for a in lowers]
    first = masks[0].astype(F32)
    xs = [jnp.where(row == col, 1.0, 0.0) - a * first for a in lowers]
    for i in range(len(LEVELS)):
        mask = masks[i + 1]
        xh = [halves(x) for x in xs]
        ys = [exact_square((hi * mask, lo * mask), x) for (hi, lo), x in zip(split, xh)]
        yh = [halves(y) for y in ys]
        zs = [exact_square(x, y) for x, y in zip(xh, yh)]
        xs = [x - z for x, z in zip(xs, zs)]
    return xs


def chunk_end(x, qkd, q, k, v, b_row, g_row, g_col, rk_row, rk_col):
    row = lax.broadcasted_iota(jnp.int32, (C, C), 0)
    col = lax.broadcasted_iota(jnp.int32, (C, C), 1)
    carried = dot(wide(*halves(x * b_row)), tall(v, v))
    key_factor = dot(wide(*halves(x * (b_row * jnp.exp(g_row) * rk_row))), tall(k, k))
    pair = wide(-key_factor, carried)
    g_end = g_col[C - 1 :, :]
    pair_hi, pair_lo = halves(pair * (jnp.exp(g_end - g_col) * rk_col))
    kt = k.T
    ab = dot(wide(kt, kt), tall(pair_hi, pair_lo))
    step = ab[:, :C] + jnp.where(row == col, jnp.exp(g_end), 0.0)
    added = ab[:, C:]
    qf = q.astype(F32)
    rq_col = lax.rsqrt(jnp.sum(qf * qf, axis=1, keepdims=True) + 1e-06)
    qo = dot(qkd, pair.astype(BF16))
    rows_q = (qo[:, :C] + jnp.exp(g_col) * qf) * rq_col
    rows_o = qo[:, C:] * rq_col
    return step, added, rows_q, rows_o


def head_parts(q_of, k_of, v_of, beta, decay_log, masks, put):
    row = lax.broadcasted_iota(jnp.int32, (C, C), 0)
    col = lax.broadcasted_iota(jnp.int32, (C, C), 1)
    sums = jnp.where(row <= col, 1.0, 0.0)
    logs = jnp.maximum(decay_log, -110.0)
    logs = tall(logs, logs)
    g = jnp.dot(logs, sums, precision=lax.Precision.HIGHEST, preferred_element_type=F32)
    stacked = tall(beta, g[:4])
    turned = stacked.T
    b_row = [beta[c : c + 1] for c in range(4)]
    b_col = [turned[:, c : c + 1] for c in range(4)]
    g_row = [g[c : c + 1] for c in range(4)]
    g_col = [turned[:, 4 + c : 5 + c] for c in range(4)]
    starts = [chunk_start(q_of(c), k_of(c), b_col[c], g_row[c], g_col[c]) for c in range(4)]
    xs = invert([s[0] for s in starts], masks)
    ends = [chunk_end(xs[c], starts[c][1], q_of(c), k_of(c), v_of(c), b_row[c], g_row[c], g_col[c], *starts[c][2:])
            for c in range(4)]
    state = None
    for c in range(4):
        step, added, rows_q, rows_o = ends[c]
        if state is None:
            state = wide(step, added)
        else:
            s_hi, s_lo = halves(state)
            moved = dot(rows_q.astype(BF16), s_hi)
            rows_q = moved[:, :C]
            rows_o = rows_o + moved[:, C:]
            state = exact_apply(halves(step), s_hi, s_lo) + wide(jnp.zeros((C, C), F32), added)
        put(c, rows_q, rows_o)
    return state


MESH = pl.DeviceIdType.MESH


def as_item(state):
    hi, lo = halves(state[:, :C])
    return jnp.concatenate([hi, lo, state[:, C:].astype(BF16)], axis=1)


def from_item(item):
    return wide(item[:, :C].astype(F32) + item[:, C : 2 * C].astype(F32), item[:, 2 * C :].astype(F32))


def join(later, earlier):
    hi, lo = halves(earlier)
    return exact_apply((later[:, :C], later[:, C : 2 * C]), hi, lo) + wide(
        jnp.zeros((C, C), F32), later[:, 2 * C :].astype(F32))


def pass_state(item, state):
    return exact_square((item[:, :C], item[:, C : 2 * C]), halves(state)) + item[:, 2 * C :].astype(F32)


def layer_kernel(q_ref, k_ref, v_ref, b_ref, d_ref, w_ref, out_ref,
                 masks, qe, own, items, group, pairs, rows, enters, entering, att, arrived, weight, total, state,
                 w_load, w_send, w_recv, g_send, g_recv, p_send, p_recv, x_send, x_recv, e_send, e_recv,
                 y_send, y_recv):
    seq, head = lax.axis_index("seq"), lax.axis_index("head")
    member, pair, line = seq % 4, (seq // 4) % 4, seq // 16
    core = seq % 2
    base = seq - member
    right, left, across = (head + 1) % 4, (head + 3) % 4, (head + 2) % 4

    def in_pairs(step):
        return line * 16 + ((pair + step) % 4) * 4 + member

    barrier = pltpu.get_barrier_semaphore()
    friends = [{"seq": base + (member ^ j)} for j in (1, 2, 3)]
    friends += [{"seq": in_pairs(j)} for j in (1, 2, 3)]
    friends += [{"seq": (seq + 16 * j) % 64} for j in (1, 2, 3)]
    friends += [{"head": (head + j) % 4} for j in (1, 2, 3)]
    for friend in friends:
        pl.semaphore_signal(barrier, inc=1, device_id=friend, device_id_type=MESH)
    load = pltpu.make_async_copy(w_ref, weight.at[head], w_load)
    load.start()
    fill_masks(masks)
    load.wait()
    pl.semaphore_wait(barrier, len(friends))

    def copy_to(source, target, send_sem, recv_sem, to):
        return pltpu.make_async_remote_copy(source, target, send_sem, recv_sem, device_id=to, device_id_type=MESH)

    def quarter(of, part):
        return weight.at[of, 2 * core + part]

    sibling = {"seq": seq ^ 1}
    to_right, to_left = {"head": right}, {"head": left}
    ra = lambda of: copy_to(quarter(of, 0), quarter(of, 0), w_send.at[0], w_recv.at[0], to_right)
    lb = lambda of: copy_to(quarter(of, 1), quarter(of, 1), w_send.at[1], w_recv.at[1], to_left)
    rb = lambda of: copy_to(quarter(of, 1), quarter(of, 1), w_send.at[2], w_recv.at[2], to_right)
    la = lambda of: copy_to(quarter(of, 0), quarter(of, 0), w_send.at[3], w_recv.at[3], to_left)
    ra2 = lambda of: copy_to(quarter(of, 0), quarter(of, 0), w_send.at[4], w_recv.at[4], to_right)
    lb2 = lambda of: copy_to(quarter(of, 1), quarter(of, 1), w_send.at[5], w_recv.at[5], to_left)

    def over(of, part, i):
        return copy_to(quarter(of, part), quarter(of, part), w_send.at[6 + i], w_recv.at[6 + i], sibling)

    ra(head).start()
    lb(head).start()
    rb(head).start()
    la(head).start()

    def item_copy(h):
        return copy_to(items.at[h], group.at[member], g_send.at[h], g_recv.at[member], {"seq": base + h})

    def pair_copy(j):
        return copy_to(pairs.at[0], pairs.at[4 - j], p_send.at[j], p_recv.at[j], {"seq": in_pairs(j)})

    def line_copy(j):
        return copy_to(rows.at[line], rows.at[line], x_send.at[j], x_recv.at[j], {"seq": (seq + 16 * j) % 64})

    def from_group():
        for j in (1, 2, 3):
            other = member ^ j
            copy_to(group.at[other], group.at[other], g_send.at[other], g_recv.at[other],
                    {"seq": base + other}).wait_recv()
        early = join(group[1], from_item(group[0]))
        late = as_item(join(group[3], from_item(group[2])))
        pairs[0] = as_item(join(late, early))
        for j in (1, 3, 2):
            pair_copy(j).start()

    def one_head(h, _):
        def four(ref):
            lines = lax.broadcasted_iota(jnp.int32, (4, 512), 0)
            mine = jnp.sum(jnp.where(lines == h, ref[...], 0.0), axis=0, keepdims=True)
            return jnp.concatenate([mine[:, c * C : (c + 1) * C] for c in range(4)], axis=0)

        def at(ref):
            return lambda c: ref[h, c * C : (c + 1) * C, :]

        def put(c, rows_q, rows_o):
            qe[h, c * C : (c + 1) * C, :] = rows_q.astype(BF16)
            own[h, c * C : (c + 1) * C, :] = rows_o

        items[h] = as_item(head_parts(at(q_ref), at(k_ref), at(v_ref), four(b_ref), four(d_ref), masks, put))

        @pl.when(h != member)
        def _():
            item_copy(h).start()

        @pl.when(h == member)
        def _():
            group[h] = items[h]

        @pl.when((h == member + 1) & (h < 3))
        def _():
            from_group()

        @pl.when(h == 2)
        def _():
            ra(left).wait_recv()
            ra2(left).start()
            lb(right).wait_recv()
            lb2(right).start()
            over(left, 0, 0).start()
            over(right, 1, 1).start()

        return 0

    lax.fori_loop(0, 4, one_head, 0)

    @pl.when(member >= 2)
    def _():
        from_group()

    for j in (1, 3, 2):
        pair_copy(j).wait_recv()
    eye = jnp.where(
        lax.broadcasted_iota(jnp.int32, (C, 2 * C), 0) == lax.broadcasted_iota(jnp.int32, (C, 2 * C), 1), 1.0, 0.0)
    run = from_item(pairs[(4 - pair) % 4])
    before = jnp.where(pair == 0, eye, run)
    for j in (1, 2, 3):
        run = join(pairs[(j + 4 - pair) % 4], run)
        if j < 3:
            before = jnp.where(pair > j, run, before)

    rows[line] = as_item(run)
    for j in (1, 2, 3):
        @pl.when(line + j < 4)
        def _():
            line_copy(j).start()

    rb(left).wait_recv()
    over(left, 1, 2).start()
    la(right).wait_recv()
    over(right, 0, 3).start()
    state[...] = jnp.zeros((C, C), F32)
    for j in (3, 2, 1):
        @pl.when(line - j >= 0)
        def _():
            line_copy(j).wait_recv()
            state[...] = pass_state(rows[line - j], state[...])

    entry = exact_square(halves(before[:, :C]), halves(state[...])) + before[:, C:]
    for i in range(4):
        enters[i] = entry.astype(BF16)
        if i < 3:
            entry = pass_state(group[i], entry)

    def enter_copy(j):
        other = member ^ j
        return copy_to(enters.at[other], entering.at[member], e_send.at[other], e_recv.at[member],
                       {"seq": base + other})

    for j in (1, 2, 3):
        enter_copy(j).start()
    entering[member] = enters[member]

    def out_copy(p, j):
        return copy_to(att.at[p, (head + j) % 4], arrived.at[p, j], y_send.at[p, j], y_recv.at[p, j],
                       {"head": (head + j) % 4})

    for h in range(4):
        @pl.when(member != h)
        def _():
            copy_to(entering.at[h], entering.at[h], e_send.at[h], e_recv.at[h], {"seq": base + h}).wait_recv()
        mine = dot(qe[h], entering[h]) + own[h]
        for t in range(4):
            att[h // 2, t, :, (h % 2) * C : (h % 2 + 1) * C] = mine[t * C : (t + 1) * C].astype(BF16)
        if h % 2 == 1:
            for j in (2, 1, 3):
                out_copy(h // 2, j).start()

    ra2(across).wait_recv()
    over(across, 0, 4).start()
    lb2(across).wait_recv()
    over(across, 1, 5).start()
    ra(head).wait_send()
    lb(head).wait_send()
    rb(head).wait_send()
    la(head).wait_send()
    ra2(left).wait_send()
    lb2(right).wait_send()

    def other_half(of, part):
        return weight.at[of, 2 * (1 - core) + part]

    for i, (of, part) in enumerate(((left, 0), (right, 1), (left, 1), (right, 0), (across, 0), (across, 1))):
        over(of, part, i).wait_send()
        copy_to(other_half(of, part), other_half(of, part), w_send.at[6 + i], w_recv.at[6 + i], sibling).wait_recv()
    for j in (1, 2, 3):
        item_copy(member ^ j).wait_send()
        pair_copy(j).wait_send()
        enter_copy(j).wait_send()

        @pl.when(line + j < 4)
        def _():
            line_copy(j).wait_send()

    def product(left_side, of, p, cols):
        w = jnp.concatenate([weight[of, 2 * p, :, cols], weight[of, 2 * p + 1, :, cols]], axis=0)
        return dot(left_side, w)

    for p in range(2):
        for j in (0, 1, 3, 2):
            if j:
                out_copy(p, j).wait()
            for n in range(4):
                cols = slice(n * 512, (n + 1) * 512)
                part = att[p, head] if j == 0 else arrived[p, j]
                more = product(part, (head + 4 - j) % 4, p, cols)
                if p or j:
                    more = total[:, cols] + more
                if p == 1 and j == 2:
                    out_ref[:, cols] = more.astype(BF16)
                else:
                    total[:, cols] = more


def layer(q, k, v, b, d, w):
    vmem = pl.BlockSpec(memory_space=pltpu.VMEM)
    dma = pltpu.SemaphoreType.DMA
    return pl.pallas_call(
        layer_kernel,
        out_shape=jax.ShapeDtypeStruct((128, 2048), BF16),
        in_specs=[vmem] * 5 + [pl.BlockSpec(memory_space=pl.ANY)],
        out_specs=vmem,
        scratch_shapes=[
            pltpu.VMEM((7, C, C), BF16),
            pltpu.VMEM((4, 512, C), BF16),
            pltpu.VMEM((4, 512, C), F32),
            pltpu.VMEM((4, C, 3 * C), BF16),
            pltpu.VMEM((4, C, 3 * C), BF16),
            pltpu.VMEM((4, C, 3 * C), BF16),
            pltpu.VMEM((4, C, 3 * C), BF16),
            pltpu.VMEM((4, C, C), BF16),
            pltpu.VMEM((4, C, C), BF16),
            pltpu.VMEM((2, 4, C, 2 * C), BF16),
            pltpu.VMEM((2, 4, C, 2 * C), BF16),
            pltpu.VMEM((4, 4, C, 2048), BF16),
            pltpu.VMEM((C, 2048), F32),
            pltpu.VMEM((C, C), F32),
            dma, dma((12,)), dma((12,)),
        ] + [dma((4,))] * 8 + [dma((2, 4))] * 2,
        compiler_params=pltpu.CompilerParams(
            collective_id=0, has_side_effects=True, vmem_limit_bytes=56 * 2**20),
    )(q, k, v, b, d, w)


def body(query, key, value, beta, log_decay, out_weight):
    turn = lambda a: a.transpose(1, 0, 2)
    return layer(turn(query), turn(key), turn(value), beta, log_decay, out_weight.reshape(4, C, 2048))


def solution(mesh):
    in_specs = (
        P("seq", "head", None),
        P("seq", "head", None),
        P("seq", "head", None),
        P("head", "seq"),
        P("head", "seq"),
        P("head", None),
    )
    out_specs = P(("seq", "head"), None)
    return jax.shard_map(body, mesh=mesh, in_specs=in_specs, out_specs=out_specs, check_vma=False)
```

```python
import jax
import jax.numpy as jnp
from jax import lax
from jax.experimental import pallas as pl
from jax.experimental.pallas import tpu as pltpu
from jax.sharding import PartitionSpec as P

C = 128
LEVELS = (2, 4, 8, 16, 32, 64)
F32, BF16 = jnp.float32, jnp.bfloat16


def dot(a, b):
    return jnp.dot(a, b, preferred_element_type=F32)


def dot_nt(a, b, precision=None):
    return lax.dot_general(a, b, (((1,), (1,)), ((), ())), precision=precision, preferred_element_type=F32)


def halves(a):
    hi = a.astype(BF16)
    return hi, (a - hi.astype(F32)).astype(BF16)


def wide(a, b):
    return jnp.concatenate([a, b], axis=1)


def tall(a, b):
    return jnp.concatenate([a, b], axis=0)


def exact_square(a_halves, b_halves):
    row = wide(*b_halves)
    both = dot(wide(*a_halves), tall(row, row))
    return both[:, :C] + both[:, C:]


def exact_apply(a_halves, b_hi, b_lo):
    return dot(wide(*a_halves), tall(b_hi, b_hi)) + dot(a_halves[0], b_lo)


def fill_masks(masks):
    row = lax.broadcasted_iota(jnp.int32, (C, C), 0)
    col = lax.broadcasted_iota(jnp.int32, (C, C), 1)
    apart = jnp.where(row > col, row ^ col, 0)
    for i, s in enumerate((1,) + LEVELS):
        masks[i] = jnp.where((apart >= s) & (apart < 2 * s), 1.0, 0.0).astype(BF16)


def chunk_start(q, k, b_col, g_row, g_col):
    row = lax.broadcasted_iota(jnp.int32, (C, C), 0)
    col = lax.broadcasted_iota(jnp.int32, (C, C), 1)
    eye = row == col
    both = dot_nt(tall(k, q), k)
    gram, query_key = both[:C], both[C:]
    diagonal = jnp.where(eye, gram, 0.0)
    rk_row = lax.rsqrt(jnp.sum(diagonal, axis=0, keepdims=True) + 1e-06)
    rk_col = lax.rsqrt(jnp.sum(diagonal, axis=1, keepdims=True) + 1e-06)
    decay = jnp.exp(jnp.where(row >= col, g_col - g_row, -1e30)) * rk_row
    lower = jnp.where(row > col, decay * gram, 0.0) * (b_col * rk_col)
    return lower, halves(decay * query_key), rk_row, rk_col


def invert(lowers, masks):
    row = lax.broadcasted_iota(jnp.int32, (C, C), 0)
    col = lax.broadcasted_iota(jnp.int32, (C, C), 1)
    split = [halves(a) for a in lowers]
    first = masks[0].astype(F32)
    xs = [jnp.where(row == col, 1.0, 0.0) - a * first for a in lowers]
    for i in range(len(LEVELS)):
        mask = masks[i + 1]
        xh = [halves(x) for x in xs]
        ys = [exact_square((hi * mask, lo * mask), x) for (hi, lo), x in zip(split, xh)]
        yh = [halves(y) for y in ys]
        zs = [exact_square(x, y) for x, y in zip(xh, yh)]
        xs = [x - z for x, z in zip(xs, zs)]
    return xs


def chunk_end(x, qkd, q, k, v, b_row, g_row, g_col, rk_row, rk_col):
    row = lax.broadcasted_iota(jnp.int32, (C, C), 0)
    col = lax.broadcasted_iota(jnp.int32, (C, C), 1)
    carried = dot(wide(*halves(x * b_row)), tall(v, v))
    key_factor = dot(wide(*halves(x * (b_row * jnp.exp(g_row) * rk_row))), tall(k, k))
    pair = wide(-key_factor, carried)
    g_end = g_col[C - 1 :, :]
    pair_hi, pair_lo = halves(pair * (jnp.exp(g_end - g_col) * rk_col))
    kt = k.T
    ab = dot(wide(kt, kt), tall(pair_hi, pair_lo))
    step = ab[:, :C] + jnp.where(row == col, jnp.exp(g_end), 0.0)
    added = ab[:, C:]
    qf = q.astype(F32)
    rq_col = lax.rsqrt(jnp.sum(qf * qf, axis=1, keepdims=True) + 1e-06)
    qo = exact_apply(qkd, *halves(pair))
    rows_q = (qo[:, :C] + jnp.exp(g_col) * qf) * rq_col
    rows_o = qo[:, C:] * rq_col
    return step, added, rows_q, rows_o


def head_parts(q_of, k_of, v_of, beta, decay_log, masks, put):
    row = lax.broadcasted_iota(jnp.int32, (C, C), 0)
    col = lax.broadcasted_iota(jnp.int32, (C, C), 1)
    sums = jnp.where(row <= col, 1.0, 0.0)
    logs = jnp.maximum(decay_log, -110.0)
    logs = tall(logs, logs)
    g = jnp.dot(logs, sums, precision=lax.Precision.HIGHEST, preferred_element_type=F32)
    stacked = tall(beta, g[:4])
    turned = stacked.T
    b_row = [beta[c : c + 1] for c in range(4)]
    b_col = [turned[:, c : c + 1] for c in range(4)]
    g_row = [g[c : c + 1] for c in range(4)]
    g_col = [turned[:, 4 + c : 5 + c] for c in range(4)]
    starts = [chunk_start(q_of(c), k_of(c), b_col[c], g_row[c], g_col[c]) for c in range(4)]
    xs = invert([s[0] for s in starts], masks)
    ends = [chunk_end(xs[c], starts[c][1], q_of(c), k_of(c), v_of(c), b_row[c], g_row[c], g_col[c], *starts[c][2:])
            for c in range(4)]
    state = None
    for c in range(4):
        step, added, rows_q, rows_o = ends[c]
        if state is None:
            state = wide(step, added)
        else:
            s_hi, s_lo = halves(state)
            moved = exact_apply(halves(rows_q), s_hi, s_lo)
            rows_q = moved[:, :C]
            rows_o = rows_o + moved[:, C:]
            state = exact_apply(halves(step), s_hi, s_lo) + wide(jnp.zeros((C, C), F32), added)
        put(c, rows_q, rows_o)
    return state


MESH = pl.DeviceIdType.MESH


def as_item(state):
    hi, lo = halves(state[:, :C])
    return jnp.concatenate([hi, lo, state[:, C:].astype(BF16)], axis=1)


def from_item(item):
    return wide(item[:, :C].astype(F32) + item[:, C : 2 * C].astype(F32), item[:, 2 * C :].astype(F32))


def join(later, earlier):
    hi, lo = halves(earlier)
    return exact_apply((later[:, :C], later[:, C : 2 * C]), hi, lo) + wide(
        jnp.zeros((C, C), F32), later[:, 2 * C :].astype(F32))


def pass_state(item, state):
    return exact_square((item[:, :C], item[:, C : 2 * C]), halves(state)) + item[:, 2 * C :].astype(F32)


def layer_kernel(q_in, k_in, v_in, b_in, d_in, w_ref, out_ref,
                 q_ref, k_ref, v_ref, b_ref, d_ref, masks, qs, ks, vs, qe, own, items, group, pairs, rows, enters, entering, att, arrived, weight,
                 total, prefix, state,
                 in_load, w_load, w_send, w_recv, g_send, g_recv, p_send, p_recv, x_send, x_recv, e_send, e_recv,
                 y_send, y_recv):
    seq, head = lax.axis_index("seq"), lax.axis_index("head")
    member, pair, line = seq % 4, (seq // 4) % 4, seq // 16
    core = seq % 2
    base = seq - member
    right, left, across = (head + 1) % 4, (head + 3) % 4, (head + 2) % 4

    def in_pairs(step):
        return line * 16 + ((pair + step) % 4) * 4 + member

    barrier = pltpu.get_barrier_semaphore()
    friends = [{"seq": base + (member ^ j)} for j in (1, 2, 3)]
    friends += [{"seq": in_pairs(j)} for j in (1, 2, 3)]
    friends += [{"seq": (seq + 16 * j) % 64} for j in (1, 2, 3)]
    friends += [{"head": (head + j) % 4} for j in (1, 2, 3)]
    for friend in friends:
        pl.semaphore_signal(barrier, inc=1, device_id=friend, device_id_type=MESH)
    load = pltpu.make_async_copy(w_ref, weight.at[head], w_load)
    load.start()
    loads = [pltpu.make_async_copy(source, target, in_load.at[i]) for i, (source, target) in enumerate(
        ((q_in, q_ref), (k_in, k_ref), (v_in, v_ref), (b_in, b_ref), (d_in, d_ref)))]
    for copy in loads:
        copy.start()
    fill_masks(masks)
    for copy in loads:
        copy.wait()
    for source, target in ((q_ref, qs), (k_ref, ks), (v_ref, vs)):
        target[...] = source[...].astype(F32).reshape(2048, C)
    load.wait()
    pl.semaphore_wait(barrier, len(friends))

    def copy_to(source, target, send_sem, recv_sem, to):
        return pltpu.make_async_remote_copy(source, target, send_sem, recv_sem, device_id=to, device_id_type=MESH)

    def quarter(of, part):
        return weight.at[of, 2 * core + part]

    sibling = {"seq": seq ^ 1}
    to_right, to_left = {"head": right}, {"head": left}
    ra = lambda of: copy_to(quarter(of, 0), quarter(of, 0), w_send.at[0], w_recv.at[0], to_right)
    lb = lambda of: copy_to(quarter(of, 1), quarter(of, 1), w_send.at[1], w_recv.at[1], to_left)
    rb = lambda of: copy_to(quarter(of, 1), quarter(of, 1), w_send.at[2], w_recv.at[2], to_right)
    la = lambda of: copy_to(quarter(of, 0), quarter(of, 0), w_send.at[3], w_recv.at[3], to_left)
    ra2 = lambda of: copy_to(quarter(of, 0), quarter(of, 0), w_send.at[4], w_recv.at[4], to_right)
    lb2 = lambda of: copy_to(quarter(of, 1), quarter(of, 1), w_send.at[5], w_recv.at[5], to_left)

    def over(of, part, i):
        return copy_to(quarter(of, part), quarter(of, part), w_send.at[6 + i], w_recv.at[6 + i], sibling)

    ra(head).start()
    lb(head).start()
    rb(head).start()
    la(head).start()

    def item_copy(h):
        return copy_to(items.at[h], group.at[member], g_send.at[h], g_recv.at[member], {"seq": base + h})

    def pair_copy(j):
        return copy_to(pairs.at[0], pairs.at[4 - j], p_send.at[j], p_recv.at[j], {"seq": in_pairs(j)})

    def line_copy(j):
        return copy_to(rows.at[line], rows.at[line], x_send.at[j], x_recv.at[j], {"seq": (seq + 16 * j) % 64})

    def enter_copy(j):
        other = member ^ j
        return copy_to(enters.at[other], entering.at[member], e_send.at[other], e_recv.at[member],
                       {"seq": base + other})

    def out_copy(h, j):
        return copy_to(att.at[(head + j) % 4, h], arrived.at[j, h], y_send.at[j, h], y_recv.at[j, h],
                       {"head": (head + j) % 4})

    def compute(h):
        def four(ref):
            lines = lax.broadcasted_iota(jnp.int32, (4, 512), 0)
            mine = jnp.sum(jnp.where(lines == h, ref[...], 0.0), axis=0, keepdims=True)
            return jnp.concatenate([mine[:, c * C : (c + 1) * C] for c in range(4)], axis=0)

        def at(ref):
            return lambda c: ref[pl.ds(c * 512 + h, C, stride=4), :].astype(BF16)

        def put(c, rows_q, rows_o):
            qe[h, c * C : (c + 1) * C, :] = rows_q.astype(BF16)
            own[h, c * C : (c + 1) * C, :] = rows_o

        items[h] = as_item(head_parts(at(qs), at(ks), at(vs), four(b_ref), four(d_ref), masks, put))

        @pl.when(h != member)
        def _():
            item_copy(h).start()

        @pl.when(h == member)
        def _():
            group[h] = items[h]

    def scan_group():
        for j in (1, 2, 3):
            other = member ^ j
            copy_to(group.at[other], group.at[other], g_send.at[other], g_recv.at[other],
                    {"seq": base + other}).wait_recv()
        early = join(group[1], from_item(group[0]))
        late = as_item(join(group[3], from_item(group[2])))
        pairs[0] = as_item(join(late, early))
        for j in (2, 1, 3):
            pair_copy(j).start()

    def scan_pairs():
        for j in (1, 3, 2):
            pair_copy(j).wait_recv()
        eye = jnp.where(
            lax.broadcasted_iota(jnp.int32, (C, 2 * C), 0) == lax.broadcasted_iota(jnp.int32, (C, 2 * C), 1), 1.0, 0.0)
        run = from_item(pairs[(4 - pair) % 4])
        before = jnp.where(pair == 0, eye, run)
        for j in (1, 2, 3):
            run = join(pairs[(j + 4 - pair) % 4], run)
            if j < 3:
                before = jnp.where(pair > j, run, before)
        rows[line] = as_item(run)
        for j in (2, 1, 3):
            @pl.when(line + j < 4)
            def _():
                line_copy(j).start()
        prefix[...] = before

    def scan_lines():
        state[...] = jnp.zeros((C, C), F32)
        for j in (3, 2, 1):
            @pl.when(line - j >= 0)
            def _():
                line_copy(j).wait_recv()
                state[...] = pass_state(rows[line - j], state[...])

        before = prefix[...]
        entry = exact_square(halves(before[:, :C]), halves(state[...])) + before[:, C:]
        for i in range(4):
            enters[i] = entry.astype(BF16)
            if i < 3:
                entry = pass_state(group[i], entry)
        for j in (1, 2, 3):
            enter_copy(j).start()
        entering[member] = enters[member]

    def apply(h):
        @pl.when(member != h)
        def _():
            copy_to(entering.at[h], entering.at[h], e_send.at[h], e_recv.at[h], {"seq": base + h}).wait_recv()
        mine = dot(qe[h], entering[h]) + own[h]
        for t in range(4):
            att[t, h] = mine[t * C : (t + 1) * C].astype(BF16)
        for j in (2, 1, 3):
            out_copy(h, j).start()

    def step(h, _):
        @pl.when(h < 4)
        def _():
            compute(h)

        @pl.when(h == member + 1)
        def _():
            scan_group()

        @pl.when(h == member + 2)
        def _():
            scan_pairs()

        @pl.when(h == member + 3)
        def _():
            scan_lines()

        @pl.when(h == 2)
        def _():
            ra(left).wait_recv()
            ra2(left).start()
            lb(right).wait_recv()
            lb2(right).start()
            over(left, 0, 0).start()
            over(right, 1, 1).start()

        @pl.when(h == 5)
        def _():
            rb(left).wait_recv()
            over(left, 1, 2).start()
            la(right).wait_recv()
            over(right, 0, 3).start()

        @pl.when(h >= 4)
        def _():
            apply(h - 4)

        return 0

    lax.fori_loop(0, 7, step, 0)
    apply(3)

    ra2(across).wait_recv()
    over(across, 0, 4).start()
    lb2(across).wait_recv()
    over(across, 1, 5).start()
    ra(head).wait_send()
    lb(head).wait_send()
    rb(head).wait_send()
    la(head).wait_send()
    ra2(left).wait_send()
    lb2(right).wait_send()
    for j in (1, 2, 3):
        item_copy(member ^ j).wait_send()
        pair_copy(j).wait_send()
        enter_copy(j).wait_send()

        @pl.when(line + j < 4)
        def _():
            line_copy(j).wait_send()

    def other_half(of, part):
        return weight.at[of, 2 * (1 - core) + part]

    for i, (of, part) in enumerate(((left, 0), (right, 1), (left, 1), (right, 0), (across, 0), (across, 1))):
        over(of, part, i).wait_send()
        copy_to(other_half(of, part), other_half(of, part), w_send.at[6 + i], w_recv.at[6 + i], sibling).wait_recv()

    def product(heads, cols):
        rows_in = jnp.concatenate(
            [att[head, h] if j == 0 else arrived[j, h] for j in range(4) for h in heads], axis=1)
        rows_w = jnp.concatenate(
            [weight[(head + 4 - j) % 4, h, :, cols] for j in range(4) for h in heads], axis=0)
        return dot(rows_in, rows_w)

    for h in range(3):
        for j in (1, 3, 2):
            out_copy(h, j).wait()
    for n in range(4):
        total[:, n * 512 : (n + 1) * 512] = product((0, 1, 2), slice(n * 512, (n + 1) * 512))
    for j in (1, 3, 2):
        out_copy(3, j).wait()
    for n in range(4):
        cols = slice(n * 512, (n + 1) * 512)
        out_ref[:, cols] = (total[:, cols] + product((3,), cols)).astype(BF16)


def layer(q, k, v, b, d, w):
    vmem = pl.BlockSpec(memory_space=pltpu.VMEM)
    dma = pltpu.SemaphoreType.DMA
    return pl.pallas_call(
        layer_kernel,
        out_shape=jax.ShapeDtypeStruct((128, 2048), BF16),
        in_specs=[pl.BlockSpec(memory_space=pltpu.HBM)] * 6,
        out_specs=vmem,
        scratch_shapes=[pltpu.VMEM((512, 4, C), BF16)] * 3 + [pltpu.VMEM((4, 512), F32)] * 2 + [
            pltpu.VMEM((7, C, C), BF16),
            pltpu.VMEM((2048, C), F32),
            pltpu.VMEM((2048, C), F32),
            pltpu.VMEM((2048, C), F32),
            pltpu.VMEM((4, 512, C), BF16),
            pltpu.VMEM((4, 512, C), F32),
            pltpu.VMEM((4, C, 3 * C), BF16),
            pltpu.VMEM((4, C, 3 * C), BF16),
            pltpu.VMEM((4, C, 3 * C), BF16),
            pltpu.VMEM((4, C, 3 * C), BF16),
            pltpu.VMEM((4, C, C), BF16),
            pltpu.VMEM((4, C, C), BF16),
            pltpu.VMEM((4, 4, C, C), BF16),
            pltpu.VMEM((4, 4, C, C), BF16),
            pltpu.VMEM((4, 4, C, 2048), BF16),
            pltpu.VMEM((C, 2048), F32),
            pltpu.VMEM((C, 2 * C), F32),
            pltpu.VMEM((C, C), F32),
            dma((5,)), dma, dma((12,)), dma((12,)),
        ] + [dma((4,))] * 8 + [dma((4, 4))] * 2,
        compiler_params=pltpu.CompilerParams(
            collective_id=0, has_side_effects=True, vmem_limit_bytes=28 * 2**20),
    )(q, k, v, b, d, w)


def body(query, key, value, beta, log_decay, out_weight):
    stay = lambda a: pltpu.with_memory_space_constraint(a, pltpu.HBM)
    return layer(stay(query), stay(key), stay(value), stay(beta), stay(log_decay), stay(out_weight.reshape(4, C, 2048)))


def solution(mesh):
    in_specs = (
        P("seq", "head", None),
        P("seq", "head", None),
        P("seq", "head", None),
        P("head", "seq"),
        P("head", "seq"),
        P("head", None),
    )
    out_specs = P(("seq", "head"), None)
    return jax.shard_map(body, mesh=mesh, in_specs=in_specs, out_specs=out_specs, check_vma=False)
```

```python
import jax
import jax.numpy as jnp
from jax import lax
from jax.experimental import pallas as pl
from jax.experimental.pallas import tpu as pltpu
from jax.sharding import PartitionSpec as P

C = 128
LEVELS = (2, 4, 8, 16, 32, 64)
F32, BF16 = jnp.float32, jnp.bfloat16


def dot(a, b):
    return jnp.dot(a, b, preferred_element_type=F32)


def dot_nt(a, b, precision=None):
    return lax.dot_general(a, b, (((1,), (1,)), ((), ())), precision=precision, preferred_element_type=F32)


def halves(a):
    hi = a.astype(BF16)
    return hi, (a - hi.astype(F32)).astype(BF16)


def wide(a, b):
    return jnp.concatenate([a, b], axis=1)


def tall(a, b):
    return jnp.concatenate([a, b], axis=0)


def exact_square(a_halves, b_halves):
    row = wide(*b_halves)
    both = dot(wide(*a_halves), tall(row, row))
    return both[:, :C] + both[:, C:]


def exact_apply(a_halves, b_hi, b_lo):
    return dot(wide(*a_halves), tall(b_hi, b_hi)) + dot(a_halves[0], b_lo)


def fill_masks(masks):
    row = lax.broadcasted_iota(jnp.int32, (C, C), 0)
    col = lax.broadcasted_iota(jnp.int32, (C, C), 1)
    apart = jnp.where(row > col, row ^ col, 0)
    for i, s in enumerate((1,) + LEVELS):
        masks[i] = jnp.where((apart >= s) & (apart < 2 * s), 1.0, 0.0).astype(BF16)


def chunk_start(k, b_col, g_row, g_col):
    row = lax.broadcasted_iota(jnp.int32, (C, C), 0)
    col = lax.broadcasted_iota(jnp.int32, (C, C), 1)
    gram = dot_nt(k, k)
    diagonal = jnp.where(row == col, gram, 0.0)
    rk_row = lax.rsqrt(jnp.sum(diagonal, axis=0, keepdims=True) + 1e-06)
    rk_col = lax.rsqrt(jnp.sum(diagonal, axis=1, keepdims=True) + 1e-06)
    decay = jnp.exp(jnp.where(row >= col, g_col - g_row, -1e30)) * rk_row
    lower = jnp.where(row > col, decay * gram, 0.0) * (b_col * rk_col)
    return lower, decay, rk_row, rk_col


def invert(lowers, masks):
    row = lax.broadcasted_iota(jnp.int32, (C, C), 0)
    col = lax.broadcasted_iota(jnp.int32, (C, C), 1)
    split = [halves(a) for a in lowers]
    first = masks[0].astype(F32)
    xs = [jnp.where(row == col, 1.0, 0.0) - a * first for a in lowers]
    for i in range(len(LEVELS)):
        mask = masks[i + 1]
        xh = [halves(x) for x in xs]
        ys = [exact_square((hi * mask, lo * mask), x) for (hi, lo), x in zip(split, xh)]
        yh = [halves(y) for y in ys]
        zs = [exact_square(x, y) for x, y in zip(xh, yh)]
        xs = [x - z for x, z in zip(xs, zs)]
    return xs


def chunk_end(x, k, v, b_row, g_row, g_col, rk_row, rk_col):
    row = lax.broadcasted_iota(jnp.int32, (C, C), 0)
    col = lax.broadcasted_iota(jnp.int32, (C, C), 1)
    carried = dot(wide(*halves(x * b_row)), tall(v, v))
    key_factor = dot(wide(*halves(x * (b_row * jnp.exp(g_row) * rk_row))), tall(k, k))
    pair = wide(-key_factor, carried)
    g_end = g_col[C - 1 :, :]
    pair_hi, pair_lo = halves(pair * (jnp.exp(g_end - g_col) * rk_col))
    kt = k.T
    ab = dot(wide(kt, kt), tall(pair_hi, pair_lo))
    step = ab[:, :C] + jnp.where(row == col, jnp.exp(g_end), 0.0)
    return pair, wide(step, ab[:, C:])


def compose(later, earlier):
    return exact_apply(halves(later[:, :C]), *halves(earlier)) + wide(jnp.zeros((C, C), F32), later[:, C:])


def key_side(k_of, v_of, beta, decay_log, masks, keep):
    row = lax.broadcasted_iota(jnp.int32, (C, C), 0)
    col = lax.broadcasted_iota(jnp.int32, (C, C), 1)
    sums = jnp.where(row <= col, 1.0, 0.0)
    logs = jnp.maximum(decay_log, -110.0)
    logs = tall(logs, logs)
    g = jnp.dot(logs, sums, precision=lax.Precision.HIGHEST, preferred_element_type=F32)
    turned = tall(beta, g[:4]).T
    b_row = [beta[c : c + 1] for c in range(4)]
    b_col = [turned[:, c : c + 1] for c in range(4)]
    g_row = [g[c : c + 1] for c in range(4)]
    g_col = [turned[:, 4 + c : 5 + c] for c in range(4)]
    starts = [chunk_start(k_of(c), b_col[c], g_row[c], g_col[c]) for c in range(4)]
    xs = invert([s[0] for s in starts], masks)
    ends = [chunk_end(xs[c], k_of(c), v_of(c), b_row[c], g_row[c], g_col[c], *starts[c][2:]) for c in range(4)]
    maps = [e[1] for e in ends]
    two = compose(maps[1], maps[0])
    other = compose(maps[3], maps[2])
    three = compose(maps[2], two)
    for c, before in enumerate((None, maps[0], two, three)):
        keep(c, starts[c][1], jnp.exp(g_col[c]), ends[c][0], before)
    return compose(other, two)


def query_side(q, k, decay, growth, pair, before):
    qf = q.astype(F32)
    rq_col = lax.rsqrt(jnp.sum(qf * qf, axis=1, keepdims=True) + 1e-06)
    qo = exact_apply(halves(decay * dot_nt(q, k)), *halves(pair))
    rows_q = (qo[:, :C] + growth * qf) * rq_col
    rows_o = qo[:, C:] * rq_col
    if before is None:
        return rows_q, rows_o
    moved = exact_apply(halves(rows_q), *halves(before))
    return moved[:, :C], rows_o + moved[:, C:]


MESH = pl.DeviceIdType.MESH


def as_item(state):
    hi, lo = halves(state[:, :C])
    return jnp.concatenate([hi, lo, state[:, C:].astype(BF16)], axis=1)


def from_item(item):
    return wide(item[:, :C].astype(F32) + item[:, C : 2 * C].astype(F32), item[:, 2 * C :].astype(F32))


def join(later, earlier):
    hi, lo = halves(earlier)
    return exact_apply((later[:, :C], later[:, C : 2 * C]), hi, lo) + wide(
        jnp.zeros((C, C), F32), later[:, 2 * C :].astype(F32))


def pass_state(item, state):
    return exact_square((item[:, :C], item[:, C : 2 * C]), halves(state)) + item[:, 2 * C :].astype(F32)


def layer_kernel(q_in, k_in, v_in, b_in, d_in, w_ref, out_ref,
                 q_ref, k_ref, v_ref, b_ref, d_ref, masks, qs, ks, vs, decays, growths, chunk_pairs, befores, qe, own, items, group, pairs, rows, enters, entering, att, arrived, weight,
                 total, group_maps, entry_maps, entry_adds, state,
                 in_load, w_load, w_send, w_recv, g_send, g_recv, p_send, p_recv, x_send, x_recv, e_send, e_recv,
                 y_send, y_recv):
    seq, head = lax.axis_index("seq"), lax.axis_index("head")
    member, pair, line = seq % 4, (seq // 4) % 4, seq // 16
    core = seq % 2
    base = seq - member
    right, left, across = (head + 1) % 4, (head + 3) % 4, (head + 2) % 4

    def in_pairs(step):
        return line * 16 + ((pair + step) % 4) * 4 + member

    barrier = pltpu.get_barrier_semaphore()
    friends = [{"seq": base + (member ^ j)} for j in (1, 2, 3)]
    friends += [{"seq": in_pairs(j)} for j in (1, 2, 3)]
    friends += [{"seq": (seq + 16 * j) % 64} for j in (1, 2, 3)]
    friends += [{"head": (head + j) % 4} for j in (1, 2, 3)]
    for friend in friends:
        pl.semaphore_signal(barrier, inc=1, device_id=friend, device_id_type=MESH)
    loads = [pltpu.make_async_copy(source, target, in_load.at[i]) for i, (source, target) in enumerate(
        ((b_in, b_ref), (d_in, d_ref), (k_in, k_ref), (v_in, v_ref), (q_in, q_ref)))]
    for copy in loads:
        copy.start()
    load = pltpu.make_async_copy(w_ref, weight.at[head], w_load)
    load.start()
    fill_masks(masks)
    for copy in loads:
        copy.wait()
    for source, target in ((q_ref, qs), (k_ref, ks), (v_ref, vs)):
        target[...] = source[...].astype(F32).reshape(2048, C)
    load.wait()
    pl.semaphore_wait(barrier, len(friends))

    def copy_to(source, target, send_sem, recv_sem, to):
        return pltpu.make_async_remote_copy(source, target, send_sem, recv_sem, device_id=to, device_id_type=MESH)

    def quarter(of, part):
        return weight.at[of, 2 * core + part]

    sibling = {"seq": seq ^ 1}
    to_right, to_left = {"head": right}, {"head": left}
    ra = lambda of: copy_to(quarter(of, 0), quarter(of, 0), w_send.at[0], w_recv.at[0], to_right)
    lb = lambda of: copy_to(quarter(of, 1), quarter(of, 1), w_send.at[1], w_recv.at[1], to_left)
    rb = lambda of: copy_to(quarter(of, 1), quarter(of, 1), w_send.at[2], w_recv.at[2], to_right)
    la = lambda of: copy_to(quarter(of, 0), quarter(of, 0), w_send.at[3], w_recv.at[3], to_left)
    ra2 = lambda of: copy_to(quarter(of, 0), quarter(of, 0), w_send.at[4], w_recv.at[4], to_right)
    lb2 = lambda of: copy_to(quarter(of, 1), quarter(of, 1), w_send.at[5], w_recv.at[5], to_left)

    def over(of, part, i):
        return copy_to(quarter(of, part), quarter(of, part), w_send.at[6 + i], w_recv.at[6 + i], sibling)

    ra(head).start()
    lb(head).start()
    rb(head).start()
    la(head).start()

    def item_copy(h):
        return copy_to(items.at[h], group.at[member], g_send.at[h], g_recv.at[member], {"seq": base + h})

    def pair_copy(j):
        return copy_to(pairs.at[0], pairs.at[4 - j], p_send.at[j], p_recv.at[j], {"seq": in_pairs(j)})

    def line_copy(j):
        return copy_to(rows.at[line], rows.at[line], x_send.at[j], x_recv.at[j], {"seq": (seq + 16 * j) % 64})

    def enter_copy(j):
        other = member ^ j
        return copy_to(enters.at[other], entering.at[member], e_send.at[other], e_recv.at[member],
                       {"seq": base + other})

    def out_copy(h, j):
        return copy_to(att.at[(head + j) % 4, h], arrived.at[j, h], y_send.at[j, h], y_recv.at[j, h],
                       {"head": (head + j) % 4})

    def at(ref, h):
        return lambda c: ref[pl.ds(c * 512 + h, C, stride=4), :].astype(BF16)

    def compute(h):
        def four(ref):
            lines = lax.broadcasted_iota(jnp.int32, (4, 512), 0)
            mine = jnp.sum(jnp.where(lines == h, ref[...], 0.0), axis=0, keepdims=True)
            return jnp.concatenate([mine[:, c * C : (c + 1) * C] for c in range(4)], axis=0)

        def keep(c, decay, growth, pair_here, before):
            decays[h, c] = decay
            growths[h, c] = growth
            chunk_pairs[h, c] = pair_here
            if c:
                befores[h, c - 1] = before

        items[h] = as_item(key_side(at(ks, h), at(vs, h), four(b_ref), four(d_ref), masks, keep))

        @pl.when(h != member)
        def _():
            item_copy(h).start()

        @pl.when(h == member)
        def _():
            group[h] = items[h]

    def compute_rows(h):
        q_of, k_of = at(qs, h), at(ks, h)
        for c in range(4):
            rows_q, rows_o = query_side(q_of(c), k_of(c), decays[h, c], growths[h, c], chunk_pairs[h, c],
                                        befores[h, c - 1] if c else None)
            qe[h, c * C : (c + 1) * C, :] = rows_q.astype(BF16)
            own[h, c * C : (c + 1) * C, :] = rows_o

    def scan_group():
        for j in (1, 2, 3):
            other = member ^ j
            copy_to(group.at[other], group.at[other], g_send.at[other], g_recv.at[other],
                    {"seq": base + other}).wait_recv()
        early = join(group[1], from_item(group[0]))
        late = as_item(join(group[3], from_item(group[2])))
        pairs[0] = as_item(join(late, early))
        for j in (2, 1, 3):
            pair_copy(j).start()
        group_maps[0] = group[0]
        group_maps[1] = as_item(early)
        group_maps[2] = as_item(join(group[2], early))

    def scan_pairs():
        for j in (1, 3, 2):
            pair_copy(j).wait_recv()
        at_pair = [pairs[(j + 4 - pair) % 4] for j in range(4)]
        first = from_item(at_pair[0])
        early = join(at_pair[1], first)
        late = as_item(join(at_pair[3], from_item(at_pair[2])))
        rows[line] = as_item(join(late, early))
        for j in (2, 1, 3):
            @pl.when(line + j < 4)
            def _():
                line_copy(j).start()
        eye = jnp.where(
            lax.broadcasted_iota(jnp.int32, (C, 2 * C), 0) == lax.broadcasted_iota(jnp.int32, (C, 2 * C), 1), 1.0, 0.0)
        before = jnp.where(pair == 0, eye, first)
        before = jnp.where(pair > 1, early, before)
        before = jnp.where(pair > 2, join(at_pair[2], early), before)
        for i in range(4):
            here = join(group_maps[i - 1], before) if i else before
            hi, lo = halves(here[:, :C])
            entry_maps[i * C : (i + 1) * C, :C] = hi
            entry_maps[i * C : (i + 1) * C, C:] = lo
            entry_adds[i * C : (i + 1) * C, :] = here[:, C:]

    def scan_lines():
        state[...] = jnp.zeros((C, C), F32)
        for i in range(3):
            @pl.when(line > i)
            def _():
                copy_to(rows.at[i], rows.at[i], x_send.at[line - i], x_recv.at[line - i],
                        {"seq": (seq + 16) % 64}).wait_recv()
                if i == 0:
                    state[...] = rows[0, :, 2 * C :].astype(F32)
                else:
                    state[...] = pass_state(rows[i], state[...])

        row = wide(*halves(state[...]))
        both = dot(entry_maps[...], tall(row, row))
        all_four = (both[:, :C] + both[:, C:] + entry_adds[...]).astype(BF16)
        for i in range(4):
            enters[i] = all_four[i * C : (i + 1) * C]
        for j in (1, 2, 3):
            enter_copy(j).start()
        entering[member] = enters[member]

    def apply(h):
        @pl.when(member != h)
        def _():
            copy_to(entering.at[h], entering.at[h], e_send.at[h], e_recv.at[h], {"seq": base + h}).wait_recv()
        mine = dot(qe[h], entering[h]) + own[h]
        for t in range(4):
            att[t, h] = mine[t * C : (t + 1) * C].astype(BF16)
        for j in (2, 1, 3):
            out_copy(h, j).start()

    def step(h, _):
        @pl.when(h >= 4)
        def _():
            compute_rows(h - 4)

        @pl.when(h < 4)
        def _():
            compute(h)

        @pl.when(h == member + 1)
        def _():
            scan_group()

        @pl.when(h == member + 2)
        def _():
            scan_pairs()

        @pl.when(h == member + 3)
        def _():
            scan_lines()

        @pl.when(h == 3)
        def _():
            ra(left).wait_recv()
            ra2(left).start()
            lb(right).wait_recv()
            lb2(right).start()
            over(left, 0, 0).start()
            over(right, 1, 1).start()

        @pl.when(h == 5)
        def _():
            rb(left).wait_recv()
            over(left, 1, 2).start()
            la(right).wait_recv()
            over(right, 0, 3).start()

        @pl.when(h >= 4)
        def _():
            apply(h - 4)

        return 0

    lax.fori_loop(0, 7, step, 0)
    compute_rows(3)
    apply(3)

    ra2(across).wait_recv()
    over(across, 0, 4).start()
    lb2(across).wait_recv()
    over(across, 1, 5).start()
    ra(head).wait_send()
    lb(head).wait_send()
    rb(head).wait_send()
    la(head).wait_send()
    ra2(left).wait_send()
    lb2(right).wait_send()
    for j in (1, 2, 3):
        item_copy(member ^ j).wait_send()
        pair_copy(j).wait_send()
        enter_copy(j).wait_send()

        @pl.when(line + j < 4)
        def _():
            line_copy(j).wait_send()

    def other_half(of, part):
        return weight.at[of, 2 * (1 - core) + part]

    for i, (of, part) in enumerate(((left, 0), (right, 1), (left, 1), (right, 0), (across, 0), (across, 1))):
        over(of, part, i).wait_send()
        copy_to(other_half(of, part), other_half(of, part), w_send.at[6 + i], w_recv.at[6 + i], sibling).wait_recv()

    def product(heads, cols):
        rows_in = jnp.concatenate(
            [att[head, h] if j == 0 else arrived[j, h] for j in range(4) for h in heads], axis=1)
        rows_w = jnp.concatenate(
            [weight[(head + 4 - j) % 4, h, :, cols] for j in range(4) for h in heads], axis=0)
        return dot(rows_in, rows_w)

    for h in range(3):
        for j in (1, 3, 2):
            out_copy(h, j).wait()
    for n in range(4):
        total[:, n * 512 : (n + 1) * 512] = product((0, 1, 2), slice(n * 512, (n + 1) * 512))
    for j in (1, 3, 2):
        out_copy(3, j).wait()
    for n in range(4):
        cols = slice(n * 512, (n + 1) * 512)
        out_ref[:, cols] = (total[:, cols] + product((3,), cols)).astype(BF16)


def layer(q, k, v, b, d, w):
    vmem = pl.BlockSpec(memory_space=pltpu.VMEM)
    dma = pltpu.SemaphoreType.DMA
    return pl.pallas_call(
        layer_kernel,
        out_shape=jax.ShapeDtypeStruct((128, 2048), BF16),
        in_specs=[pl.BlockSpec(memory_space=pltpu.HBM)] * 6,
        out_specs=vmem,
        scratch_shapes=[pltpu.VMEM((512, 4, C), BF16)] * 3 + [pltpu.VMEM((4, 512), F32)] * 2 + [
            pltpu.VMEM((7, C, C), BF16),
            pltpu.VMEM((2048, C), F32),
            pltpu.VMEM((2048, C), F32),
            pltpu.VMEM((2048, C), F32),
            pltpu.VMEM((4, 4, C, C), F32),
            pltpu.VMEM((4, 4, C, 1), F32),
            pltpu.VMEM((4, 4, C, 2 * C), F32),
            pltpu.VMEM((4, 3, C, 2 * C), F32),
            pltpu.VMEM((4, 512, C), BF16),
            pltpu.VMEM((4, 512, C), F32),
            pltpu.VMEM((4, C, 3 * C), BF16),
            pltpu.VMEM((4, C, 3 * C), BF16),
            pltpu.VMEM((4, C, 3 * C), BF16),
            pltpu.VMEM((4, C, 3 * C), BF16),
            pltpu.VMEM((4, C, C), BF16),
            pltpu.VMEM((4, C, C), BF16),
            pltpu.VMEM((4, 4, C, C), BF16),
            pltpu.VMEM((4, 4, C, C), BF16),
            pltpu.VMEM((4, 4, C, 2048), BF16),
            pltpu.VMEM((C, 2048), F32),
            pltpu.VMEM((3, C, 3 * C), BF16),
            pltpu.VMEM((4 * C, 2 * C), BF16),
            pltpu.VMEM((4 * C, C), F32),
            pltpu.VMEM((C, C), F32),
            dma((5,)), dma, dma((12,)), dma((12,)),
        ] + [dma((4,))] * 8 + [dma((4, 4))] * 2,
        compiler_params=pltpu.CompilerParams(
            collective_id=0, has_side_effects=True, vmem_limit_bytes=40 * 2**20),
    )(q, k, v, b, d, w)


def body(query, key, value, beta, log_decay, out_weight):
    stay = lambda a: pltpu.with_memory_space_constraint(a, pltpu.HBM)
    return layer(stay(query), stay(key), stay(value), stay(beta), stay(log_decay), stay(out_weight.reshape(4, C, 2048)))


def solution(mesh):
    in_specs = (
        P("seq", "head", None),
        P("seq", "head", None),
        P("seq", "head", None),
        P("head", "seq"),
        P("head", "seq"),
        P("head", None),
    )
    out_specs = P(("seq", "head"), None)
    return jax.shard_map(body, mesh=mesh, in_specs=in_specs, out_specs=out_specs, check_vma=False)
```

```python
import jax
import jax.numpy as jnp
from jax import lax
from jax.experimental import pallas as pl
from jax.experimental.pallas import tpu as pltpu
from jax.sharding import PartitionSpec as P

C = 128
LEVELS = (2, 4, 8, 16, 32, 64)
MIDDLE = 2
F32, BF16 = jnp.float32, jnp.bfloat16


def dot(a, b):
    return jnp.dot(a, b, preferred_element_type=F32)


def dot_nt(a, b, precision=None):
    return lax.dot_general(a, b, (((1,), (1,)), ((), ())), precision=precision, preferred_element_type=F32)


def halves(a):
    hi = a.astype(BF16)
    return hi, (a - hi.astype(F32)).astype(BF16)


def wide(a, b):
    return jnp.concatenate([a, b], axis=1)


def tall(a, b):
    return jnp.concatenate([a, b], axis=0)


def exact_square(a_halves, b_halves):
    row = wide(*b_halves)
    both = dot(wide(*a_halves), tall(row, row))
    return both[:, :C] + both[:, C:]


def exact_apply(a_halves, b_hi, b_lo):
    return dot(wide(*a_halves), tall(b_hi, b_hi)) + dot(a_halves[0], b_lo)


def fill_masks(masks):
    row = lax.broadcasted_iota(jnp.int32, (C, C), 0)
    col = lax.broadcasted_iota(jnp.int32, (C, C), 1)
    apart = jnp.where(row > col, row ^ col, 0)
    for i, s in enumerate((1,) + LEVELS):
        masks[i] = jnp.where((apart >= s) & (apart < 2 * s), 1.0, 0.0).astype(BF16)


def chunk_start(k, b_col, g_row, g_col):
    row = lax.broadcasted_iota(jnp.int32, (C, C), 0)
    col = lax.broadcasted_iota(jnp.int32, (C, C), 1)
    gram = dot_nt(k, k)
    diagonal = jnp.where(row == col, gram, 0.0)
    rk_row = lax.rsqrt(jnp.sum(diagonal, axis=0, keepdims=True) + 1e-06)
    rk_col = lax.rsqrt(jnp.sum(diagonal, axis=1, keepdims=True) + 1e-06)
    decay = jnp.exp(jnp.where(row >= col, g_col - g_row, -1e30)) * rk_row
    lower = jnp.where(row > col, decay * gram, 0.0) * (b_col * rk_col)
    return lower, decay, rk_row, rk_col


def invert(lowers, masks, middle):
    row = lax.broadcasted_iota(jnp.int32, (C, C), 0)
    col = lax.broadcasted_iota(jnp.int32, (C, C), 1)
    split = [halves(a) for a in lowers]
    first = masks[0].astype(F32)
    xs = [jnp.where(row == col, 1.0, 0.0) - a * first for a in lowers]
    for i in range(len(LEVELS)):
        mask = masks[i + 1]
        xh = [halves(x) for x in xs]
        ys = [exact_square((hi * mask, lo * mask), x) for (hi, lo), x in zip(split, xh)]
        yh = [halves(y) for y in ys]
        zs = [exact_square(x, y) for x, y in zip(xh, yh)]
        xs = [x - z for x, z in zip(xs, zs)]
        if i == MIDDLE:
            middle()
    return xs


def chunk_end(x, k, v, b_row, g_row, g_col, rk_row, rk_col):
    row = lax.broadcasted_iota(jnp.int32, (C, C), 0)
    col = lax.broadcasted_iota(jnp.int32, (C, C), 1)
    carried = dot(wide(*halves(x * b_row)), tall(v, v))
    key_factor = dot(wide(*halves(x * (b_row * jnp.exp(g_row) * rk_row))), tall(k, k))
    pair = wide(-key_factor, carried)
    g_end = g_col[C - 1 :, :]
    pair_hi, pair_lo = halves(pair * (jnp.exp(g_end - g_col) * rk_col))
    kt = k.T
    ab = dot(wide(kt, kt), tall(pair_hi, pair_lo))
    step = ab[:, :C] + jnp.where(row == col, jnp.exp(g_end), 0.0)
    return pair, wide(step, ab[:, C:])


def compose(later, earlier):
    return exact_apply(halves(later[:, :C]), *halves(earlier)) + wide(jnp.zeros((C, C), F32), later[:, C:])


def running_sums(beta, decay_log):
    row = lax.broadcasted_iota(jnp.int32, (C, C), 0)
    col = lax.broadcasted_iota(jnp.int32, (C, C), 1)
    sums = jnp.where(row <= col, 1.0, 0.0)
    logs = jnp.maximum(decay_log, -110.0)
    g = jnp.dot(tall(logs, logs), sums, precision=lax.Precision.HIGHEST, preferred_element_type=F32)
    turned = tall(beta, g[:4]).T
    return [(beta[c : c + 1], turned[:, c : c + 1], g[c : c + 1], turned[:, 4 + c : 5 + c]) for c in range(4)]


def key_side(heads, masks, middle):
    rates = [running_sums(beta, logs) for _, _, beta, logs, _ in heads]
    starts = [[chunk_start(head[0](c), *rate[c][1:]) for c in range(4)] for head, rate in zip(heads, rates)]
    xs = invert([start[0] for four in starts for start in four], masks, middle)
    results = []
    for i, (k_of, v_of, _, _, keep) in enumerate(heads):
        ends = [chunk_end(xs[4 * i + c], k_of(c), v_of(c), rates[i][c][0], *rates[i][c][2:], *starts[i][c][2:])
                for c in range(4)]
        maps = [e[1] for e in ends]
        two = compose(maps[1], maps[0])
        other = compose(maps[3], maps[2])
        three = compose(maps[2], two)
        for c, before in enumerate((None, maps[0], two, three)):
            keep(c, starts[i][c][1], jnp.exp(rates[i][c][3]), ends[c][0], before)
        results.append(compose(other, two))
    return results


def query_side(q, k, decay, growth, pair, before):
    qf = q.astype(F32)
    rq_col = lax.rsqrt(jnp.sum(qf * qf, axis=1, keepdims=True) + 1e-06)
    qo = exact_apply(halves(decay * dot_nt(q, k)), *halves(pair))
    rows_q = (qo[:, :C] + growth * qf) * rq_col
    rows_o = qo[:, C:] * rq_col
    if before is None:
        return rows_q, rows_o
    moved = exact_apply(halves(rows_q), *halves(before))
    return moved[:, :C], rows_o + moved[:, C:]


MESH = pl.DeviceIdType.MESH


def as_item(state):
    hi, lo = halves(state[:, :C])
    return jnp.concatenate([hi, lo, state[:, C:].astype(BF16)], axis=1)


def from_item(item):
    return wide(item[:, :C].astype(F32) + item[:, C : 2 * C].astype(F32), item[:, 2 * C :].astype(F32))


def join(later, earlier):
    hi, lo = halves(earlier)
    return exact_apply((later[:, :C], later[:, C : 2 * C]), hi, lo) + wide(
        jnp.zeros((C, C), F32), later[:, 2 * C :].astype(F32))


def pass_state(item, state):
    return exact_square((item[:, :C], item[:, C : 2 * C]), halves(state)) + item[:, 2 * C :].astype(F32)


def layer_kernel(q_in, k_in, v_in, b_in, d_in, w_ref, out_ref,
                 q_ref, k_ref, v_ref, b_ref, d_ref, masks, qs, ks, vs, decays, growths, chunk_pairs, befores, qe, own, items, group, pairs, rows, enters, entering, att, arrived, weight,
                 total, group_maps, entry_maps, entry_adds, state,
                 in_load, w_load, w_send, w_recv, g_send, g_recv, p_send, p_recv, x_send, x_recv, e_send, e_recv,
                 y_send, y_recv):
    seq, head = lax.axis_index("seq"), lax.axis_index("head")
    member, pair, line = seq % 4, (seq // 4) % 4, seq // 16
    core = seq % 2
    base = seq - member
    right, left, across = (head + 1) % 4, (head + 3) % 4, (head + 2) % 4

    def in_pairs(step):
        return line * 16 + ((pair + step) % 4) * 4 + member

    barrier = pltpu.get_barrier_semaphore()
    friends = [{"seq": base + (member ^ j)} for j in (1, 2, 3)]
    friends += [{"seq": in_pairs(j)} for j in (1, 2, 3)]
    friends += [{"seq": (seq + 16 * j) % 64} for j in (1, 2, 3)]
    friends += [{"head": (head + j) % 4} for j in (1, 2, 3)]
    for friend in friends:
        pl.semaphore_signal(barrier, inc=1, device_id=friend, device_id_type=MESH)
    loads = [pltpu.make_async_copy(source, target, in_load.at[i]) for i, (source, target) in enumerate(
        ((b_in, b_ref), (d_in, d_ref), (k_in, k_ref), (v_in, v_ref), (q_in, q_ref)))]
    for copy in loads:
        copy.start()
    load = pltpu.make_async_copy(w_ref, weight.at[head], w_load)
    load.start()
    fill_masks(masks)
    for copy in loads[:4]:
        copy.wait()
    for source, target in ((k_ref, ks), (v_ref, vs)):
        target[...] = source[...].astype(F32).reshape(2048, C)

    def copy_to(source, target, send_sem, recv_sem, to):
        return pltpu.make_async_remote_copy(source, target, send_sem, recv_sem, device_id=to, device_id_type=MESH)

    def quarter(of, part):
        return weight.at[of, 2 * core + part]

    sibling = {"seq": seq ^ 1}
    to_right, to_left = {"head": right}, {"head": left}
    ra = lambda of: copy_to(quarter(of, 0), quarter(of, 0), w_send.at[0], w_recv.at[0], to_right)
    lb = lambda of: copy_to(quarter(of, 1), quarter(of, 1), w_send.at[1], w_recv.at[1], to_left)
    rb = lambda of: copy_to(quarter(of, 1), quarter(of, 1), w_send.at[2], w_recv.at[2], to_right)
    la = lambda of: copy_to(quarter(of, 0), quarter(of, 0), w_send.at[3], w_recv.at[3], to_left)
    ra2 = lambda of: copy_to(quarter(of, 0), quarter(of, 0), w_send.at[4], w_recv.at[4], to_right)
    lb2 = lambda of: copy_to(quarter(of, 1), quarter(of, 1), w_send.at[5], w_recv.at[5], to_left)

    def over(of, part, i):
        return copy_to(quarter(of, part), quarter(of, part), w_send.at[6 + i], w_recv.at[6 + i], sibling)

    def greet():
        load.wait()
        pl.semaphore_wait(barrier, len(friends))
        ra(head).start()
        lb(head).start()
        rb(head).start()
        la(head).start()

    def item_copy(h):
        return copy_to(items.at[h], group.at[member], g_send.at[h], g_recv.at[member], {"seq": base + h})

    def pair_copy(j):
        return copy_to(pairs.at[0], pairs.at[4 - j], p_send.at[j], p_recv.at[j], {"seq": in_pairs(j)})

    def line_copy(j):
        return copy_to(rows.at[line], rows.at[line], x_send.at[j], x_recv.at[j], {"seq": (seq + 16 * j) % 64})

    def enter_copy(j):
        other = member ^ j
        return copy_to(enters.at[other], entering.at[member], e_send.at[other], e_recv.at[member],
                       {"seq": base + other})

    def out_copy(h, j):
        return copy_to(att.at[(head + j) % 4, h], arrived.at[j, h], y_send.at[j, h], y_recv.at[j, h],
                       {"head": (head + j) % 4})

    def at(ref, h):
        return lambda c: ref[pl.ds(c * 512 + h, C, stride=4), :].astype(BF16)

    def compute(two):
        def head_of(h):
            def four(ref):
                lines = lax.broadcasted_iota(jnp.int32, (4, 512), 0)
                mine = jnp.sum(jnp.where(lines == h, ref[...], 0.0), axis=0, keepdims=True)
                return jnp.concatenate([mine[:, c * C : (c + 1) * C] for c in range(4)], axis=0)

            def keep(c, decay, growth, pair_here, before):
                decays[h, c] = decay
                growths[h, c] = growth
                chunk_pairs[h, c] = pair_here
                if c:
                    befores[h, c - 1] = before

            return at(ks, h), at(vs, h), four(b_ref), four(d_ref), keep

        def middle():
            @pl.when(two == 0)
            def _():
                greet()

            @pl.when((two == 1) & (member < 2))
            def _():
                scan_group()

        heads = [2 * two, 2 * two + 1]
        for h, result in zip(heads, key_side([head_of(h) for h in heads], masks, middle)):
            items[h] = as_item(result)

            @pl.when(h != member)
            def _():
                item_copy(h).start()

            @pl.when(h == member)
            def _():
                group[h] = items[h]

        return 0

    def compute_rows(h):
        q_of, k_of = at(qs, h), at(ks, h)
        for c in range(4):
            rows_q, rows_o = query_side(q_of(c), k_of(c), decays[h, c], growths[h, c], chunk_pairs[h, c],
                                        befores[h, c - 1] if c else None)
            qe[h, c * C : (c + 1) * C, :] = rows_q.astype(BF16)
            own[h, c * C : (c + 1) * C, :] = rows_o

    def scan_group():
        for j in (1, 2, 3):
            other = member ^ j
            copy_to(group.at[other], group.at[other], g_send.at[other], g_recv.at[other],
                    {"seq": base + other}).wait_recv()
        early = join(group[1], from_item(group[0]))
        late = as_item(join(group[3], from_item(group[2])))
        pairs[0] = as_item(join(late, early))
        for j in (2, 1, 3):
            pair_copy(j).start()
        group_maps[0] = group[0]
        group_maps[1] = as_item(early)
        group_maps[2] = as_item(join(group[2], early))

    def scan_pairs():
        for j in (1, 3, 2):
            pair_copy(j).wait_recv()
        at_pair = [pairs[(j + 4 - pair) % 4] for j in range(4)]
        first = from_item(at_pair[0])
        early = join(at_pair[1], first)
        late = as_item(join(at_pair[3], from_item(at_pair[2])))
        rows[line] = as_item(join(late, early))
        for j in (2, 1, 3):
            @pl.when(line + j < 4)
            def _():
                line_copy(j).start()
        eye = jnp.where(
            lax.broadcasted_iota(jnp.int32, (C, 2 * C), 0) == lax.broadcasted_iota(jnp.int32, (C, 2 * C), 1), 1.0, 0.0)
        before = jnp.where(pair == 0, eye, first)
        before = jnp.where(pair > 1, early, before)
        before = jnp.where(pair > 2, join(at_pair[2], early), before)
        for i in range(4):
            here = join(group_maps[i - 1], before) if i else before
            hi, lo = halves(here[:, :C])
            entry_maps[i * C : (i + 1) * C, :C] = hi
            entry_maps[i * C : (i + 1) * C, C:] = lo
            entry_adds[i * C : (i + 1) * C, :] = here[:, C:]

    def scan_lines():
        state[...] = jnp.zeros((C, C), F32)
        for i in range(3):
            @pl.when(line > i)
            def _():
                copy_to(rows.at[i], rows.at[i], x_send.at[line - i], x_recv.at[line - i],
                        {"seq": (seq + 16) % 64}).wait_recv()
                if i == 0:
                    state[...] = rows[0, :, 2 * C :].astype(F32)
                else:
                    state[...] = pass_state(rows[i], state[...])

        row = wide(*halves(state[...]))
        both = dot(entry_maps[...], tall(row, row))
        all_four = (both[:, :C] + both[:, C:] + entry_adds[...]).astype(BF16)
        for i in range(4):
            enters[i] = all_four[i * C : (i + 1) * C]
        for j in (1, 2, 3):
            enter_copy(j).start()
        entering[member] = enters[member]

    def apply(h):
        @pl.when(member != h)
        def _():
            copy_to(entering.at[h], entering.at[h], e_send.at[h], e_recv.at[h], {"seq": base + h}).wait_recv()
        mine = dot(qe[h], entering[h]) + own[h]
        for t in range(4):
            att[t, h] = mine[t * C : (t + 1) * C].astype(BF16)
        for j in (2, 1, 3):
            out_copy(h, j).start()

    lax.fori_loop(0, 2, lambda two, _: compute(two), 0)
    loads[4].wait()
    qs[...] = q_ref[...].astype(F32).reshape(2048, C)
    late = member // 2

    def step(t, _):
        compute_rows(t)

        @pl.when((t == 0) & (late == 1))
        def _():
            scan_group()

        @pl.when(t == late + 1)
        def _():
            scan_pairs()

        @pl.when(t == late + 2)
        def _():
            scan_lines()

        @pl.when(t == 1)
        def _():
            ra(left).wait_recv()
            ra2(left).start()
            lb(right).wait_recv()
            lb2(right).start()
            over(left, 0, 0).start()
            over(right, 1, 1).start()

        @pl.when(t == 2)
        def _():
            rb(left).wait_recv()
            over(left, 1, 2).start()
            la(right).wait_recv()
            over(right, 0, 3).start()

        return 0

    lax.fori_loop(0, 4, step, 0)

    def step_out(h, _):
        apply(h)
        return 0

    lax.fori_loop(0, 4, step_out, 0)

    ra2(across).wait_recv()
    over(across, 0, 4).start()
    lb2(across).wait_recv()
    over(across, 1, 5).start()
    ra(head).wait_send()
    lb(head).wait_send()
    rb(head).wait_send()
    la(head).wait_send()
    ra2(left).wait_send()
    lb2(right).wait_send()
    for j in (1, 2, 3):
        item_copy(member ^ j).wait_send()
        pair_copy(j).wait_send()
        enter_copy(j).wait_send()

        @pl.when(line + j < 4)
        def _():
            line_copy(j).wait_send()

    def other_half(of, part):
        return weight.at[of, 2 * (1 - core) + part]

    for i, (of, part) in enumerate(((left, 0), (right, 1), (left, 1), (right, 0), (across, 0), (across, 1))):
        over(of, part, i).wait_send()
        copy_to(other_half(of, part), other_half(of, part), w_send.at[6 + i], w_recv.at[6 + i], sibling).wait_recv()

    def product(heads, cols):
        rows_in = jnp.concatenate(
            [att[head, h] if j == 0 else arrived[j, h] for j in range(4) for h in heads], axis=1)
        rows_w = jnp.concatenate(
            [weight[(head + 4 - j) % 4, h, :, cols] for j in range(4) for h in heads], axis=0)
        return dot(rows_in, rows_w)

    for h in range(3):
        for j in (1, 3, 2):
            out_copy(h, j).wait()
    for n in range(4):
        total[:, n * 512 : (n + 1) * 512] = product((0, 1, 2), slice(n * 512, (n + 1) * 512))
    for j in (1, 3, 2):
        out_copy(3, j).wait()
    for n in range(4):
        cols = slice(n * 512, (n + 1) * 512)
        out_ref[:, cols] = (total[:, cols] + product((3,), cols)).astype(BF16)


def layer(q, k, v, b, d, w):
    vmem = pl.BlockSpec(memory_space=pltpu.VMEM)
    dma = pltpu.SemaphoreType.DMA
    return pl.pallas_call(
        layer_kernel,
        out_shape=jax.ShapeDtypeStruct((128, 2048), BF16),
        in_specs=[pl.BlockSpec(memory_space=pltpu.HBM)] * 6,
        out_specs=vmem,
        scratch_shapes=[pltpu.VMEM((512, 4, C), BF16)] * 3 + [pltpu.VMEM((4, 512), F32)] * 2 + [
            pltpu.VMEM((7, C, C), BF16),
            pltpu.VMEM((2048, C), F32),
            pltpu.VMEM((2048, C), F32),
            pltpu.VMEM((2048, C), F32),
            pltpu.VMEM((4, 4, C, C), F32),
            pltpu.VMEM((4, 4, C, 1), F32),
            pltpu.VMEM((4, 4, C, 2 * C), F32),
            pltpu.VMEM((4, 3, C, 2 * C), F32),
            pltpu.VMEM((4, 512, C), BF16),
            pltpu.VMEM((4, 512, C), F32),
            pltpu.VMEM((4, C, 3 * C), BF16),
            pltpu.VMEM((4, C, 3 * C), BF16),
            pltpu.VMEM((4, C, 3 * C), BF16),
            pltpu.VMEM((4, C, 3 * C), BF16),
            pltpu.VMEM((4, C, C), BF16),
            pltpu.VMEM((4, C, C), BF16),
            pltpu.VMEM((4, 4, C, C), BF16),
            pltpu.VMEM((4, 4, C, C), BF16),
            pltpu.VMEM((4, 4, C, 2048), BF16),
            pltpu.VMEM((C, 2048), F32),
            pltpu.VMEM((3, C, 3 * C), BF16),
            pltpu.VMEM((4 * C, 2 * C), BF16),
            pltpu.VMEM((4 * C, C), F32),
            pltpu.VMEM((C, C), F32),
            dma((5,)), dma, dma((12,)), dma((12,)),
        ] + [dma((4,))] * 8 + [dma((4, 4))] * 2,
        compiler_params=pltpu.CompilerParams(
            collective_id=0, has_side_effects=True, vmem_limit_bytes=40 * 2**20),
    )(q, k, v, b, d, w)


def body(query, key, value, beta, log_decay, out_weight):
    stay = lambda a: pltpu.with_memory_space_constraint(a, pltpu.HBM)
    return layer(stay(query), stay(key), stay(value), stay(beta), stay(log_decay), stay(out_weight.reshape(4, C, 2048)))


def solution(mesh):
    in_specs = (
        P("seq", "head", None),
        P("seq", "head", None),
        P("seq", "head", None),
        P("head", "seq"),
        P("head", "seq"),
        P("head", None),
    )
    out_specs = P(("seq", "head"), None)
    return jax.shard_map(body, mesh=mesh, in_specs=in_specs, out_specs=out_specs, check_vma=False)
```

```python
import jax
import jax.numpy as jnp
from jax import lax
from jax.experimental import pallas as pl
from jax.experimental.pallas import tpu as pltpu
from jax.sharding import PartitionSpec as P

C = 128
LEVELS = (2, 4, 8, 16, 32, 64)
MIDDLE = 2
F32, BF16 = jnp.float32, jnp.bfloat16


def dot(a, b):
    return jnp.dot(a, b, preferred_element_type=F32)


def dot_nt(a, b, precision=None):
    return lax.dot_general(a, b, (((1,), (1,)), ((), ())), precision=precision, preferred_element_type=F32)


def halves(a):
    hi = a.astype(BF16)
    return hi, (a - hi.astype(F32)).astype(BF16)


def wide(a, b):
    return jnp.concatenate([a, b], axis=1)


def tall(a, b):
    return jnp.concatenate([a, b], axis=0)


def exact_square(a_halves, b_halves):
    row = wide(*b_halves)
    both = dot(wide(*a_halves), tall(row, row))
    return both[:, :C] + both[:, C:]


def exact_apply(a_halves, b_hi, b_lo):
    return dot(wide(*a_halves), tall(b_hi, b_hi)) + dot(a_halves[0], b_lo)


def fill_masks(masks):
    row = lax.broadcasted_iota(jnp.int32, (C, C), 0)
    col = lax.broadcasted_iota(jnp.int32, (C, C), 1)
    apart = jnp.where(row > col, row ^ col, 0)
    for i, s in enumerate((1,) + LEVELS):
        masks[i] = jnp.where((apart >= s) & (apart < 2 * s), 1.0, 0.0).astype(BF16)


def chunk_start(k, b_col, g_row, g_col):
    row = lax.broadcasted_iota(jnp.int32, (C, C), 0)
    col = lax.broadcasted_iota(jnp.int32, (C, C), 1)
    gram = dot_nt(k, k)
    diagonal = jnp.where(row == col, gram, 0.0)
    rk_row = lax.rsqrt(jnp.sum(diagonal, axis=0, keepdims=True) + 1e-06)
    rk_col = lax.rsqrt(jnp.sum(diagonal, axis=1, keepdims=True) + 1e-06)
    decay = jnp.exp(jnp.where(row >= col, g_col - g_row, -1e30)) * rk_row
    lower = jnp.where(row > col, decay * gram, 0.0) * (b_col * rk_col)
    return lower, decay, rk_row, rk_col


def invert(lowers, masks, middle):
    row = lax.broadcasted_iota(jnp.int32, (C, C), 0)
    col = lax.broadcasted_iota(jnp.int32, (C, C), 1)
    split = [halves(a) for a in lowers]
    first = masks[0].astype(F32)
    xs = [jnp.where(row == col, 1.0, 0.0) - a * first for a in lowers]
    for i in range(len(LEVELS)):
        mask = masks[i + 1]
        xh = [halves(x) for x in xs]
        ys = [exact_square((hi * mask, lo * mask), x) for (hi, lo), x in zip(split, xh)]
        yh = [halves(y) for y in ys]
        zs = [exact_square(x, y) for x, y in zip(xh, yh)]
        xs = [x - z for x, z in zip(xs, zs)]
        if i == MIDDLE:
            middle()
    return xs


def chunk_end(x, k, v, b_row, g_row, g_col, rk_row, rk_col):
    row = lax.broadcasted_iota(jnp.int32, (C, C), 0)
    col = lax.broadcasted_iota(jnp.int32, (C, C), 1)
    carried = dot(wide(*halves(x * b_row)), tall(v, v))
    key_factor = dot(wide(*halves(x * (b_row * jnp.exp(g_row) * rk_row))), tall(k, k))
    pair = wide(-key_factor, carried)
    g_end = g_col[C - 1 :, :]
    pair_hi, pair_lo = halves(pair * (jnp.exp(g_end - g_col) * rk_col))
    kt = k.T
    ab = dot(wide(kt, kt), tall(pair_hi, pair_lo))
    step = ab[:, :C] + jnp.where(row == col, jnp.exp(g_end), 0.0)
    return pair, wide(step, ab[:, C:])


def compose(later, earlier):
    return exact_apply(halves(later[:, :C]), *halves(earlier)) + wide(jnp.zeros((C, C), F32), later[:, C:])


def running_sums(beta, decay_log):
    row = lax.broadcasted_iota(jnp.int32, (C, C), 0)
    col = lax.broadcasted_iota(jnp.int32, (C, C), 1)
    sums = jnp.where(row <= col, 1.0, 0.0)
    logs = jnp.maximum(decay_log, -110.0)
    g = jnp.dot(tall(logs, logs), sums, precision=lax.Precision.HIGHEST, preferred_element_type=F32)
    turned = tall(beta, g[:4]).T
    return [(beta[c : c + 1], turned[:, c : c + 1], g[c : c + 1], turned[:, 4 + c : 5 + c]) for c in range(4)]


def key_side(heads, masks, middle):
    rates = [running_sums(beta, logs) for _, _, beta, logs, _ in heads]
    starts = [[chunk_start(head[0](c), *rate[c][1:]) for c in range(4)] for head, rate in zip(heads, rates)]
    xs = invert([start[0] for four in starts for start in four], masks, middle)
    results = []
    for i, (k_of, v_of, _, _, keep) in enumerate(heads):
        ends = [chunk_end(xs[4 * i + c], k_of(c), v_of(c), rates[i][c][0], *rates[i][c][2:], *starts[i][c][2:])
                for c in range(4)]
        maps = [e[1] for e in ends]
        two = compose(maps[1], maps[0])
        other = compose(maps[3], maps[2])
        three = compose(maps[2], two)
        for c, before in enumerate((None, maps[0], two, three)):
            keep(c, starts[i][c][1], jnp.exp(rates[i][c][3]), ends[c][0], before)
        results.append(compose(other, two))
    return results


def query_side(q, k, decay, growth, pair, before):
    qf = q.astype(F32)
    rq_col = lax.rsqrt(jnp.sum(qf * qf, axis=1, keepdims=True) + 1e-06)
    qo = exact_apply(halves(decay * dot_nt(q, k)), *halves(pair))
    rows_q = (qo[:, :C] + growth * qf) * rq_col
    rows_o = qo[:, C:] * rq_col
    if before is None:
        return rows_q, rows_o
    moved = exact_apply(halves(rows_q), *halves(before))
    return moved[:, :C], rows_o + moved[:, C:]


MESH = pl.DeviceIdType.MESH


def as_item(state):
    hi, lo = halves(state[:, :C])
    return jnp.concatenate([hi, lo, state[:, C:].astype(BF16)], axis=1)


def from_item(item):
    return wide(item[:, :C].astype(F32) + item[:, C : 2 * C].astype(F32), item[:, 2 * C :].astype(F32))


def join(later, earlier):
    hi, lo = halves(earlier)
    return exact_apply((later[:, :C], later[:, C : 2 * C]), hi, lo) + wide(
        jnp.zeros((C, C), F32), later[:, 2 * C :].astype(F32))


def pass_state(item, state):
    return exact_square((item[:, :C], item[:, C : 2 * C]), halves(state)) + item[:, 2 * C :].astype(F32)


def swapped(i):
    return (i % 2) * 2 + i // 2


def layer_kernel(q_in, k_in, v_in, b_in, d_in, w_ref, out_ref,
                 q_ref, k_ref, v_ref, b_ref, d_ref, masks, qs, ks, vs, decays, growths, chunk_pairs, befores, qe, own, items, group, pairs, rows, enters, entering, att, arrived, weight,
                 total, group_maps, entry_maps, entry_adds, state,
                 in_load, w_load, w_send, w_recv, g_send, g_recv, p_send, p_recv, x_send, x_recv, e_send, e_recv,
                 y_send, y_recv):
    seq, head = lax.axis_index("seq"), lax.axis_index("head")
    member, pair, line = seq % 4, (seq // 4) % 4, seq // 16
    core = seq % 2
    base = seq - member
    mine = swapped(member)
    late = mine // 2
    right, left, across = (head + 1) % 4, (head + 3) % 4, (head + 2) % 4

    def in_pairs(step):
        return line * 16 + ((pair + step) % 4) * 4 + member

    barrier = pltpu.get_barrier_semaphore()
    friends = [{"seq": base + (member ^ j)} for j in (1, 2, 3)]
    friends += [{"seq": in_pairs(j)} for j in (1, 2, 3)]
    friends += [{"seq": (seq + 16 * j) % 64} for j in (1, 2, 3)]
    friends += [{"head": (head + j) % 4} for j in (1, 2, 3)]
    for friend in friends:
        pl.semaphore_signal(barrier, inc=1, device_id=friend, device_id_type=MESH)
    loads = [pltpu.make_async_copy(source, target, in_load.at[i]) for i, (source, target) in enumerate(
        ((b_in, b_ref), (d_in, d_ref), (k_in, k_ref), (v_in, v_ref), (q_in, q_ref)))]
    for copy in loads:
        copy.start()
    load = pltpu.make_async_copy(w_ref, weight.at[head], w_load)
    load.start()
    fill_masks(masks)
    for copy in loads[:4]:
        copy.wait()
    for source, target in ((k_ref, ks), (v_ref, vs)):
        target[...] = source[...].astype(F32).reshape(2048, C)

    def copy_to(source, target, send_sem, recv_sem, to):
        return pltpu.make_async_remote_copy(source, target, send_sem, recv_sem, device_id=to, device_id_type=MESH)

    def quarter(of, part):
        return weight.at[of, 2 * core + part]

    sibling = {"seq": seq ^ 1}
    to_right, to_left = {"head": right}, {"head": left}
    ra = lambda of: copy_to(quarter(of, 0), quarter(of, 0), w_send.at[0], w_recv.at[0], to_right)
    lb = lambda of: copy_to(quarter(of, 1), quarter(of, 1), w_send.at[1], w_recv.at[1], to_left)
    rb = lambda of: copy_to(quarter(of, 1), quarter(of, 1), w_send.at[2], w_recv.at[2], to_right)
    la = lambda of: copy_to(quarter(of, 0), quarter(of, 0), w_send.at[3], w_recv.at[3], to_left)
    ra2 = lambda of: copy_to(quarter(of, 0), quarter(of, 0), w_send.at[4], w_recv.at[4], to_right)
    lb2 = lambda of: copy_to(quarter(of, 1), quarter(of, 1), w_send.at[5], w_recv.at[5], to_left)

    def over(of, part, i):
        return copy_to(quarter(of, part), quarter(of, part), w_send.at[6 + i], w_recv.at[6 + i], sibling)

    def greet():
        load.wait()
        pl.semaphore_wait(barrier, len(friends))
        ra(head).start()
        lb(head).start()
        rb(head).start()
        la(head).start()

    def item_copy(h):
        return copy_to(items.at[h], group.at[member], g_send.at[h], g_recv.at[member], {"seq": base + swapped(h)})

    def pair_copy(j):
        return copy_to(pairs.at[0], pairs.at[4 - j], p_send.at[j], p_recv.at[j], {"seq": in_pairs(j)})

    def line_copy(j):
        return copy_to(rows.at[line], rows.at[line], x_send.at[j], x_recv.at[j], {"seq": (seq + 16 * j) % 64})

    def enter_copy(j):
        other = member ^ j
        return copy_to(enters.at[other], entering.at[mine], e_send.at[other], e_recv.at[mine],
                       {"seq": base + other})

    def out_copy(h, j):
        return copy_to(att.at[(head + j) % 4, h], arrived.at[j, h], y_send.at[j, h], y_recv.at[j, h],
                       {"head": (head + j) % 4})

    def at(ref, h):
        return lambda c: ref[pl.ds(c * 512 + h, C, stride=4), :].astype(BF16)

    def compute(two):
        def head_of(h):
            def four(ref):
                lines = lax.broadcasted_iota(jnp.int32, (4, 512), 0)
                mine = jnp.sum(jnp.where(lines == h, ref[...], 0.0), axis=0, keepdims=True)
                return jnp.concatenate([mine[:, c * C : (c + 1) * C] for c in range(4)], axis=0)

            def keep(c, decay, growth, pair_here, before):
                decays[h, c] = decay
                growths[h, c] = growth
                chunk_pairs[h, c] = pair_here
                if c:
                    befores[h, c - 1] = before

            return at(ks, h), at(vs, h), four(b_ref), four(d_ref), keep

        def middle():
            @pl.when(two == 0)
            def _():
                greet()

            @pl.when((two == 1) & (late == 0))
            def _():
                scan_group()

        heads = [2 * two, 2 * two + 1]
        for h, result in zip(heads, key_side([head_of(h) for h in heads], masks, middle)):
            items[h] = as_item(result)

            @pl.when(h != mine)
            def _():
                item_copy(h).start()

            @pl.when(h == mine)
            def _():
                group[member] = items[h]

        return 0

    def compute_rows(h):
        q_of, k_of = at(qs, h), at(ks, h)
        for c in range(4):
            rows_q, rows_o = query_side(q_of(c), k_of(c), decays[h, c], growths[h, c], chunk_pairs[h, c],
                                        befores[h, c - 1] if c else None)
            qe[h, c * C : (c + 1) * C, :] = rows_q.astype(BF16)
            own[h, c * C : (c + 1) * C, :] = rows_o

    def scan_group():
        for j in (1, 2, 3):
            other = member ^ j
            copy_to(group.at[other], group.at[other], g_send.at[other], g_recv.at[other],
                    {"seq": base + other}).wait_recv()
        early = join(group[1], from_item(group[0]))
        late = as_item(join(group[3], from_item(group[2])))
        pairs[0] = as_item(join(late, early))
        for j in (2, 1, 3):
            pair_copy(j).start()
        group_maps[0] = group[0]
        group_maps[1] = as_item(early)
        group_maps[2] = as_item(join(group[2], early))

    def scan_pairs():
        for j in (1, 3, 2):
            pair_copy(j).wait_recv()
        at_pair = [pairs[(j + 4 - pair) % 4] for j in range(4)]
        first = from_item(at_pair[0])
        early = join(at_pair[1], first)
        late = as_item(join(at_pair[3], from_item(at_pair[2])))
        rows[line] = as_item(join(late, early))
        for j in (2, 1, 3):
            @pl.when(line + j < 4)
            def _():
                line_copy(j).start()
        eye = jnp.where(
            lax.broadcasted_iota(jnp.int32, (C, 2 * C), 0) == lax.broadcasted_iota(jnp.int32, (C, 2 * C), 1), 1.0, 0.0)
        before = jnp.where(pair == 0, eye, first)
        before = jnp.where(pair > 1, early, before)
        before = jnp.where(pair > 2, join(at_pair[2], early), before)
        for i in range(4):
            here = join(group_maps[i - 1], before) if i else before
            hi, lo = halves(here[:, :C])
            entry_maps[i * C : (i + 1) * C, :C] = hi
            entry_maps[i * C : (i + 1) * C, C:] = lo
            entry_adds[i * C : (i + 1) * C, :] = here[:, C:]

    def scan_lines():
        state[...] = jnp.zeros((C, C), F32)
        for i in range(3):
            @pl.when(line > i)
            def _():
                copy_to(rows.at[i], rows.at[i], x_send.at[line - i], x_recv.at[line - i],
                        {"seq": (seq + 16) % 64}).wait_recv()
                if i == 0:
                    state[...] = rows[0, :, 2 * C :].astype(F32)
                else:
                    state[...] = pass_state(rows[i], state[...])

        row = wide(*halves(state[...]))
        both = dot(entry_maps[...], tall(row, row))
        all_four = (both[:, :C] + both[:, C:] + entry_adds[...]).astype(BF16)
        for i in range(4):
            enters[i] = all_four[i * C : (i + 1) * C]
        for j in (1, 2, 3):
            enter_copy(j).start()
        entering[mine] = enters[member]

    def apply(h):
        @pl.when(mine != h)
        def _():
            copy_to(entering.at[h], entering.at[h], e_send.at[h], e_recv.at[h],
                    {"seq": base + swapped(h)}).wait_recv()
        rows_here = dot(qe[h], entering[h]) + own[h]
        for t in range(4):
            att[t, h] = rows_here[t * C : (t + 1) * C].astype(BF16)
        for j in (2, 1, 3):
            out_copy(h, j).start()

    lax.fori_loop(0, 2, lambda two, _: compute(two), 0)
    loads[4].wait()
    qs[...] = q_ref[...].astype(F32).reshape(2048, C)

    def step_out(h, _):
        apply(h)
        return 0

    def step(t, _):
        compute_rows(t)

        @pl.when(t == 3)
        def _():
            lax.fori_loop(0, 2, step_out, 0)

        @pl.when((t == 0) & (late == 1))
        def _():
            scan_group()

        @pl.when(t == late + 1)
        def _():
            scan_pairs()

        @pl.when(t == late + 2)
        def _():
            scan_lines()

        @pl.when(t == 1)
        def _():
            ra(left).wait_recv()
            ra2(left).start()
            lb(right).wait_recv()
            lb2(right).start()
            over(left, 0, 0).start()
            over(right, 1, 1).start()

        @pl.when(t == 2)
        def _():
            rb(left).wait_recv()
            over(left, 1, 2).start()
            la(right).wait_recv()
            over(right, 0, 3).start()

        return 0

    lax.fori_loop(0, 4, step, 0)

    lax.fori_loop(2, 4, step_out, 0)

    ra2(across).wait_recv()
    over(across, 0, 4).start()
    lb2(across).wait_recv()
    over(across, 1, 5).start()
    ra(head).wait_send()
    lb(head).wait_send()
    rb(head).wait_send()
    la(head).wait_send()
    ra2(left).wait_send()
    lb2(right).wait_send()
    for j in (1, 2, 3):
        item_copy(swapped(member ^ j)).wait_send()
        pair_copy(j).wait_send()
        enter_copy(j).wait_send()

        @pl.when(line + j < 4)
        def _():
            line_copy(j).wait_send()

    def other_half(of, part):
        return weight.at[of, 2 * (1 - core) + part]

    for i, (of, part) in enumerate(((left, 0), (right, 1), (left, 1), (right, 0), (across, 0), (across, 1))):
        over(of, part, i).wait_send()
        copy_to(other_half(of, part), other_half(of, part), w_send.at[6 + i], w_recv.at[6 + i], sibling).wait_recv()

    def product(heads, cols):
        rows_in = jnp.concatenate(
            [att[head, h] if j == 0 else arrived[j, h] for j in range(4) for h in heads], axis=1)
        rows_w = jnp.concatenate(
            [weight[(head + 4 - j) % 4, h, :, cols] for j in range(4) for h in heads], axis=0)
        return dot(rows_in, rows_w)

    for h in range(3):
        for j in (1, 3, 2):
            out_copy(h, j).wait()
    for n in range(4):
        total[:, n * 512 : (n + 1) * 512] = product((0, 1, 2), slice(n * 512, (n + 1) * 512))
    for j in (1, 3, 2):
        out_copy(3, j).wait()
    for n in range(4):
        cols = slice(n * 512, (n + 1) * 512)
        out_ref[:, cols] = (total[:, cols] + product((3,), cols)).astype(BF16)


def layer(q, k, v, b, d, w):
    vmem = pl.BlockSpec(memory_space=pltpu.VMEM)
    dma = pltpu.SemaphoreType.DMA
    return pl.pallas_call(
        layer_kernel,
        out_shape=jax.ShapeDtypeStruct((128, 2048), BF16),
        in_specs=[pl.BlockSpec(memory_space=pltpu.HBM)] * 6,
        out_specs=vmem,
        scratch_shapes=[pltpu.VMEM((512, 4, C), BF16)] * 3 + [pltpu.VMEM((4, 512), F32)] * 2 + [
            pltpu.VMEM((7, C, C), BF16),
            pltpu.VMEM((2048, C), F32),
            pltpu.VMEM((2048, C), F32),
            pltpu.VMEM((2048, C), F32),
            pltpu.VMEM((4, 4, C, C), F32),
            pltpu.VMEM((4, 4, C, 1), F32),
            pltpu.VMEM((4, 4, C, 2 * C), F32),
            pltpu.VMEM((4, 3, C, 2 * C), F32),
            pltpu.VMEM((4, 512, C), BF16),
            pltpu.VMEM((4, 512, C), F32),
            pltpu.VMEM((4, C, 3 * C), BF16),
            pltpu.VMEM((4, C, 3 * C), BF16),
            pltpu.VMEM((4, C, 3 * C), BF16),
            pltpu.VMEM((4, C, 3 * C), BF16),
            pltpu.VMEM((4, C, C), BF16),
            pltpu.VMEM((4, C, C), BF16),
            pltpu.VMEM((4, 4, C, C), BF16),
            pltpu.VMEM((4, 4, C, C), BF16),
            pltpu.VMEM((4, 4, C, 2048), BF16),
            pltpu.VMEM((C, 2048), F32),
            pltpu.VMEM((3, C, 3 * C), BF16),
            pltpu.VMEM((4 * C, 2 * C), BF16),
            pltpu.VMEM((4 * C, C), F32),
            pltpu.VMEM((C, C), F32),
            dma((5,)), dma, dma((12,)), dma((12,)),
        ] + [dma((4,))] * 8 + [dma((4, 4))] * 2,
        compiler_params=pltpu.CompilerParams(
            collective_id=0, has_side_effects=True, vmem_limit_bytes=40 * 2**20),
    )(q, k, v, b, d, w)


def body(query, key, value, beta, log_decay, out_weight):
    stay = lambda a: pltpu.with_memory_space_constraint(a, pltpu.HBM)
    return layer(stay(query), stay(key), stay(value), stay(beta), stay(log_decay), stay(out_weight.reshape(4, C, 2048)))


def solution(mesh):
    in_specs = (
        P("seq", "head", None),
        P("seq", "head", None),
        P("seq", "head", None),
        P("head", "seq"),
        P("head", "seq"),
        P("head", None),
    )
    out_specs = P(("seq", "head"), None)
    return jax.shard_map(body, mesh=mesh, in_specs=in_specs, out_specs=out_specs, check_vma=False)
```

```python
import jax
import jax.numpy as jnp
from jax import lax
from jax.experimental import pallas as pl
from jax.experimental.pallas import tpu as pltpu
from jax.sharding import PartitionSpec as P

C = 128
LEVELS = (2, 4, 8, 16, 32, 64)
MIDDLE = 2
F32, BF16 = jnp.float32, jnp.bfloat16


def dot(a, b):
    return jnp.dot(a, b, preferred_element_type=F32)


def dot_nt(a, b, precision=None):
    return lax.dot_general(a, b, (((1,), (1,)), ((), ())), precision=precision, preferred_element_type=F32)


def halves(a):
    hi = a.astype(BF16)
    return hi, (a - hi.astype(F32)).astype(BF16)


def wide(a, b):
    return jnp.concatenate([a, b], axis=1)


def tall(a, b):
    return jnp.concatenate([a, b], axis=0)


def exact_square(a_halves, b_halves):
    row = wide(*b_halves)
    both = dot(wide(*a_halves), tall(row, row))
    return both[:, :C] + both[:, C:]


def exact_apply(a_halves, b_hi, b_lo):
    return dot(wide(*a_halves), tall(b_hi, b_hi)) + dot(a_halves[0], b_lo)


def fill_masks(masks):
    row = lax.broadcasted_iota(jnp.int32, (C, C), 0)
    col = lax.broadcasted_iota(jnp.int32, (C, C), 1)
    apart = jnp.where(row > col, row ^ col, 0)
    for i, s in enumerate((1,) + LEVELS):
        masks[i] = jnp.where((apart >= s) & (apart < 2 * s), 1.0, 0.0).astype(BF16)


def chunk_start(k, b_col, g_row, g_col):
    row = lax.broadcasted_iota(jnp.int32, (C, C), 0)
    col = lax.broadcasted_iota(jnp.int32, (C, C), 1)
    gram = dot_nt(k, k)
    diagonal = jnp.where(row == col, gram, 0.0)
    rk_row = lax.rsqrt(jnp.sum(diagonal, axis=0, keepdims=True) + 1e-06)
    rk_col = lax.rsqrt(jnp.sum(diagonal, axis=1, keepdims=True) + 1e-06)
    decay = jnp.exp(jnp.where(row >= col, g_col - g_row, -1e30)) * rk_row
    lower = jnp.where(row > col, decay * gram, 0.0) * (b_col * rk_col)
    return lower, decay, rk_row, rk_col


def invert(lowers, masks, middle):
    row = lax.broadcasted_iota(jnp.int32, (C, C), 0)
    col = lax.broadcasted_iota(jnp.int32, (C, C), 1)
    split = [halves(a) for a in lowers]
    first = masks[0].astype(F32)
    xs = [jnp.where(row == col, 1.0, 0.0) - a * first for a in lowers]
    for i in range(len(LEVELS)):
        mask = masks[i + 1]
        xh = [halves(x) for x in xs]
        ys = [exact_square((hi * mask, lo * mask), x) for (hi, lo), x in zip(split, xh)]
        yh = [halves(y) for y in ys]
        zs = [exact_square(x, y) for x, y in zip(xh, yh)]
        xs = [x - z for x, z in zip(xs, zs)]
        if i == MIDDLE:
            middle()
    return xs


def chunk_end(x, k, v, b_row, g_row, g_col, rk_row, rk_col):
    row = lax.broadcasted_iota(jnp.int32, (C, C), 0)
    col = lax.broadcasted_iota(jnp.int32, (C, C), 1)
    carried = dot(wide(*halves(x * b_row)), tall(v, v))
    key_factor = dot(wide(*halves(x * (b_row * jnp.exp(g_row) * rk_row))), tall(k, k))
    pair = wide(-key_factor, carried)
    g_end = g_col[C - 1 :, :]
    pair_hi, pair_lo = halves(pair * (jnp.exp(g_end - g_col) * rk_col))
    kt = k.T
    ab = dot(wide(kt, kt), tall(pair_hi, pair_lo))
    step = ab[:, :C] + jnp.where(row == col, jnp.exp(g_end), 0.0)
    return pair, wide(step, ab[:, C:])


def compose(later, earlier):
    return exact_apply(halves(later[:, :C]), *halves(earlier)) + wide(jnp.zeros((C, C), F32), later[:, C:])


def running_sums(beta, decay_log):
    row = lax.broadcasted_iota(jnp.int32, (C, C), 0)
    col = lax.broadcasted_iota(jnp.int32, (C, C), 1)
    sums = jnp.where(row <= col, 1.0, 0.0)
    logs = jnp.maximum(decay_log, -110.0)
    g = jnp.dot(tall(logs, logs), sums, precision=lax.Precision.HIGHEST, preferred_element_type=F32)
    turned = tall(beta, g[:4]).T
    return [(beta[c : c + 1], turned[:, c : c + 1], g[c : c + 1], turned[:, 4 + c : 5 + c]) for c in range(4)]


def key_side(heads, masks, middle):
    rates = [running_sums(beta, logs) for _, _, beta, logs, _ in heads]
    starts = [[chunk_start(head[0](c), *rate[c][1:]) for c in range(4)] for head, rate in zip(heads, rates)]
    xs = invert([start[0] for four in starts for start in four], masks, middle)
    results = []
    for i, (k_of, v_of, _, _, keep) in enumerate(heads):
        ends = [chunk_end(xs[4 * i + c], k_of(c), v_of(c), rates[i][c][0], *rates[i][c][2:], *starts[i][c][2:])
                for c in range(4)]
        maps = [e[1] for e in ends]
        two = compose(maps[1], maps[0])
        other = compose(maps[3], maps[2])
        three = compose(maps[2], two)
        for c, before in enumerate((None, maps[0], two, three)):
            keep(c, starts[i][c][1], jnp.exp(rates[i][c][3]), ends[c][0], before)
        results.append(compose(other, two))
    return results


def query_side(q, k, decay, growth, pair, before):
    qf = q.astype(F32)
    rq_col = lax.rsqrt(jnp.sum(qf * qf, axis=1, keepdims=True) + 1e-06)
    qo = exact_apply(halves(decay * dot_nt(q, k)), *halves(pair))
    rows_q = (qo[:, :C] + growth * qf) * rq_col
    rows_o = qo[:, C:] * rq_col
    if before is None:
        return rows_q, rows_o
    moved = exact_apply(halves(rows_q), *halves(before))
    return moved[:, :C], rows_o + moved[:, C:]


MESH = pl.DeviceIdType.MESH


def as_item(state):
    hi, lo = halves(state[:, :C])
    return jnp.concatenate([hi, lo, state[:, C:].astype(BF16)], axis=1)


def from_item(item):
    return wide(item[:, :C].astype(F32) + item[:, C : 2 * C].astype(F32), item[:, 2 * C :].astype(F32))


def join(later, earlier):
    hi, lo = halves(earlier)
    return exact_apply((later[:, :C], later[:, C : 2 * C]), hi, lo) + wide(
        jnp.zeros((C, C), F32), later[:, 2 * C :].astype(F32))


def pass_state(item, state):
    return exact_square((item[:, :C], item[:, C : 2 * C]), halves(state)) + item[:, 2 * C :].astype(F32)


def swapped(i):
    return (i % 2) * 2 + i // 2


def layer_kernel(q_in, k_in, v_in, b_in, d_in, w_ref, out_ref,
                 q_ref, k_ref, v_ref, b_ref, d_ref, masks, qs, ks, vs, decays, growths, chunk_pairs, befores, qe, own, items, group, pairs, rows, enters, entering, att, arrived, weight,
                 total, group_maps, entry_maps, entry_adds, state,
                 in_load, w_load, w_send, w_recv, g_send, g_recv, p_send, p_recv, x_send, x_recv, e_send, e_recv,
                 y_send, y_recv):
    seq, head = lax.axis_index("seq"), lax.axis_index("head")
    member, pair, line = seq % 4, (seq // 4) % 4, seq // 16
    core = seq % 2
    base = seq - member
    mine = swapped(member)
    late = mine // 2
    right, left, across = (head + 1) % 4, (head + 3) % 4, (head + 2) % 4

    def in_pairs(step):
        return line * 16 + ((pair + step) % 4) * 4 + member

    barrier = pltpu.get_barrier_semaphore()
    friends = [{"seq": base + (member ^ j)} for j in (1, 2, 3)]
    friends += [{"seq": in_pairs(j)} for j in (1, 2, 3)]
    friends += [{"seq": (seq + 16 * j) % 64} for j in (1, 2, 3)]
    friends += [{"head": (head + j) % 4} for j in (1, 2, 3)]
    for friend in friends:
        pl.semaphore_signal(barrier, inc=1, device_id=friend, device_id_type=MESH)
    loads = [pltpu.make_async_copy(source, target, in_load.at[i]) for i, (source, target) in enumerate(
        ((b_in, b_ref), (d_in, d_ref), (k_in, k_ref), (v_in, v_ref), (q_in, q_ref)))]
    for copy in loads:
        copy.start()
    load = pltpu.make_async_copy(w_ref, weight.at[head], w_load)
    load.start()
    fill_masks(masks)
    for copy in loads[:4]:
        copy.wait()
    for source, target in ((k_ref, ks), (v_ref, vs)):
        target[...] = source[...].astype(F32).reshape(2048, C)

    def copy_to(source, target, send_sem, recv_sem, to):
        return pltpu.make_async_remote_copy(source, target, send_sem, recv_sem, device_id=to, device_id_type=MESH)

    def quarter(of, part):
        return weight.at[of, 2 * core + part]

    sibling = {"seq": seq ^ 1}
    to_right, to_left = {"head": right}, {"head": left}
    ra = lambda of: copy_to(quarter(of, 0), quarter(of, 0), w_send.at[0], w_recv.at[0], to_right)
    lb = lambda of: copy_to(quarter(of, 1), quarter(of, 1), w_send.at[1], w_recv.at[1], to_left)
    rb = lambda of: copy_to(quarter(of, 1), quarter(of, 1), w_send.at[2], w_recv.at[2], to_right)
    la = lambda of: copy_to(quarter(of, 0), quarter(of, 0), w_send.at[3], w_recv.at[3], to_left)
    ra2 = lambda of: copy_to(quarter(of, 0), quarter(of, 0), w_send.at[4], w_recv.at[4], to_right)
    lb2 = lambda of: copy_to(quarter(of, 1), quarter(of, 1), w_send.at[5], w_recv.at[5], to_left)

    def over(of, part, i):
        return copy_to(quarter(of, part), quarter(of, part), w_send.at[6 + i], w_recv.at[6 + i], sibling)

    def greet():
        load.wait()
        pl.semaphore_wait(barrier, len(friends))
        ra(head).start()
        lb(head).start()

    def item_copy(h):
        return copy_to(items.at[h], group.at[member], g_send.at[h], g_recv.at[member], {"seq": base + swapped(h)})

    def pair_copy(j):
        return copy_to(pairs.at[0], pairs.at[4 - j], p_send.at[j], p_recv.at[j], {"seq": in_pairs(j)})

    def line_copy(j):
        return copy_to(rows.at[line], rows.at[line], x_send.at[j], x_recv.at[j], {"seq": (seq + 16 * j) % 64})

    def enter_copy(j):
        other = member ^ j
        return copy_to(enters.at[other], entering.at[mine], e_send.at[other], e_recv.at[mine],
                       {"seq": base + other})

    def out_copy(h, j):
        return copy_to(att.at[(head + j) % 4, h], arrived.at[j, h], y_send.at[j, h], y_recv.at[j, h],
                       {"head": (head + j) % 4})

    def at(ref, h):
        return lambda c: ref[pl.ds(c * 512 + h, C, stride=4), :].astype(BF16)

    def compute(two):
        def head_of(h):
            def four(ref):
                lines = lax.broadcasted_iota(jnp.int32, (4, 512), 0)
                mine = jnp.sum(jnp.where(lines == h, ref[...], 0.0), axis=0, keepdims=True)
                return jnp.concatenate([mine[:, c * C : (c + 1) * C] for c in range(4)], axis=0)

            def keep(c, decay, growth, pair_here, before):
                decays[h, c] = decay
                growths[h, c] = growth
                chunk_pairs[h, c] = pair_here
                if c:
                    befores[h, c - 1] = before

            return at(ks, h), at(vs, h), four(b_ref), four(d_ref), keep

        def middle():
            @pl.when(two == 0)
            def _():
                greet()

            @pl.when(two == 1)
            def _():
                rb(head).start()
                la(head).start()

            @pl.when((two == 1) & (late == 0))
            def _():
                scan_group()

        heads = [2 * two, 2 * two + 1]
        for h, result in zip(heads, key_side([head_of(h) for h in heads], masks, middle)):
            items[h] = as_item(result)

            @pl.when(h != mine)
            def _():
                item_copy(h).start()

            @pl.when(h == mine)
            def _():
                group[member] = items[h]

        return 0

    def compute_rows(h):
        q_of, k_of = at(qs, h), at(ks, h)
        for c in range(4):
            rows_q, rows_o = query_side(q_of(c), k_of(c), decays[h, c], growths[h, c], chunk_pairs[h, c],
                                        befores[h, c - 1] if c else None)
            qe[h, c * C : (c + 1) * C, :] = rows_q.astype(BF16)
            own[h, c * C : (c + 1) * C, :] = rows_o

    def scan_group():
        for j in (1, 2, 3):
            other = member ^ j
            copy_to(group.at[other], group.at[other], g_send.at[other], g_recv.at[other],
                    {"seq": base + other}).wait_recv()
        early = join(group[1], from_item(group[0]))
        late = as_item(join(group[3], from_item(group[2])))
        pairs[0] = as_item(join(late, early))
        for j in (2, 1, 3):
            pair_copy(j).start()
        group_maps[0] = group[0]
        group_maps[1] = as_item(early)
        group_maps[2] = as_item(join(group[2], early))

    def scan_pairs():
        for j in (1, 3, 2):
            pair_copy(j).wait_recv()
        at_pair = [pairs[(j + 4 - pair) % 4] for j in range(4)]
        first = from_item(at_pair[0])
        early = join(at_pair[1], first)
        late = as_item(join(at_pair[3], from_item(at_pair[2])))
        rows[line] = as_item(join(late, early))
        for j in (2, 1, 3):
            @pl.when(line + j < 4)
            def _():
                line_copy(j).start()
        eye = jnp.where(
            lax.broadcasted_iota(jnp.int32, (C, 2 * C), 0) == lax.broadcasted_iota(jnp.int32, (C, 2 * C), 1), 1.0, 0.0)
        before = jnp.where(pair == 0, eye, first)
        before = jnp.where(pair > 1, early, before)
        before = jnp.where(pair > 2, join(at_pair[2], early), before)
        for i in range(4):
            here = join(group_maps[i - 1], before) if i else before
            hi, lo = halves(here[:, :C])
            entry_maps[i * C : (i + 1) * C, :C] = hi
            entry_maps[i * C : (i + 1) * C, C:] = lo
            entry_adds[i * C : (i + 1) * C, :] = here[:, C:]

    def scan_lines():
        state[...] = jnp.zeros((C, C), F32)
        for i in range(3):
            @pl.when(line > i)
            def _():
                copy_to(rows.at[i], rows.at[i], x_send.at[line - i], x_recv.at[line - i],
                        {"seq": (seq + 16) % 64}).wait_recv()
                if i == 0:
                    state[...] = rows[0, :, 2 * C :].astype(F32)
                else:
                    state[...] = pass_state(rows[i], state[...])

        row = wide(*halves(state[...]))
        both = dot(entry_maps[...], tall(row, row))
        all_four = (both[:, :C] + both[:, C:] + entry_adds[...]).astype(BF16)
        for i in range(4):
            enters[i] = all_four[i * C : (i + 1) * C]
        for j in (1, 2, 3):
            enter_copy(j).start()
        entering[mine] = enters[member]

    def apply(h):
        @pl.when(mine != h)
        def _():
            copy_to(entering.at[h], entering.at[h], e_send.at[h], e_recv.at[h],
                    {"seq": base + swapped(h)}).wait_recv()
        rows_here = dot(qe[h], entering[h]) + own[h]
        for t in range(4):
            att[t, h] = rows_here[t * C : (t + 1) * C].astype(BF16)
        for j in (2, 1, 3):
            out_copy(h, j).start()

    lax.fori_loop(0, 2, lambda two, _: compute(two), 0)
    ra(left).wait_recv()
    ra2(left).start()
    lb(right).wait_recv()
    lb2(right).start()
    over(left, 0, 0).start()
    over(right, 1, 1).start()
    loads[4].wait()
    qs[...] = q_ref[...].astype(F32).reshape(2048, C)

    def step_out(h, _):
        apply(h)
        return 0

    def step(t, _):
        compute_rows(t)

        @pl.when(t == 3)
        def _():
            lax.fori_loop(0, 2, step_out, 0)

        @pl.when((t == 0) & (late == 1))
        def _():
            scan_group()

        @pl.when(t == late + 1)
        def _():
            scan_pairs()

        @pl.when(t == late + 2)
        def _():
            scan_lines()

        @pl.when(t == 1)
        def _():
            rb(left).wait_recv()
            over(left, 1, 2).start()
            la(right).wait_recv()
            over(right, 0, 3).start()

        @pl.when(t == 2)
        def _():
            ra2(across).wait_recv()
            over(across, 0, 4).start()
            lb2(across).wait_recv()
            over(across, 1, 5).start()

        return 0

    lax.fori_loop(0, 4, step, 0)

    lax.fori_loop(2, 4, step_out, 0)

    ra(head).wait_send()
    lb(head).wait_send()
    rb(head).wait_send()
    la(head).wait_send()
    ra2(left).wait_send()
    lb2(right).wait_send()
    for j in (1, 2, 3):
        item_copy(swapped(member ^ j)).wait_send()
        pair_copy(j).wait_send()
        enter_copy(j).wait_send()

        @pl.when(line + j < 4)
        def _():
            line_copy(j).wait_send()

    def other_half(of, part):
        return weight.at[of, 2 * (1 - core) + part]

    for i, (of, part) in enumerate(((left, 0), (right, 1), (left, 1), (right, 0), (across, 0), (across, 1))):
        over(of, part, i).wait_send()
        copy_to(other_half(of, part), other_half(of, part), w_send.at[6 + i], w_recv.at[6 + i], sibling).wait_recv()

    def product(heads, cols):
        rows_in = jnp.concatenate(
            [att[head, h] if j == 0 else arrived[j, h] for j in range(4) for h in heads], axis=1)
        rows_w = jnp.concatenate(
            [weight[(head + 4 - j) % 4, h, :, cols] for j in range(4) for h in heads], axis=0)
        return dot(rows_in, rows_w)

    for h in range(3):
        for j in (1, 3, 2):
            out_copy(h, j).wait()
    for n in range(4):
        total[:, n * 512 : (n + 1) * 512] = product((0, 1, 2), slice(n * 512, (n + 1) * 512))
    for j in (1, 3, 2):
        out_copy(3, j).wait()
    for n in range(4):
        cols = slice(n * 512, (n + 1) * 512)
        out_ref[:, cols] = (total[:, cols] + product((3,), cols)).astype(BF16)


def layer(q, k, v, b, d, w):
    vmem = pl.BlockSpec(memory_space=pltpu.VMEM)
    dma = pltpu.SemaphoreType.DMA
    return pl.pallas_call(
        layer_kernel,
        out_shape=jax.ShapeDtypeStruct((128, 2048), BF16),
        in_specs=[pl.BlockSpec(memory_space=pltpu.HBM)] * 6,
        out_specs=vmem,
        scratch_shapes=[pltpu.VMEM((512, 4, C), BF16)] * 3 + [pltpu.VMEM((4, 512), F32)] * 2 + [
            pltpu.VMEM((7, C, C), BF16),
            pltpu.VMEM((2048, C), F32),
            pltpu.VMEM((2048, C), F32),
            pltpu.VMEM((2048, C), F32),
            pltpu.VMEM((4, 4, C, C), F32),
            pltpu.VMEM((4, 4, C, 1), F32),
            pltpu.VMEM((4, 4, C, 2 * C), F32),
            pltpu.VMEM((4, 3, C, 2 * C), F32),
            pltpu.VMEM((4, 512, C), BF16),
            pltpu.VMEM((4, 512, C), F32),
            pltpu.VMEM((4, C, 3 * C), BF16),
            pltpu.VMEM((4, C, 3 * C), BF16),
            pltpu.VMEM((4, C, 3 * C), BF16),
            pltpu.VMEM((4, C, 3 * C), BF16),
            pltpu.VMEM((4, C, C), BF16),
            pltpu.VMEM((4, C, C), BF16),
            pltpu.VMEM((4, 4, C, C), BF16),
            pltpu.VMEM((4, 4, C, C), BF16),
            pltpu.VMEM((4, 4, C, 2048), BF16),
            pltpu.VMEM((C, 2048), F32),
            pltpu.VMEM((3, C, 3 * C), BF16),
            pltpu.VMEM((4 * C, 2 * C), BF16),
            pltpu.VMEM((4 * C, C), F32),
            pltpu.VMEM((C, C), F32),
            dma((5,)), dma, dma((12,)), dma((12,)),
        ] + [dma((4,))] * 8 + [dma((4, 4))] * 2,
        compiler_params=pltpu.CompilerParams(
            collective_id=0, has_side_effects=True, vmem_limit_bytes=40 * 2**20),
    )(q, k, v, b, d, w)


def body(query, key, value, beta, log_decay, out_weight):
    stay = lambda a: pltpu.with_memory_space_constraint(a, pltpu.HBM)
    return layer(stay(query), stay(key), stay(value), stay(beta), stay(log_decay), stay(out_weight.reshape(4, C, 2048)))


def solution(mesh):
    in_specs = (
        P("seq", "head", None),
        P("seq", "head", None),
        P("seq", "head", None),
        P("head", "seq"),
        P("head", "seq"),
        P("head", None),
    )
    out_specs = P(("seq", "head"), None)
    return jax.shard_map(body, mesh=mesh, in_specs=in_specs, out_specs=out_specs, check_vma=False)
```

```python
import jax
import jax.numpy as jnp
from jax import lax
from jax.experimental import pallas as pl
from jax.experimental.pallas import tpu as pltpu
from jax.sharding import PartitionSpec as P

C = 128
LEVELS = (2, 4, 8, 16, 32, 64)
F32, BF16 = jnp.float32, jnp.bfloat16


def dot(a, b):
    return jnp.dot(a, b, preferred_element_type=F32)


def dot_nt(a, b, precision=None):
    return lax.dot_general(a, b, (((1,), (1,)), ((), ())), precision=precision, preferred_element_type=F32)


def halves(a):
    hi = a.astype(BF16)
    return hi, (a - hi.astype(F32)).astype(BF16)


def wide(a, b):
    return jnp.concatenate([a, b], axis=1)


def tall(a, b):
    return jnp.concatenate([a, b], axis=0)


def exact_square(a_halves, b_halves):
    row = wide(*b_halves)
    both = dot(wide(*a_halves), tall(row, row))
    return both[:, :C] + both[:, C:]


def exact_apply(a_halves, b_hi, b_lo):
    return dot(wide(*a_halves), tall(b_hi, b_hi)) + dot(a_halves[0], b_lo)


def fill_masks(masks):
    row = lax.broadcasted_iota(jnp.int32, (C, C), 0)
    col = lax.broadcasted_iota(jnp.int32, (C, C), 1)
    apart = jnp.where(row > col, row ^ col, 0)
    for i, s in enumerate((1,) + LEVELS):
        masks[i] = jnp.where((apart >= s) & (apart < 2 * s), 1.0, 0.0).astype(BF16)


def chunk_start(k, b_col, g_row, g_col):
    row = lax.broadcasted_iota(jnp.int32, (C, C), 0)
    col = lax.broadcasted_iota(jnp.int32, (C, C), 1)
    gram = dot_nt(k, k)
    diagonal = jnp.where(row == col, gram, 0.0)
    rk_row = lax.rsqrt(jnp.sum(diagonal, axis=0, keepdims=True) + 1e-06)
    rk_col = lax.rsqrt(jnp.sum(diagonal, axis=1, keepdims=True) + 1e-06)
    decay = jnp.exp(jnp.where(row >= col, g_col - g_row, -1e30)) * rk_row
    lower = jnp.where(row > col, decay * gram, 0.0) * (b_col * rk_col)
    return lower, decay, rk_row, rk_col


def invert(lowers, masks, middle):
    row = lax.broadcasted_iota(jnp.int32, (C, C), 0)
    col = lax.broadcasted_iota(jnp.int32, (C, C), 1)
    split = [halves(a) for a in lowers]
    first = masks[0].astype(F32)
    xs = [jnp.where(row == col, 1.0, 0.0) - a * first for a in lowers]
    for i in range(len(LEVELS)):
        mask = masks[i + 1]
        xh = [halves(x) for x in xs]
        ys = [exact_square((hi * mask, lo * mask), x) for (hi, lo), x in zip(split, xh)]
        yh = [halves(y) for y in ys]
        zs = [exact_square(x, y) for x, y in zip(xh, yh)]
        xs = [x - z for x, z in zip(xs, zs)]
        middle(i)
    return xs


def chunk_end(x, k, v, b_row, g_row, g_col, rk_row, rk_col):
    row = lax.broadcasted_iota(jnp.int32, (C, C), 0)
    col = lax.broadcasted_iota(jnp.int32, (C, C), 1)
    carried = dot(wide(*halves(x * b_row)), tall(v, v))
    key_factor = dot(wide(*halves(x * (b_row * jnp.exp(g_row) * rk_row))), tall(k, k))
    pair = wide(-key_factor, carried)
    g_end = g_col[C - 1 :, :]
    pair_hi, pair_lo = halves(pair * (jnp.exp(g_end - g_col) * rk_col))
    kt = k.T
    ab = dot(wide(kt, kt), tall(pair_hi, pair_lo))
    step = ab[:, :C] + jnp.where(row == col, jnp.exp(g_end), 0.0)
    return pair, wide(step, ab[:, C:])


def compose(later, earlier):
    return exact_apply(halves(later[:, :C]), *halves(earlier)) + wide(jnp.zeros((C, C), F32), later[:, C:])


def running_sums(beta, decay_log):
    row = lax.broadcasted_iota(jnp.int32, (C, C), 0)
    col = lax.broadcasted_iota(jnp.int32, (C, C), 1)
    sums = jnp.where(row <= col, 1.0, 0.0)
    logs = jnp.maximum(decay_log, -110.0)
    g = jnp.dot(tall(logs, logs), sums, precision=lax.Precision.HIGHEST, preferred_element_type=F32)
    turned = tall(beta, g[:4]).T
    return [(beta[c : c + 1], turned[:, c : c + 1], g[c : c + 1], turned[:, 4 + c : 5 + c]) for c in range(4)]


def key_side(heads, masks, middle):
    rates = [running_sums(beta, logs) for _, _, beta, logs, _ in heads]
    starts = [[chunk_start(head[0](c), *rate[c][1:]) for c in range(4)] for head, rate in zip(heads, rates)]
    xs = invert([start[0] for four in starts for start in four], masks, middle)
    results = []
    for i, (k_of, v_of, _, _, keep) in enumerate(heads):
        ends = [chunk_end(xs[4 * i + c], k_of(c), v_of(c), rates[i][c][0], *rates[i][c][2:], *starts[i][c][2:])
                for c in range(4)]
        maps = [e[1] for e in ends]
        two = compose(maps[1], maps[0])
        other = compose(maps[3], maps[2])
        three = compose(maps[2], two)
        for c, before in enumerate((None, maps[0], two, three)):
            keep(c, starts[i][c][1], jnp.exp(rates[i][c][3]), ends[c][0], before)
        results.append(compose(other, two))
    return results


def query_side(q, k, decay, growth, pair, before):
    qf = q.astype(F32)
    rq_col = lax.rsqrt(jnp.sum(qf * qf, axis=1, keepdims=True) + 1e-06)
    qo = exact_apply(halves(decay * dot_nt(q, k)), *halves(pair))
    rows_q = (qo[:, :C] + growth * qf) * rq_col
    rows_o = qo[:, C:] * rq_col
    if before is None:
        return rows_q, rows_o
    moved = exact_apply(halves(rows_q), *halves(before))
    return moved[:, :C], rows_o + moved[:, C:]


MESH = pl.DeviceIdType.MESH


def as_item(state):
    hi, lo = halves(state[:, :C])
    return jnp.concatenate([hi, lo, state[:, C:].astype(BF16)], axis=1)


def from_item(item):
    return wide(item[:, :C].astype(F32) + item[:, C : 2 * C].astype(F32), item[:, 2 * C :].astype(F32))


def join(later, earlier):
    hi, lo = halves(earlier)
    return exact_apply((later[:, :C], later[:, C : 2 * C]), hi, lo) + wide(
        jnp.zeros((C, C), F32), later[:, 2 * C :].astype(F32))


def pass_state(item, state):
    return exact_square((item[:, :C], item[:, C : 2 * C]), halves(state)) + item[:, 2 * C :].astype(F32)


def swapped(i):
    return (i % 2) * 2 + i // 2


def layer_kernel(q_in, k_in, v_in, b_in, d_in, w_ref, out_ref,
                 q_ref, k_ref, v_ref, b_ref, d_ref, masks, qs, ks, vs, decays, growths, chunk_pairs, befores, qe, own, items, group, pairs, rows, enters, entering, att, arrived, weight,
                 total, group_maps, entry_maps, entry_adds, state,
                 in_load, w_load, w_send, w_recv, g_send, g_recv, p_send, p_recv, x_send, x_recv, e_send, e_recv,
                 y_send, y_recv):
    seq, head = lax.axis_index("seq"), lax.axis_index("head")
    member, pair, line = seq % 4, (seq // 4) % 4, seq // 16
    core = seq % 2
    base = seq - member
    mine = swapped(member)
    late = mine // 2
    right, left, across = (head + 1) % 4, (head + 3) % 4, (head + 2) % 4

    def in_pairs(step):
        return line * 16 + ((pair + step) % 4) * 4 + member

    barrier = pltpu.get_barrier_semaphore()
    friends = [{"seq": base + (member ^ j)} for j in (1, 2, 3)]
    friends += [{"seq": in_pairs(j)} for j in (1, 2, 3)]
    friends += [{"seq": (seq + 16 * j) % 64} for j in (1, 2, 3)]
    friends += [{"head": (head + j) % 4} for j in (1, 2, 3)]
    for friend in friends:
        pl.semaphore_signal(barrier, inc=1, device_id=friend, device_id_type=MESH)
    loads = [pltpu.make_async_copy(source, target, in_load.at[i]) for i, (source, target) in enumerate(
        ((b_in, b_ref), (d_in, d_ref), (k_in, k_ref), (v_in, v_ref), (q_in, q_ref)))]
    for copy in loads:
        copy.start()
    load = pltpu.make_async_copy(w_ref, weight.at[head], w_load)
    load.start()
    fill_masks(masks)
    for copy in loads[:4]:
        copy.wait()
    for source, target in ((k_ref, ks), (v_ref, vs)):
        target[...] = source[...].astype(F32).reshape(2048, C)

    def copy_to(source, target, send_sem, recv_sem, to):
        return pltpu.make_async_remote_copy(source, target, send_sem, recv_sem, device_id=to, device_id_type=MESH)

    sibling = {"seq": seq ^ 1}
    to_right, to_left = {"head": right}, {"head": left}
    to_next, to_last = {"seq": (seq + 16) % 64}, {"seq": (seq + 48) % 64}
    block = 2 * core + line % 2
    block_x = 2 * core + 1 - line % 2
    top, low = pl.ds(0, 64), pl.ds(64, 64)

    def same(ref, i, to):
        return copy_to(ref, ref, w_send.at[i], w_recv.at[i], to)

    def go_right(of):
        return same(weight.at[of, block], 0, to_right)

    def go_left(of):
        return same(weight.at[of, block], 1, to_left)

    def relay_right(of):
        return same(weight.at[of, block, top], 2, to_right)

    def relay_left(of):
        return same(weight.at[of, block, low], 3, to_left)

    def go_next(of, i, at_block=block):
        return same(weight.at[of, at_block, top], 4 + i, to_next)

    def go_last(of, i, at_block=block):
        return same(weight.at[of, at_block, low], 7 + i, to_last)

    def over(of, i, at_block):
        return same(weight.at[of, at_block], 10 + i, sibling)

    def share(of, i):
        go_next(of, i).start()
        go_last(of, i).start()
        over(of, i, block).start()

    def share_x(of, i):
        go_next(of, i, block_x).wait_recv()
        go_last(of, i, block_x).wait_recv()
        over(of, 3 + i, block_x).start()

    def greet():
        load.wait()
        pl.semaphore_wait(barrier, len(friends))
        go_right(head).start()
        go_left(head).start()

    def item_copy(h):
        return copy_to(items.at[h], group.at[member], g_send.at[h], g_recv.at[member], {"seq": base + swapped(h)})

    def pair_copy(j):
        return copy_to(pairs.at[0], pairs.at[4 - j], p_send.at[j], p_recv.at[j], {"seq": in_pairs(j)})

    def line_copy(j):
        return copy_to(rows.at[line], rows.at[line], x_send.at[j], x_recv.at[j], {"seq": (seq + 16 * j) % 64})

    def enter_copy(j):
        other = member ^ j
        return copy_to(enters.at[other], entering.at[mine], e_send.at[other], e_recv.at[mine],
                       {"seq": base + other})

    def out_copy(h, j):
        return copy_to(att.at[(head + j) % 4, h], arrived.at[j, h], y_send.at[j, h], y_recv.at[j, h],
                       {"head": (head + j) % 4})

    def at(ref, h):
        return lambda c: ref[pl.ds(c * 512 + h, C, stride=4), :].astype(BF16)

    def compute(two):
        def head_of(h):
            def four(ref):
                lines = lax.broadcasted_iota(jnp.int32, (4, 512), 0)
                mine = jnp.sum(jnp.where(lines == h, ref[...], 0.0), axis=0, keepdims=True)
                return jnp.concatenate([mine[:, c * C : (c + 1) * C] for c in range(4)], axis=0)

            def keep(c, decay, growth, pair_here, before):
                decays[h, c] = decay
                growths[h, c] = growth
                chunk_pairs[h, c] = pair_here
                if c:
                    befores[h, c - 1] = before

            return at(ks, h), at(vs, h), four(b_ref), four(d_ref), keep

        def middle(i):
            if i == 0:
                @pl.when(two == 0)
                def _():
                    greet()

            if i == 3:
                @pl.when((two == 1) & (late == 0))
                def _():
                    scan_group()

        heads = [2 * two, 2 * two + 1]
        for h, result in zip(heads, key_side([head_of(h) for h in heads], masks, middle)):
            items[h] = as_item(result)

            @pl.when(h != mine)
            def _():
                item_copy(h).start()

            @pl.when(h == mine)
            def _():
                group[member] = items[h]

        return 0

    def compute_rows(h):
        q_of, k_of = at(qs, h), at(ks, h)
        for c in range(4):
            rows_q, rows_o = query_side(q_of(c), k_of(c), decays[h, c], growths[h, c], chunk_pairs[h, c],
                                        befores[h, c - 1] if c else None)
            qe[h, c * C : (c + 1) * C, :] = rows_q.astype(BF16)
            own[h, c * C : (c + 1) * C, :] = rows_o

    def scan_group():
        for j in (1, 2, 3):
            other = member ^ j
            copy_to(group.at[other], group.at[other], g_send.at[other], g_recv.at[other],
                    {"seq": base + other}).wait_recv()
        early = join(group[1], from_item(group[0]))
        late = as_item(join(group[3], from_item(group[2])))
        pairs[0] = as_item(join(late, early))
        for j in (2, 1, 3):
            pair_copy(j).start()
        group_maps[0] = group[0]
        group_maps[1] = as_item(early)
        group_maps[2] = as_item(join(group[2], early))

    def scan_pairs():
        for j in (1, 3, 2):
            pair_copy(j).wait_recv()
        at_pair = [pairs[(j + 4 - pair) % 4] for j in range(4)]
        first = from_item(at_pair[0])
        early = join(at_pair[1], first)
        late = as_item(join(at_pair[3], from_item(at_pair[2])))
        rows[line] = as_item(join(late, early))
        for j in (2, 1, 3):
            @pl.when(line + j < 4)
            def _():
                line_copy(j).start()
        eye = jnp.where(
            lax.broadcasted_iota(jnp.int32, (C, 2 * C), 0) == lax.broadcasted_iota(jnp.int32, (C, 2 * C), 1), 1.0, 0.0)
        before = jnp.where(pair == 0, eye, first)
        before = jnp.where(pair > 1, early, before)
        before = jnp.where(pair > 2, join(at_pair[2], early), before)
        for i in range(4):
            here = join(group_maps[i - 1], before) if i else before
            hi, lo = halves(here[:, :C])
            entry_maps[i * C : (i + 1) * C, :C] = hi
            entry_maps[i * C : (i + 1) * C, C:] = lo
            entry_adds[i * C : (i + 1) * C, :] = here[:, C:]

    def scan_lines():
        state[...] = jnp.zeros((C, C), F32)
        for i in range(3):
            @pl.when(line > i)
            def _():
                copy_to(rows.at[i], rows.at[i], x_send.at[line - i], x_recv.at[line - i],
                        {"seq": (seq + 16) % 64}).wait_recv()
                if i == 0:
                    state[...] = rows[0, :, 2 * C :].astype(F32)
                else:
                    state[...] = pass_state(rows[i], state[...])

        row = wide(*halves(state[...]))
        both = dot(entry_maps[...], tall(row, row))
        all_four = (both[:, :C] + both[:, C:] + entry_adds[...]).astype(BF16)
        for i in range(4):
            enters[i] = all_four[i * C : (i + 1) * C]
        for j in (1, 2, 3):
            enter_copy(j).start()
        entering[mine] = enters[member]

    def apply(h):
        @pl.when(mine != h)
        def _():
            copy_to(entering.at[h], entering.at[h], e_send.at[h], e_recv.at[h],
                    {"seq": base + swapped(h)}).wait_recv()
        rows_here = dot(qe[h], entering[h]) + own[h]
        for t in range(4):
            att[t, h] = rows_here[t * C : (t + 1) * C].astype(BF16)
        for j in (2, 1, 3):
            out_copy(h, j).start()

    lax.fori_loop(0, 2, lambda two, _: compute(two), 0)
    go_right(left).wait_recv()
    relay_right(left).start()
    go_left(right).wait_recv()
    relay_left(right).start()
    share(left, 0)
    share(right, 1)
    loads[4].wait()
    qs[...] = q_ref[...].astype(F32).reshape(2048, C)

    def step_out(h, _):
        apply(h)
        return 0

    def step(t, _):
        compute_rows(t)

        @pl.when(t == 3)
        def _():
            lax.fori_loop(0, 2, step_out, 0)

        @pl.when((t == 0) & (late == 1))
        def _():
            scan_group()

        @pl.when(t == late + 1)
        def _():
            scan_pairs()

        @pl.when(t == late + 2)
        def _():
            scan_lines()

        @pl.when(t == 1)
        def _():
            relay_right(across).wait_recv()
            relay_left(across).wait_recv()
            share(across, 2)

        @pl.when(t == 2)
        def _():
            share_x(left, 0)
            share_x(right, 1)

        return 0

    lax.fori_loop(0, 4, step, 0)

    lax.fori_loop(2, 4, step_out, 0)

    share_x(across, 2)
    go_right(head).wait_send()
    go_left(head).wait_send()
    relay_right(left).wait_send()
    relay_left(right).wait_send()
    for j in (1, 2, 3):
        item_copy(swapped(member ^ j)).wait_send()
        pair_copy(j).wait_send()
        enter_copy(j).wait_send()

        @pl.when(line + j < 4)
        def _():
            line_copy(j).wait_send()

    for i, of in enumerate((left, right, across)):
        go_next(of, i).wait_send()
        go_last(of, i).wait_send()
        for k, at_block in ((0, block), (3, block_x)):
            over(of, i + k, at_block).wait_send()
            over(of, i + k, (at_block + 2) % 4).wait_recv()

    def product(heads, cols):
        rows_in = jnp.concatenate(
            [att[head, h] if j == 0 else arrived[j, h] for j in range(4) for h in heads], axis=1)
        rows_w = jnp.concatenate(
            [weight[(head + 4 - j) % 4, h, :, cols] for j in range(4) for h in heads], axis=0)
        return dot(rows_in, rows_w)

    for h in range(3):
        for j in (1, 3, 2):
            out_copy(h, j).wait()
    for n in range(4):
        total[:, n * 512 : (n + 1) * 512] = product((0, 1, 2), slice(n * 512, (n + 1) * 512))
    for j in (1, 3, 2):
        out_copy(3, j).wait()
    for n in range(4):
        cols = slice(n * 512, (n + 1) * 512)
        out_ref[:, cols] = (total[:, cols] + product((3,), cols)).astype(BF16)


def layer(q, k, v, b, d, w):
    vmem = pl.BlockSpec(memory_space=pltpu.VMEM)
    dma = pltpu.SemaphoreType.DMA
    return pl.pallas_call(
        layer_kernel,
        out_shape=jax.ShapeDtypeStruct((128, 2048), BF16),
        in_specs=[pl.BlockSpec(memory_space=pltpu.HBM)] * 6,
        out_specs=vmem,
        scratch_shapes=[pltpu.VMEM((512, 4, C), BF16)] * 3 + [pltpu.VMEM((4, 512), F32)] * 2 + [
            pltpu.VMEM((7, C, C), BF16),
            pltpu.VMEM((2048, C), F32),
            pltpu.VMEM((2048, C), F32),
            pltpu.VMEM((2048, C), F32),
            pltpu.VMEM((4, 4, C, C), F32),
            pltpu.VMEM((4, 4, C, 1), F32),
            pltpu.VMEM((4, 4, C, 2 * C), F32),
            pltpu.VMEM((4, 3, C, 2 * C), F32),
            pltpu.VMEM((4, 512, C), BF16),
            pltpu.VMEM((4, 512, C), F32),
            pltpu.VMEM((4, C, 3 * C), BF16),
            pltpu.VMEM((4, C, 3 * C), BF16),
            pltpu.VMEM((4, C, 3 * C), BF16),
            pltpu.VMEM((4, C, 3 * C), BF16),
            pltpu.VMEM((4, C, C), BF16),
            pltpu.VMEM((4, C, C), BF16),
            pltpu.VMEM((4, 4, C, C), BF16),
            pltpu.VMEM((4, 4, C, C), BF16),
            pltpu.VMEM((4, 4, C, 2048), BF16),
            pltpu.VMEM((C, 2048), F32),
            pltpu.VMEM((3, C, 3 * C), BF16),
            pltpu.VMEM((4 * C, 2 * C), BF16),
            pltpu.VMEM((4 * C, C), F32),
            pltpu.VMEM((C, C), F32),
            dma((5,)), dma, dma((16,)), dma((16,)),
        ] + [dma((4,))] * 8 + [dma((4, 4))] * 2,
        compiler_params=pltpu.CompilerParams(
            collective_id=0, has_side_effects=True, vmem_limit_bytes=40 * 2**20),
    )(q, k, v, b, d, w)


def body(query, key, value, beta, log_decay, out_weight):
    stay = lambda a: pltpu.with_memory_space_constraint(a, pltpu.HBM)
    return layer(stay(query), stay(key), stay(value), stay(beta), stay(log_decay), stay(out_weight.reshape(4, C, 2048)))


def solution(mesh):
    in_specs = (
        P("seq", "head", None),
        P("seq", "head", None),
        P("seq", "head", None),
        P("head", "seq"),
        P("head", "seq"),
        P("head", None),
    )
    out_specs = P(("seq", "head"), None)
    return jax.shard_map(body, mesh=mesh, in_specs=in_specs, out_specs=out_specs, check_vma=False)
```

```python
import jax
import jax.numpy as jnp
from jax import lax
from jax.experimental import pallas as pl
from jax.experimental.pallas import tpu as pltpu
from jax.sharding import PartitionSpec as P

C = 128
LEVELS = (2, 4, 8, 16, 32, 64)
F32, BF16 = jnp.float32, jnp.bfloat16


def dot(a, b):
    return jnp.dot(a, b, preferred_element_type=F32)


def dot_nt(a, b, precision=None):
    return lax.dot_general(a, b, (((1,), (1,)), ((), ())), precision=precision, preferred_element_type=F32)


def halves(a):
    hi = a.astype(BF16)
    return hi, (a - hi.astype(F32)).astype(BF16)


def wide(a, b):
    return jnp.concatenate([a, b], axis=1)


def tall(a, b):
    return jnp.concatenate([a, b], axis=0)


def exact_square(a_halves, b_halves):
    row = wide(*b_halves)
    both = dot(wide(*a_halves), tall(row, row))
    return both[:, :C] + both[:, C:]


def exact_apply(a_halves, b_hi, b_lo):
    return dot(wide(*a_halves), tall(b_hi, b_hi)) + dot(a_halves[0], b_lo)


def fill_masks(masks):
    row = lax.broadcasted_iota(jnp.int32, (C, C), 0)
    col = lax.broadcasted_iota(jnp.int32, (C, C), 1)
    apart = jnp.where(row > col, row ^ col, 0)
    for i, s in enumerate((1,) + LEVELS):
        masks[i] = jnp.where((apart >= s) & (apart < 2 * s), 1.0, 0.0).astype(BF16)


def chunk_start(k, b_col, g_row, g_col):
    row = lax.broadcasted_iota(jnp.int32, (C, C), 0)
    col = lax.broadcasted_iota(jnp.int32, (C, C), 1)
    gram = dot_nt(k, k)
    diagonal = jnp.where(row == col, gram, 0.0)
    rk_row = lax.rsqrt(jnp.sum(diagonal, axis=0, keepdims=True) + 1e-06)
    rk_col = lax.rsqrt(jnp.sum(diagonal, axis=1, keepdims=True) + 1e-06)
    decay = jnp.exp(jnp.where(row >= col, g_col - g_row, -1e30)) * rk_row
    lower = jnp.where(row > col, decay * gram, 0.0) * (b_col * rk_col)
    return lower, decay, rk_row, rk_col


def invert(lowers, masks, middle):
    row = lax.broadcasted_iota(jnp.int32, (C, C), 0)
    col = lax.broadcasted_iota(jnp.int32, (C, C), 1)
    split = [halves(a) for a in lowers]
    first = masks[0].astype(F32)
    xs = [jnp.where(row == col, 1.0, 0.0) - a * first for a in lowers]
    for i in range(len(LEVELS)):
        mask = masks[i + 1]
        xh = [halves(x) for x in xs]
        ys = [exact_square((hi * mask, lo * mask), x) for (hi, lo), x in zip(split, xh)]
        yh = [halves(y) for y in ys]
        zs = [exact_square(x, y) for x, y in zip(xh, yh)]
        xs = [x - z for x, z in zip(xs, zs)]
        middle(i)
    return xs


def chunk_end(x, k, v, b_row, g_row, g_col, rk_row, rk_col):
    row = lax.broadcasted_iota(jnp.int32, (C, C), 0)
    col = lax.broadcasted_iota(jnp.int32, (C, C), 1)
    carried = dot(wide(*halves(x * b_row)), tall(v, v))
    key_factor = dot(wide(*halves(x * (b_row * jnp.exp(g_row) * rk_row))), tall(k, k))
    pair = wide(-key_factor, carried)
    g_end = g_col[C - 1 :, :]
    pair_hi, pair_lo = halves(pair * (jnp.exp(g_end - g_col) * rk_col))
    kt = k.T
    ab = dot(wide(kt, kt), tall(pair_hi, pair_lo))
    step = ab[:, :C] + jnp.where(row == col, jnp.exp(g_end), 0.0)
    return pair, wide(step, ab[:, C:])


def compose(later, earlier):
    return exact_apply(halves(later[:, :C]), *halves(earlier)) + wide(jnp.zeros((C, C), F32), later[:, C:])


def running_sums(beta, decay_log):
    row = lax.broadcasted_iota(jnp.int32, (C, C), 0)
    col = lax.broadcasted_iota(jnp.int32, (C, C), 1)
    sums = jnp.where(row <= col, 1.0, 0.0)
    logs = jnp.maximum(decay_log, -110.0)
    g = jnp.dot(tall(logs, logs), sums, precision=lax.Precision.HIGHEST, preferred_element_type=F32)
    turned = tall(beta, g[:4]).T
    return [(beta[c : c + 1], turned[:, c : c + 1], g[c : c + 1], turned[:, 4 + c : 5 + c]) for c in range(4)]


def key_side(heads, masks, middle):
    rates = [running_sums(beta, logs) for _, _, beta, logs, _ in heads]
    starts = [[chunk_start(head[0](c), *rate[c][1:]) for c in range(4)] for head, rate in zip(heads, rates)]
    xs = invert([start[0] for four in starts for start in four], masks, middle)
    results = []
    for i, (k_of, v_of, _, _, keep) in enumerate(heads):
        ends = [chunk_end(xs[4 * i + c], k_of(c), v_of(c), rates[i][c][0], *rates[i][c][2:], *starts[i][c][2:])
                for c in range(4)]
        maps = [e[1] for e in ends]
        two = compose(maps[1], maps[0])
        other = compose(maps[3], maps[2])
        three = compose(maps[2], two)
        for c, before in enumerate((None, maps[0], two, three)):
            keep(c, starts[i][c][1], jnp.exp(rates[i][c][3]), ends[c][0], before)
        results.append(compose(other, two))
    return results


def query_side(q, k, decay, growth, pair, before):
    qf = q.astype(F32)
    rq_col = lax.rsqrt(jnp.sum(qf * qf, axis=1, keepdims=True) + 1e-06)
    qo = exact_apply(halves(decay * dot_nt(q, k)), *halves(pair))
    rows_q = (qo[:, :C] + growth * qf) * rq_col
    rows_o = qo[:, C:] * rq_col
    if before is None:
        return rows_q, rows_o
    moved = exact_apply(halves(rows_q), *halves(before))
    return moved[:, :C], rows_o + moved[:, C:]


MESH = pl.DeviceIdType.MESH


def as_item(state):
    hi, lo = halves(state[:, :C])
    return jnp.concatenate([hi, lo, state[:, C:].astype(BF16)], axis=1)


def from_item(item):
    return wide(item[:, :C].astype(F32) + item[:, C : 2 * C].astype(F32), item[:, 2 * C :].astype(F32))


def join(later, earlier):
    hi, lo = halves(earlier)
    return exact_apply((later[:, :C], later[:, C : 2 * C]), hi, lo) + wide(
        jnp.zeros((C, C), F32), later[:, 2 * C :].astype(F32))


def pass_state(item, state):
    return exact_square((item[:, :C], item[:, C : 2 * C]), halves(state)) + item[:, 2 * C :].astype(F32)


def swapped(i):
    return (i % 2) * 2 + i // 2


def layer_kernel(q_in, k_in, v_in, b_in, d_in, w_ref, out_ref,
                 q_ref, k_ref, v_ref, b_ref, d_ref, masks, qs, ks, vs, decays, growths, chunk_pairs, befores, qe, own, items, group, pairs, rows, enters, entering, att, arrived, weight,
                 total, group_maps, entry_maps, entry_adds, state,
                 in_load, w_load, w_send, w_recv, g_send, g_recv, p_send, p_recv, x_send, x_recv, e_send, e_recv,
                 y_send, y_recv):
    seq, head = lax.axis_index("seq"), lax.axis_index("head")
    member, pair, line = seq % 4, (seq // 4) % 4, seq // 16
    core = seq % 2
    base = seq - member
    mine = swapped(member)
    late = mine // 2
    right, left, across = (head + 1) % 4, (head + 3) % 4, (head + 2) % 4

    def in_pairs(step):
        return line * 16 + ((pair + step) % 4) * 4 + member

    barrier = pltpu.get_barrier_semaphore()
    friends = [{"seq": base + (member ^ j)} for j in (1, 2, 3)]
    friends += [{"seq": in_pairs(j)} for j in (1, 2, 3)]
    friends += [{"seq": (seq + 16 * j) % 64} for j in (1, 2, 3)]
    friends += [{"head": (head + j) % 4} for j in (1, 2, 3)]
    for friend in friends:
        pl.semaphore_signal(barrier, inc=1, device_id=friend, device_id_type=MESH)
    loads = [pltpu.make_async_copy(source, target, in_load.at[i]) for i, (source, target) in enumerate(
        ((b_in, b_ref), (d_in, d_ref), (k_in, k_ref), (v_in, v_ref), (q_in, q_ref)))]
    for copy in loads:
        copy.start()
    load = pltpu.make_async_copy(w_ref, weight.at[head], w_load)
    load.start()
    fill_masks(masks)
    for copy in loads[:4]:
        copy.wait()

    def copy_to(source, target, send_sem, recv_sem, to):
        return pltpu.make_async_remote_copy(source, target, send_sem, recv_sem, device_id=to, device_id_type=MESH)

    sibling = {"seq": seq ^ 1}
    to_right, to_left = {"head": right}, {"head": left}
    to_next, to_last = {"seq": (seq + 16) % 64}, {"seq": (seq + 48) % 64}
    block = 2 * core + line % 2
    block_x = 2 * core + 1 - line % 2
    top, low = pl.ds(0, 64), pl.ds(64, 64)

    def same(ref, i, to):
        return copy_to(ref, ref, w_send.at[i], w_recv.at[i], to)

    def go_right(of):
        return same(weight.at[of, block], 0, to_right)

    def go_left(of):
        return same(weight.at[of, block], 1, to_left)

    def relay_right(of):
        return same(weight.at[of, block, top], 2, to_right)

    def relay_left(of):
        return same(weight.at[of, block, low], 3, to_left)

    def go_next(of, i, at_block=block):
        return same(weight.at[of, at_block, top], 4 + i, to_next)

    def go_last(of, i, at_block=block):
        return same(weight.at[of, at_block, low], 7 + i, to_last)

    def over(of, i, at_block):
        return same(weight.at[of, at_block], 10 + i, sibling)

    def share(of, i):
        go_next(of, i).start()
        go_last(of, i).start()
        over(of, i, block).start()

    def share_x(of, i):
        go_next(of, i, block_x).wait_recv()
        go_last(of, i, block_x).wait_recv()
        over(of, 3 + i, block_x).start()

    load.wait()
    pl.semaphore_wait(barrier, len(friends))
    go_right(head).start()
    go_left(head).start()
    for source, target in ((k_ref, ks), (v_ref, vs)):
        target[...] = source[...].astype(F32).reshape(2048, C)

    def item_copy(h):
        return copy_to(items.at[h], group.at[member], g_send.at[h], g_recv.at[member], {"seq": base + swapped(h)})

    def pair_copy(j):
        return copy_to(pairs.at[0], pairs.at[4 - j], p_send.at[j], p_recv.at[j], {"seq": in_pairs(j)})

    def line_copy(j):
        return copy_to(rows.at[line], rows.at[line], x_send.at[j], x_recv.at[j], {"seq": (seq + 16 * j) % 64})

    def enter_copy(j):
        other = member ^ j
        return copy_to(enters.at[other], entering.at[mine], e_send.at[other], e_recv.at[mine],
                       {"seq": base + other})

    def out_copy(h, j):
        return copy_to(att.at[(head + j) % 4, h], arrived.at[j, h], y_send.at[j, h], y_recv.at[j, h],
                       {"head": (head + j) % 4})

    def at(ref, h):
        return lambda c: ref[pl.ds(c * 512 + h, C, stride=4), :].astype(BF16)

    def compute(two):
        def head_of(h):
            def four(ref):
                lines = lax.broadcasted_iota(jnp.int32, (4, 512), 0)
                mine = jnp.sum(jnp.where(lines == h, ref[...], 0.0), axis=0, keepdims=True)
                return jnp.concatenate([mine[:, c * C : (c + 1) * C] for c in range(4)], axis=0)

            def keep(c, decay, growth, pair_here, before):
                decays[h, c] = decay
                growths[h, c] = growth
                chunk_pairs[h, c] = pair_here
                if c:
                    befores[h, c - 1] = before

            return at(ks, h), at(vs, h), four(b_ref), four(d_ref), keep

        def middle(i):
            if i == 3:
                @pl.when((two == 1) & (late == 0))
                def _():
                    scan_group()

            if i == 4:
                @pl.when(two == 1)
                def _():
                    go_right(left).wait_recv()
                    relay_right(left).start()
                    go_left(right).wait_recv()
                    relay_left(right).start()
                    share(left, 0)
                    share(right, 1)

        heads = [2 * two, 2 * two + 1]
        for h, result in zip(heads, key_side([head_of(h) for h in heads], masks, middle)):
            items[h] = as_item(result)

            @pl.when(h != mine)
            def _():
                item_copy(h).start()

            @pl.when(h == mine)
            def _():
                group[member] = items[h]

        return 0

    def compute_rows(h):
        q_of, k_of = at(qs, h), at(ks, h)
        for c in range(4):
            rows_q, rows_o = query_side(q_of(c), k_of(c), decays[h, c], growths[h, c], chunk_pairs[h, c],
                                        befores[h, c - 1] if c else None)
            qe[h, c * C : (c + 1) * C, :] = rows_q.astype(BF16)
            own[h, c * C : (c + 1) * C, :] = rows_o

    def scan_group():
        for j in (1, 2, 3):
            other = member ^ j
            copy_to(group.at[other], group.at[other], g_send.at[other], g_recv.at[other],
                    {"seq": base + other}).wait_recv()
        early = join(group[1], from_item(group[0]))
        late = as_item(join(group[3], from_item(group[2])))
        pairs[0] = as_item(join(late, early))
        for j in (2, 1, 3):
            pair_copy(j).start()
        group_maps[0] = group[0]
        group_maps[1] = as_item(early)
        group_maps[2] = as_item(join(group[2], early))

    def scan_pairs():
        for j in (1, 3, 2):
            pair_copy(j).wait_recv()
        at_pair = [pairs[(j + 4 - pair) % 4] for j in range(4)]
        first = from_item(at_pair[0])
        early = join(at_pair[1], first)
        late = as_item(join(at_pair[3], from_item(at_pair[2])))
        rows[line] = as_item(join(late, early))
        for j in (2, 1, 3):
            @pl.when(line + j < 4)
            def _():
                line_copy(j).start()
        eye = jnp.where(
            lax.broadcasted_iota(jnp.int32, (C, 2 * C), 0) == lax.broadcasted_iota(jnp.int32, (C, 2 * C), 1), 1.0, 0.0)
        before = jnp.where(pair == 0, eye, first)
        before = jnp.where(pair > 1, early, before)
        before = jnp.where(pair > 2, join(at_pair[2], early), before)
        for i in range(4):
            here = join(group_maps[i - 1], before) if i else before
            hi, lo = halves(here[:, :C])
            entry_maps[i * C : (i + 1) * C, :C] = hi
            entry_maps[i * C : (i + 1) * C, C:] = lo
            entry_adds[i * C : (i + 1) * C, :] = here[:, C:]

    def scan_lines():
        state[...] = jnp.zeros((C, C), F32)
        for i in range(3):
            @pl.when(line > i)
            def _():
                copy_to(rows.at[i], rows.at[i], x_send.at[line - i], x_recv.at[line - i],
                        {"seq": (seq + 16) % 64}).wait_recv()
                if i == 0:
                    state[...] = rows[0, :, 2 * C :].astype(F32)
                else:
                    state[...] = pass_state(rows[i], state[...])

        row = wide(*halves(state[...]))
        both = dot(entry_maps[...], tall(row, row))
        all_four = (both[:, :C] + both[:, C:] + entry_adds[...]).astype(BF16)
        for i in range(4):
            enters[i] = all_four[i * C : (i + 1) * C]
        for j in (1, 2, 3):
            enter_copy(j).start()
        entering[mine] = enters[member]

    def apply(h):
        @pl.when(mine != h)
        def _():
            copy_to(entering.at[h], entering.at[h], e_send.at[h], e_recv.at[h],
                    {"seq": base + swapped(h)}).wait_recv()
        rows_here = dot(qe[h], entering[h]) + own[h]
        for t in range(4):
            att[t, h] = rows_here[t * C : (t + 1) * C].astype(BF16)
        for j in (2, 1, 3):
            out_copy(h, j).start()

    lax.fori_loop(0, 2, lambda two, _: compute(two), 0)
    loads[4].wait()
    qs[...] = q_ref[...].astype(F32).reshape(2048, C)

    def step_out(h, _):
        apply(h)
        return 0

    def step(t, _):
        compute_rows(t)

        @pl.when(t == 3)
        def _():
            lax.fori_loop(0, 2, step_out, 0)

        @pl.when((t == 0) & (late == 1))
        def _():
            scan_group()

        @pl.when(t == late + 1)
        def _():
            scan_pairs()

        @pl.when(t == late + 2)
        def _():
            scan_lines()

        @pl.when(t == 0)
        def _():
            relay_right(across).wait_recv()
            relay_left(across).wait_recv()
            share(across, 2)

        @pl.when(t == 1)
        def _():
            share_x(left, 0)
            share_x(right, 1)

        @pl.when(t == 2)
        def _():
            share_x(across, 2)

        return 0

    lax.fori_loop(0, 4, step, 0)

    lax.fori_loop(2, 4, step_out, 0)

    go_right(head).wait_send()
    go_left(head).wait_send()
    relay_right(left).wait_send()
    relay_left(right).wait_send()
    for j in (1, 2, 3):
        item_copy(swapped(member ^ j)).wait_send()
        pair_copy(j).wait_send()
        enter_copy(j).wait_send()

        @pl.when(line + j < 4)
        def _():
            line_copy(j).wait_send()

    for i, of in enumerate((left, right, across)):
        go_next(of, i).wait_send()
        go_last(of, i).wait_send()
        for k, at_block in ((0, block), (3, block_x)):
            over(of, i + k, at_block).wait_send()
            over(of, i + k, (at_block + 2) % 4).wait_recv()

    def product(heads, cols):
        rows_in = jnp.concatenate(
            [att[head, h] if j == 0 else arrived[j, h] for j in range(4) for h in heads], axis=1)
        rows_w = jnp.concatenate(
            [weight[(head + 4 - j) % 4, h, :, cols] for j in range(4) for h in heads], axis=0)
        return dot(rows_in, rows_w)

    for h in range(3):
        for j in (1, 3, 2):
            out_copy(h, j).wait()
    for n in range(4):
        total[:, n * 512 : (n + 1) * 512] = product((0, 1, 2), slice(n * 512, (n + 1) * 512))
    for j in (1, 3, 2):
        out_copy(3, j).wait()
    for n in range(4):
        cols = slice(n * 512, (n + 1) * 512)
        out_ref[:, cols] = (total[:, cols] + product((3,), cols)).astype(BF16)


def layer(q, k, v, b, d, w):
    vmem = pl.BlockSpec(memory_space=pltpu.VMEM)
    dma = pltpu.SemaphoreType.DMA
    return pl.pallas_call(
        layer_kernel,
        out_shape=jax.ShapeDtypeStruct((128, 2048), BF16),
        in_specs=[pl.BlockSpec(memory_space=pltpu.HBM)] * 6,
        out_specs=vmem,
        scratch_shapes=[pltpu.VMEM((512, 4, C), BF16)] * 3 + [pltpu.VMEM((4, 512), F32)] * 2 + [
            pltpu.VMEM((7, C, C), BF16),
            pltpu.VMEM((2048, C), F32),
            pltpu.VMEM((2048, C), F32),
            pltpu.VMEM((2048, C), F32),
            pltpu.VMEM((4, 4, C, C), F32),
            pltpu.VMEM((4, 4, C, 1), F32),
            pltpu.VMEM((4, 4, C, 2 * C), F32),
            pltpu.VMEM((4, 3, C, 2 * C), F32),
            pltpu.VMEM((4, 512, C), BF16),
            pltpu.VMEM((4, 512, C), F32),
            pltpu.VMEM((4, C, 3 * C), BF16),
            pltpu.VMEM((4, C, 3 * C), BF16),
            pltpu.VMEM((4, C, 3 * C), BF16),
            pltpu.VMEM((4, C, 3 * C), BF16),
            pltpu.VMEM((4, C, C), BF16),
            pltpu.VMEM((4, C, C), BF16),
            pltpu.VMEM((4, 4, C, C), BF16),
            pltpu.VMEM((4, 4, C, C), BF16),
            pltpu.VMEM((4, 4, C, 2048), BF16),
            pltpu.VMEM((C, 2048), F32),
            pltpu.VMEM((3, C, 3 * C), BF16),
            pltpu.VMEM((4 * C, 2 * C), BF16),
            pltpu.VMEM((4 * C, C), F32),
            pltpu.VMEM((C, C), F32),
            dma((5,)), dma, dma((16,)), dma((16,)),
        ] + [dma((4,))] * 8 + [dma((4, 4))] * 2,
        compiler_params=pltpu.CompilerParams(
            collective_id=0, has_side_effects=True, vmem_limit_bytes=40 * 2**20),
    )(q, k, v, b, d, w)


def body(query, key, value, beta, log_decay, out_weight):
    stay = lambda a: pltpu.with_memory_space_constraint(a, pltpu.HBM)
    return layer(stay(query), stay(key), stay(value), stay(beta), stay(log_decay), stay(out_weight.reshape(4, C, 2048)))


def solution(mesh):
    in_specs = (
        P("seq", "head", None),
        P("seq", "head", None),
        P("seq", "head", None),
        P("head", "seq"),
        P("head", "seq"),
        P("head", None),
    )
    out_specs = P(("seq", "head"), None)
    return jax.shard_map(body, mesh=mesh, in_specs=in_specs, out_specs=out_specs, check_vma=False)
```

```python
import jax
import jax.numpy as jnp
from jax import lax
from jax.experimental import pallas as pl
from jax.experimental.pallas import tpu as pltpu
from jax.sharding import PartitionSpec as P

C = 128
LEVELS = (2, 4, 8, 16, 32, 64)
F32, BF16 = jnp.float32, jnp.bfloat16


def dot(a, b):
    return jnp.dot(a, b, preferred_element_type=F32)


def dot_nt(a, b, precision=None):
    return lax.dot_general(a, b, (((1,), (1,)), ((), ())), precision=precision, preferred_element_type=F32)


def halves(a):
    hi = a.astype(BF16)
    return hi, (a - hi.astype(F32)).astype(BF16)


def wide(a, b):
    return jnp.concatenate([a, b], axis=1)


def tall(a, b):
    return jnp.concatenate([a, b], axis=0)


def exact_square(a_halves, b_halves):
    row = wide(*b_halves)
    both = dot(wide(*a_halves), tall(row, row))
    return both[:, :C] + both[:, C:]


def exact_apply(a_halves, b_hi, b_lo):
    return dot(wide(*a_halves), tall(b_hi, b_hi)) + dot(a_halves[0], b_lo)


def fill_masks(masks):
    row = lax.broadcasted_iota(jnp.int32, (C, C), 0)
    col = lax.broadcasted_iota(jnp.int32, (C, C), 1)
    apart = jnp.where(row > col, row ^ col, 0)
    for i, s in enumerate((1,) + LEVELS):
        masks[i] = jnp.where((apart >= s) & (apart < 2 * s), 1.0, 0.0).astype(BF16)


def chunk_start(k, b_col, g_row, g_col):
    row = lax.broadcasted_iota(jnp.int32, (C, C), 0)
    col = lax.broadcasted_iota(jnp.int32, (C, C), 1)
    gram = dot_nt(k, k)
    diagonal = jnp.where(row == col, gram, 0.0)
    rk_row = lax.rsqrt(jnp.sum(diagonal, axis=0, keepdims=True) + 1e-06)
    rk_col = lax.rsqrt(jnp.sum(diagonal, axis=1, keepdims=True) + 1e-06)
    decay = jnp.exp(jnp.where(row >= col, g_col - g_row, -1e30)) * rk_row
    lower = jnp.where(row > col, decay * gram, 0.0) * (b_col * rk_col)
    return lower, decay, rk_row, rk_col


def invert(lowers, masks, middle):
    row = lax.broadcasted_iota(jnp.int32, (C, C), 0)
    col = lax.broadcasted_iota(jnp.int32, (C, C), 1)
    split = [halves(a) for a in lowers]
    first = masks[0].astype(F32)
    xs = [jnp.where(row == col, 1.0, 0.0) - a * first for a in lowers]
    for i in range(len(LEVELS)):
        mask = masks[i + 1]
        xh = [halves(x) for x in xs]
        ys = [exact_square((hi * mask, lo * mask), x) for (hi, lo), x in zip(split, xh)]
        yh = [halves(y) for y in ys]
        zs = [exact_square(x, y) for x, y in zip(xh, yh)]
        xs = [x - z for x, z in zip(xs, zs)]
        middle(i)
    return xs


def chunk_end(x, k, v, b_row, g_row, g_col, rk_row, rk_col):
    row = lax.broadcasted_iota(jnp.int32, (C, C), 0)
    col = lax.broadcasted_iota(jnp.int32, (C, C), 1)
    carried = dot(wide(*halves(x * b_row)), tall(v, v))
    key_factor = dot(wide(*halves(x * (b_row * jnp.exp(g_row) * rk_row))), tall(k, k))
    pair = wide(-key_factor, carried)
    g_end = g_col[C - 1 :, :]
    pair_hi, pair_lo = halves(pair * (jnp.exp(g_end - g_col) * rk_col))
    kt = k.T
    ab = dot(wide(kt, kt), tall(pair_hi, pair_lo))
    step = ab[:, :C] + jnp.where(row == col, jnp.exp(g_end), 0.0)
    return pair, wide(step, ab[:, C:])


def compose(later, earlier):
    return exact_apply(halves(later[:, :C]), *halves(earlier)) + wide(jnp.zeros((C, C), F32), later[:, C:])


def running_sums(beta, decay_log):
    row = lax.broadcasted_iota(jnp.int32, (C, C), 0)
    col = lax.broadcasted_iota(jnp.int32, (C, C), 1)
    sums = jnp.where(row <= col, 1.0, 0.0)
    logs = jnp.maximum(decay_log, -110.0)
    g = jnp.dot(tall(logs, logs), sums, precision=lax.Precision.HIGHEST, preferred_element_type=F32)
    turned = tall(beta, g[:4]).T
    return [(beta[c : c + 1], turned[:, c : c + 1], g[c : c + 1], turned[:, 4 + c : 5 + c]) for c in range(4)]


def key_side(heads, masks, middle):
    rates = [running_sums(beta, logs) for _, _, beta, logs, _ in heads]
    starts = [[chunk_start(head[0](c), *rate[c][1:]) for c in range(4)] for head, rate in zip(heads, rates)]
    xs = invert([start[0] for four in starts for start in four], masks, middle)
    results = []
    for i, (k_of, v_of, _, _, keep) in enumerate(heads):
        ends = [chunk_end(xs[4 * i + c], k_of(c), v_of(c), rates[i][c][0], *rates[i][c][2:], *starts[i][c][2:])
                for c in range(4)]
        maps = [e[1] for e in ends]
        two = compose(maps[1], maps[0])
        other = compose(maps[3], maps[2])
        three = compose(maps[2], two)
        for c, before in enumerate((None, maps[0], two, three)):
            keep(c, starts[i][c][1], jnp.exp(rates[i][c][3]), ends[c][0], before)
        results.append(compose(other, two))
    return results


def query_side(q, k, decay, growth, pair, before):
    qf = q.astype(F32)
    rq_col = lax.rsqrt(jnp.sum(qf * qf, axis=1, keepdims=True) + 1e-06)
    qo = exact_apply(halves(decay * dot_nt(q, k)), *halves(pair))
    rows_q = (qo[:, :C] + growth * qf) * rq_col
    rows_o = qo[:, C:] * rq_col
    if before is None:
        return rows_q, rows_o
    moved = exact_apply(halves(rows_q), *halves(before))
    return moved[:, :C], rows_o + moved[:, C:]


MESH = pl.DeviceIdType.MESH


def as_item(state):
    hi, lo = halves(state[:, :C])
    return jnp.concatenate([hi, lo, state[:, C:].astype(BF16)], axis=1)


def from_item(item):
    return wide(item[:, :C].astype(F32) + item[:, C : 2 * C].astype(F32), item[:, 2 * C :].astype(F32))


def join(later, earlier):
    hi, lo = halves(earlier)
    return exact_apply((later[:, :C], later[:, C : 2 * C]), hi, lo) + wide(
        jnp.zeros((C, C), F32), later[:, 2 * C :].astype(F32))


def pass_state(item, state):
    return exact_square((item[:, :C], item[:, C : 2 * C]), halves(state)) + item[:, 2 * C :].astype(F32)


def swapped(i):
    return (i % 2) * 2 + i // 2


def layer_kernel(q_in, k_in, v_in, b_in, d_in, w_ref, out_ref,
                 q_ref, k_ref, v_ref, b_ref, d_ref, masks, qs, ks, vs, decays, growths, chunk_pairs, befores, qe, own, items, group, pairs, rows, enters, entering, att, arrived, weight,
                 total, group_maps, entry_maps, entry_adds, state,
                 in_load, w_load, w_send, w_recv, g_send, g_recv, p_send, p_recv, x_send, x_recv, e_send, e_recv,
                 y_send, y_recv):
    seq, head = lax.axis_index("seq"), lax.axis_index("head")
    member, pair, line = seq % 4, (seq // 4) % 4, seq // 16
    core = seq % 2
    base = seq - member
    mine = swapped(member)
    late = mine // 2
    right, left, across = (head + 1) % 4, (head + 3) % 4, (head + 2) % 4

    def in_pairs(step):
        return line * 16 + ((pair + step) % 4) * 4 + member

    barrier = pltpu.get_barrier_semaphore()
    friends = [{"seq": base + (member ^ j)} for j in (1, 2, 3)]
    friends += [{"seq": in_pairs(j)} for j in (1, 2, 3)]
    friends += [{"seq": (seq + 16 * j) % 64} for j in (1, 2, 3)]
    friends += [{"head": (head + j) % 4} for j in (1, 2, 3)]
    for friend in friends:
        pl.semaphore_signal(barrier, inc=1, device_id=friend, device_id_type=MESH)
    loads = [pltpu.make_async_copy(source, target, in_load.at[i]) for i, (source, target) in enumerate(
        ((b_in, b_ref), (d_in, d_ref), (k_in, k_ref), (v_in, v_ref), (q_in, q_ref)))]
    for copy in loads:
        copy.start()
    load = pltpu.make_async_copy(w_ref, weight.at[head], w_load)
    load.start()
    fill_masks(masks)
    for copy in loads[:4]:
        copy.wait()

    def copy_to(source, target, send_sem, recv_sem, to):
        return pltpu.make_async_remote_copy(source, target, send_sem, recv_sem, device_id=to, device_id_type=MESH)

    sibling = {"seq": seq ^ 1}
    to_right, to_left = {"head": right}, {"head": left}
    to_next, to_last = {"seq": (seq + 16) % 64}, {"seq": (seq + 48) % 64}
    block = 2 * core + line % 2
    block_x = 2 * core + 1 - line % 2
    top, low = pl.ds(0, 64), pl.ds(64, 64)

    def same(ref, i, to):
        return copy_to(ref, ref, w_send.at[i], w_recv.at[i], to)

    def go_right(of):
        return same(weight.at[of, block], 0, to_right)

    def go_left(of):
        return same(weight.at[of, block], 1, to_left)

    def relay_right(of):
        return same(weight.at[of, block, top], 2, to_right)

    def relay_left(of):
        return same(weight.at[of, block, low], 3, to_left)

    def go_next(of, i, at_block=block):
        return same(weight.at[of, at_block, top], 4 + i, to_next)

    def go_last(of, i, at_block=block):
        return same(weight.at[of, at_block, low], 7 + i, to_last)

    def over(of, i, at_block):
        return same(weight.at[of, at_block], 10 + i, sibling)

    def share(of, i):
        go_next(of, i).start()
        go_last(of, i).start()
        over(of, i, block).start()

    def share_x(of, i):
        go_next(of, i, block_x).wait_recv()
        go_last(of, i, block_x).wait_recv()
        over(of, 3 + i, block_x).start()

    load.wait()
    pl.semaphore_wait(barrier, len(friends))
    go_right(head).start()
    go_left(head).start()
    for source, target in ((k_ref, ks), (v_ref, vs)):
        target[...] = source[...].astype(F32).reshape(2048, C)

    def item_copy(h):
        return copy_to(items.at[h], group.at[member], g_send.at[h], g_recv.at[member], {"seq": base + swapped(h)})

    def pair_copy(j):
        return copy_to(pairs.at[0], pairs.at[4 - j], p_send.at[j], p_recv.at[j], {"seq": in_pairs(j)})

    def line_copy(j):
        return copy_to(rows.at[line], rows.at[line], x_send.at[j], x_recv.at[j], {"seq": (seq + 16 * j) % 64})

    def enter_copy(j):
        other = member ^ j
        return copy_to(enters.at[other], entering.at[mine], e_send.at[other], e_recv.at[mine],
                       {"seq": base + other})

    def out_copy(h, j):
        return copy_to(att.at[(head + j) % 4, h], arrived.at[j, h], y_send.at[j, h], y_recv.at[j, h],
                       {"head": (head + j) % 4})

    def at(ref, h):
        return lambda c: ref[pl.ds(c * 512 + h, C, stride=4), :].astype(BF16)

    def compute(two):
        def head_of(h):
            def four(ref):
                lines = lax.broadcasted_iota(jnp.int32, (4, 512), 0)
                mine = jnp.sum(jnp.where(lines == h, ref[...], 0.0), axis=0, keepdims=True)
                return jnp.concatenate([mine[:, c * C : (c + 1) * C] for c in range(4)], axis=0)

            def keep(c, decay, growth, pair_here, before):
                decays[h, c] = decay
                growths[h, c] = growth
                chunk_pairs[h, c] = pair_here
                if c:
                    befores[h, c - 1] = before

            return at(ks, h), at(vs, h), four(b_ref), four(d_ref), keep

        def middle(i):
            if i == 3:
                @pl.when((two == 1) & (late == 0))
                def _():
                    scan_group()

        heads = [2 * two, 2 * two + 1]
        for h, result in zip(heads, key_side([head_of(h) for h in heads], masks, middle)):
            items[h] = as_item(result)

            @pl.when(h != mine)
            def _():
                item_copy(h).start()

            @pl.when(h == mine)
            def _():
                group[member] = items[h]

        return 0

    def compute_rows(h):
        q_of, k_of = at(qs, h), at(ks, h)
        for c in range(4):
            rows_q, rows_o = query_side(q_of(c), k_of(c), decays[h, c], growths[h, c], chunk_pairs[h, c],
                                        befores[h, c - 1] if c else None)
            qe[h, c * C : (c + 1) * C, :] = rows_q.astype(BF16)
            own[h, c * C : (c + 1) * C, :] = rows_o

    def scan_group():
        for j in (1, 2, 3):
            other = member ^ j
            copy_to(group.at[other], group.at[other], g_send.at[other], g_recv.at[other],
                    {"seq": base + other}).wait_recv()
        early = join(group[1], from_item(group[0]))
        late = as_item(join(group[3], from_item(group[2])))
        pairs[0] = as_item(join(late, early))
        for j in (2, 1, 3):
            pair_copy(j).start()
        group_maps[0] = group[0]
        group_maps[1] = as_item(early)
        group_maps[2] = as_item(join(group[2], early))

    def scan_pairs():
        for j in (1, 3, 2):
            pair_copy(j).wait_recv()
        at_pair = [pairs[(j + 4 - pair) % 4] for j in range(4)]
        first = from_item(at_pair[0])
        early = join(at_pair[1], first)
        late = as_item(join(at_pair[3], from_item(at_pair[2])))
        rows[line] = as_item(join(late, early))
        for j in (2, 1, 3):
            @pl.when(line + j < 4)
            def _():
                line_copy(j).start()
        eye = jnp.where(
            lax.broadcasted_iota(jnp.int32, (C, 2 * C), 0) == lax.broadcasted_iota(jnp.int32, (C, 2 * C), 1), 1.0, 0.0)
        before = jnp.where(pair == 0, eye, first)
        before = jnp.where(pair > 1, early, before)
        before = jnp.where(pair > 2, join(at_pair[2], early), before)
        for i in range(4):
            here = join(group_maps[i - 1], before) if i else before
            hi, lo = halves(here[:, :C])
            entry_maps[i * C : (i + 1) * C, :C] = hi
            entry_maps[i * C : (i + 1) * C, C:] = lo
            entry_adds[i * C : (i + 1) * C, :] = here[:, C:]

    def scan_lines():
        state[...] = jnp.zeros((C, C), F32)
        for i in range(3):
            @pl.when(line > i)
            def _():
                copy_to(rows.at[i], rows.at[i], x_send.at[line - i], x_recv.at[line - i],
                        {"seq": (seq + 16) % 64}).wait_recv()
                if i == 0:
                    state[...] = rows[0, :, 2 * C :].astype(F32)
                else:
                    state[...] = pass_state(rows[i], state[...])

        row = wide(*halves(state[...]))
        both = dot(entry_maps[...], tall(row, row))
        all_four = (both[:, :C] + both[:, C:] + entry_adds[...]).astype(BF16)
        for i in range(4):
            enters[i] = all_four[i * C : (i + 1) * C]
        for j in (1, 2, 3):
            enter_copy(j).start()
        entering[mine] = enters[member]

    def apply(h):
        @pl.when(mine != h)
        def _():
            copy_to(entering.at[h], entering.at[h], e_send.at[h], e_recv.at[h],
                    {"seq": base + swapped(h)}).wait_recv()
        rows_here = dot(qe[h], entering[h]) + own[h]
        for t in range(4):
            att[t, h] = rows_here[t * C : (t + 1) * C].astype(BF16)
        for j in (2, 1, 3):
            out_copy(h, j).start()

    lax.fori_loop(0, 2, lambda two, _: compute(two), 0)
    go_right(left).wait_recv()
    relay_right(left).start()
    go_left(right).wait_recv()
    relay_left(right).start()
    share(left, 0)
    share(right, 1)
    loads[4].wait()
    qs[...] = q_ref[...].astype(F32).reshape(2048, C)

    def step_out(h, _):
        apply(h)
        return 0

    def step(t, _):
        compute_rows(t)

        @pl.when(t == 3)
        def _():
            lax.fori_loop(0, 2, step_out, 0)

        @pl.when((t == 0) & (late == 1))
        def _():
            scan_group()

        @pl.when(t == late + 1)
        def _():
            scan_pairs()

        @pl.when(t == late + 2)
        def _():
            scan_lines()

        @pl.when(t == 1)
        def _():
            relay_right(across).wait_recv()
            relay_left(across).wait_recv()
            share(across, 2)

        @pl.when(t == 2)
        def _():
            share_x(left, 0)
            share_x(right, 1)

        return 0

    lax.fori_loop(0, 4, step, 0)

    lax.fori_loop(2, 4, step_out, 0)

    share_x(across, 2)
    go_right(head).wait_send()
    go_left(head).wait_send()
    relay_right(left).wait_send()
    relay_left(right).wait_send()
    for j in (1, 2, 3):
        item_copy(swapped(member ^ j)).wait_send()
        pair_copy(j).wait_send()
        enter_copy(j).wait_send()

        @pl.when(line + j < 4)
        def _():
            line_copy(j).wait_send()

    for i, of in enumerate((left, right, across)):
        go_next(of, i).wait_send()
        go_last(of, i).wait_send()
        for k, at_block in ((0, block), (3, block_x)):
            over(of, i + k, at_block).wait_send()
            over(of, i + k, (at_block + 2) % 4).wait_recv()

    def product(heads, cols):
        rows_in = jnp.concatenate(
            [att[head, h] if j == 0 else arrived[j, h] for j in range(4) for h in heads], axis=1)
        rows_w = jnp.concatenate(
            [weight[(head + 4 - j) % 4, h, :, cols] for j in range(4) for h in heads], axis=0)
        return dot(rows_in, rows_w)

    for h in range(3):
        for j in (1, 3, 2):
            out_copy(h, j).wait()
    for n in range(4):
        total[:, n * 512 : (n + 1) * 512] = product((0, 1, 2), slice(n * 512, (n + 1) * 512))
    for j in (1, 3, 2):
        out_copy(3, j).wait()
    for n in range(4):
        cols = slice(n * 512, (n + 1) * 512)
        out_ref[:, cols] = (total[:, cols] + product((3,), cols)).astype(BF16)


def layer(q, k, v, b, d, w):
    vmem = pl.BlockSpec(memory_space=pltpu.VMEM)
    dma = pltpu.SemaphoreType.DMA
    return pl.pallas_call(
        layer_kernel,
        out_shape=jax.ShapeDtypeStruct((128, 2048), BF16),
        in_specs=[pl.BlockSpec(memory_space=pltpu.HBM)] * 6,
        out_specs=vmem,
        scratch_shapes=[pltpu.VMEM((512, 4, C), BF16)] * 3 + [pltpu.VMEM((4, 512), F32)] * 2 + [
            pltpu.VMEM((7, C, C), BF16),
            pltpu.VMEM((2048, C), F32),
            pltpu.VMEM((2048, C), F32),
            pltpu.VMEM((2048, C), F32),
            pltpu.VMEM((4, 4, C, C), F32),
            pltpu.VMEM((4, 4, C, 1), F32),
            pltpu.VMEM((4, 4, C, 2 * C), F32),
            pltpu.VMEM((4, 3, C, 2 * C), F32),
            pltpu.VMEM((4, 512, C), BF16),
            pltpu.VMEM((4, 512, C), F32),
            pltpu.VMEM((4, C, 3 * C), BF16),
            pltpu.VMEM((4, C, 3 * C), BF16),
            pltpu.VMEM((4, C, 3 * C), BF16),
            pltpu.VMEM((4, C, 3 * C), BF16),
            pltpu.VMEM((4, C, C), BF16),
            pltpu.VMEM((4, C, C), BF16),
            pltpu.VMEM((4, 4, C, C), BF16),
            pltpu.VMEM((4, 4, C, C), BF16),
            pltpu.VMEM((4, 4, C, 2048), BF16),
            pltpu.VMEM((C, 2048), F32),
            pltpu.VMEM((3, C, 3 * C), BF16),
            pltpu.VMEM((4 * C, 2 * C), BF16),
            pltpu.VMEM((4 * C, C), F32),
            pltpu.VMEM((C, C), F32),
            dma((5,)), dma, dma((16,)), dma((16,)),
        ] + [dma((4,))] * 8 + [dma((4, 4))] * 2,
        compiler_params=pltpu.CompilerParams(
            collective_id=0, has_side_effects=True, vmem_limit_bytes=40 * 2**20),
    )(q, k, v, b, d, w)


def body(query, key, value, beta, log_decay, out_weight):
    stay = lambda a: pltpu.with_memory_space_constraint(a, pltpu.HBM)
    return layer(stay(query), stay(key), stay(value), stay(beta), stay(log_decay), stay(out_weight.reshape(4, C, 2048)))


def solution(mesh):
    in_specs = (
        P("seq", "head", None),
        P("seq", "head", None),
        P("seq", "head", None),
        P("head", "seq"),
        P("head", "seq"),
        P("head", None),
    )
    out_specs = P(("seq", "head"), None)
    return jax.shard_map(body, mesh=mesh, in_specs=in_specs, out_specs=out_specs, check_vma=False)
```

```python
import jax
import jax.numpy as jnp
from jax import lax
from jax.experimental import pallas as pl
from jax.experimental.pallas import tpu as pltpu
from jax.sharding import PartitionSpec as P

C = 128
LEVELS = (2, 4, 8, 16, 32, 64)
F32, BF16 = jnp.float32, jnp.bfloat16


def dot(a, b):
    return jnp.dot(a, b, preferred_element_type=F32)


def dot_nt(a, b, precision=None):
    return lax.dot_general(a, b, (((1,), (1,)), ((), ())), precision=precision, preferred_element_type=F32)


def halves(a):
    hi = a.astype(BF16)
    return hi, (a - hi.astype(F32)).astype(BF16)


def wide(a, b):
    return jnp.concatenate([a, b], axis=1)


def tall(a, b):
    return jnp.concatenate([a, b], axis=0)


def exact_square(a_halves, b_halves):
    row = wide(*b_halves)
    both = dot(wide(*a_halves), tall(row, row))
    return both[:, :C] + both[:, C:]


def exact_apply(a_halves, b_hi, b_lo):
    return dot(wide(*a_halves), tall(b_hi, b_hi)) + dot(a_halves[0], b_lo)


def fill_masks(masks):
    row = lax.broadcasted_iota(jnp.int32, (C, C), 0)
    col = lax.broadcasted_iota(jnp.int32, (C, C), 1)
    apart = jnp.where(row > col, row ^ col, 0)
    for i, s in enumerate((1,) + LEVELS):
        masks[i] = jnp.where((apart >= s) & (apart < 2 * s), 1.0, 0.0).astype(BF16)


def chunk_start(k, b_col, g_row, g_col):
    row = lax.broadcasted_iota(jnp.int32, (C, C), 0)
    col = lax.broadcasted_iota(jnp.int32, (C, C), 1)
    gram = dot_nt(k, k)
    diagonal = jnp.where(row == col, gram, 0.0)
    rk_row = lax.rsqrt(jnp.sum(diagonal, axis=0, keepdims=True) + 1e-06)
    rk_col = lax.rsqrt(jnp.sum(diagonal, axis=1, keepdims=True) + 1e-06)
    decay = jnp.exp(jnp.where(row >= col, g_col - g_row, -1e30)) * rk_row
    lower = jnp.where(row > col, decay * gram, 0.0) * (b_col * rk_col)
    return lower, decay, rk_row, rk_col


def invert(lowers, masks, middle):
    row = lax.broadcasted_iota(jnp.int32, (C, C), 0)
    col = lax.broadcasted_iota(jnp.int32, (C, C), 1)
    split = [halves(a) for a in lowers]
    first = masks[0].astype(F32)
    xs = [jnp.where(row == col, 1.0, 0.0) - a * first for a in lowers]
    for i in range(len(LEVELS)):
        mask = masks[i + 1]
        xh = [halves(x) for x in xs]
        ys = [exact_square((hi * mask, lo * mask), x) for (hi, lo), x in zip(split, xh)]
        yh = [halves(y) for y in ys]
        zs = [exact_square(x, y) for x, y in zip(xh, yh)]
        xs = [x - z for x, z in zip(xs, zs)]
        middle(i)
    return xs


def chunk_end(x, k, v, b_row, g_row, g_col, rk_row, rk_col):
    row = lax.broadcasted_iota(jnp.int32, (C, C), 0)
    col = lax.broadcasted_iota(jnp.int32, (C, C), 1)
    carried = dot(wide(*halves(x * b_row)), tall(v, v))
    key_factor = dot(wide(*halves(x * (b_row * jnp.exp(g_row) * rk_row))), tall(k, k))
    pair = wide(-key_factor, carried)
    g_end = g_col[C - 1 :, :]
    pair_hi, pair_lo = halves(pair * (jnp.exp(g_end - g_col) * rk_col))
    kt = k.T
    ab = dot(wide(kt, kt), tall(pair_hi, pair_lo))
    step = ab[:, :C] + jnp.where(row == col, jnp.exp(g_end), 0.0)
    return pair, wide(step, ab[:, C:])


def compose(later, earlier):
    return exact_apply(halves(later[:, :C]), *halves(earlier)) + wide(jnp.zeros((C, C), F32), later[:, C:])


def running_sums(beta, decay_log):
    row = lax.broadcasted_iota(jnp.int32, (C, C), 0)
    col = lax.broadcasted_iota(jnp.int32, (C, C), 1)
    sums = jnp.where(row <= col, 1.0, 0.0)
    logs = jnp.maximum(decay_log, -110.0)
    g = jnp.dot(tall(logs, logs), sums, precision=lax.Precision.HIGHEST, preferred_element_type=F32)
    turned = tall(beta, g[:4]).T
    return [(beta[c : c + 1], turned[:, c : c + 1], g[c : c + 1], turned[:, 4 + c : 5 + c]) for c in range(4)]


def key_side(heads, masks, middle):
    rates = [running_sums(beta, logs) for _, _, beta, logs, _ in heads]
    starts = [[chunk_start(head[0](c), *rate[c][1:]) for c in range(4)] for head, rate in zip(heads, rates)]
    xs = invert([start[0] for four in starts for start in four], masks, middle)
    results = []
    for i, (k_of, v_of, _, _, keep) in enumerate(heads):
        ends = [chunk_end(xs[4 * i + c], k_of(c), v_of(c), rates[i][c][0], *rates[i][c][2:], *starts[i][c][2:])
                for c in range(4)]
        maps = [e[1] for e in ends]
        two = compose(maps[1], maps[0])
        other = compose(maps[3], maps[2])
        three = compose(maps[2], two)
        for c, before in enumerate((None, maps[0], two, three)):
            keep(c, starts[i][c][1], jnp.exp(rates[i][c][3]), ends[c][0], before)
        results.append(compose(other, two))
    return results


def query_side(q, k, decay, growth, pair, before):
    qf = q.astype(F32)
    rq_col = lax.rsqrt(jnp.sum(qf * qf, axis=1, keepdims=True) + 1e-06)
    qo = exact_apply(halves(decay * dot_nt(q, k)), *halves(pair))
    rows_q = (qo[:, :C] + growth * qf) * rq_col
    rows_o = qo[:, C:] * rq_col
    if before is None:
        return rows_q, rows_o
    moved = exact_apply(halves(rows_q), *halves(before))
    return moved[:, :C], rows_o + moved[:, C:]


MESH = pl.DeviceIdType.MESH


def as_item(state):
    hi, lo = halves(state[:, :C])
    return jnp.concatenate([hi, lo, state[:, C:].astype(BF16)], axis=1)


def from_item(item):
    return wide(item[:, :C].astype(F32) + item[:, C : 2 * C].astype(F32), item[:, 2 * C :].astype(F32))


def join(later, earlier):
    hi, lo = halves(earlier)
    return exact_apply((later[:, :C], later[:, C : 2 * C]), hi, lo) + wide(
        jnp.zeros((C, C), F32), later[:, 2 * C :].astype(F32))


def pass_state(item, state):
    return exact_square((item[:, :C], item[:, C : 2 * C]), halves(state)) + item[:, 2 * C :].astype(F32)


def swapped(i):
    return (i % 2) * 2 + i // 2


def layer_kernel(q_in, k_in, v_in, b_in, d_in, w_ref, out_ref,
                 q_ref, k_ref, v_ref, b_ref, d_ref, masks, qs, ks, vs, decays, growths, chunk_pairs, befores, qe, own, items, group, pairs, rows, enters, entering, att, arrived, weight,
                 total, group_maps, entry_maps, entry_adds, state,
                 in_load, w_load, w_send, w_recv, g_send, g_recv, p_send, p_recv, x_send, x_recv, e_send, e_recv,
                 y_send, y_recv):
    seq, head = lax.axis_index("seq"), lax.axis_index("head")
    member, pair, line = seq % 4, (seq // 4) % 4, seq // 16
    core = seq % 2
    base = seq - member
    mine = swapped(member)
    late = mine // 2
    right, left, across = (head + 1) % 4, (head + 3) % 4, (head + 2) % 4

    def in_pairs(step):
        return line * 16 + ((pair + step) % 4) * 4 + member

    barrier = pltpu.get_barrier_semaphore()
    friends = [{"seq": base + (member ^ j)} for j in (1, 2, 3)]
    friends += [{"seq": in_pairs(j)} for j in (1, 2, 3)]
    friends += [{"seq": (seq + 16 * j) % 64} for j in (1, 2, 3)]
    friends += [{"head": (head + j) % 4} for j in (1, 2, 3)]
    for friend in friends:
        pl.semaphore_signal(barrier, inc=1, device_id=friend, device_id_type=MESH)
    loads = [pltpu.make_async_copy(source, target, in_load.at[i]) for i, (source, target) in enumerate(
        ((b_in, b_ref), (d_in, d_ref), (k_in, k_ref), (v_in, v_ref), (q_in, q_ref)))]
    for copy in loads:
        copy.start()
    load = pltpu.make_async_copy(w_ref, weight.at[head], w_load)
    load.start()
    fill_masks(masks)
    for copy in loads[:4]:
        copy.wait()
    for source, target in ((k_ref, ks), (v_ref, vs)):
        target[...] = source[...].astype(F32).reshape(2048, C)

    def copy_to(source, target, send_sem, recv_sem, to):
        return pltpu.make_async_remote_copy(source, target, send_sem, recv_sem, device_id=to, device_id_type=MESH)

    sibling = {"seq": seq ^ 1}
    to_right, to_left = {"head": right}, {"head": left}
    to_next, to_last = {"seq": (seq + 16) % 64}, {"seq": (seq + 48) % 64}
    block = 2 * core + line % 2
    block_x = 2 * core + 1 - line % 2
    top, low = pl.ds(0, 64), pl.ds(64, 64)

    def same(ref, i, to):
        return copy_to(ref, ref, w_send.at[i], w_recv.at[i], to)

    def go_right(of):
        return same(weight.at[of, block], 0, to_right)

    def go_left(of):
        return same(weight.at[of, block], 1, to_left)

    def relay_right(of):
        return same(weight.at[of, block, top], 2, to_right)

    def relay_left(of):
        return same(weight.at[of, block, low], 3, to_left)

    def go_next(of, i, at_block=block):
        return same(weight.at[of, at_block, top], 4 + i, to_next)

    def go_last(of, i, at_block=block):
        return same(weight.at[of, at_block, low], 7 + i, to_last)

    def over(of, i, at_block):
        return same(weight.at[of, at_block], 10 + i, sibling)

    def share(of, i):
        go_next(of, i).start()
        go_last(of, i).start()
        over(of, i, block).start()

    def share_x(of, i):
        go_next(of, i, block_x).wait_recv()
        go_last(of, i, block_x).wait_recv()
        over(of, 3 + i, block_x).start()

    def greet():
        load.wait()
        pl.semaphore_wait(barrier, len(friends))
        go_right(head).start()
        go_left(head).start()

    def item_copy(h):
        return copy_to(items.at[h], group.at[member], g_send.at[h], g_recv.at[member], {"seq": base + swapped(h)})

    def pair_copy(j):
        return copy_to(pairs.at[0], pairs.at[4 - j], p_send.at[j], p_recv.at[j], {"seq": in_pairs(j)})

    def line_copy(j):
        return copy_to(rows.at[line], rows.at[line], x_send.at[j], x_recv.at[j], {"seq": (seq + 16 * j) % 64})

    def enter_copy(j):
        other = member ^ j
        return copy_to(enters.at[other], entering.at[mine], e_send.at[other], e_recv.at[mine],
                       {"seq": base + other})

    def out_copy(h, j):
        return copy_to(att.at[(head + j) % 4, h], arrived.at[j, h], y_send.at[j, h], y_recv.at[j, h],
                       {"head": (head + j) % 4})

    def at(ref, h):
        return lambda c: ref[pl.ds(c * 512 + h, C, stride=4), :].astype(BF16)

    def compute(two):
        def head_of(h):
            def four(ref):
                lines = lax.broadcasted_iota(jnp.int32, (4, 512), 0)
                mine = jnp.sum(jnp.where(lines == h, ref[...], 0.0), axis=0, keepdims=True)
                return jnp.concatenate([mine[:, c * C : (c + 1) * C] for c in range(4)], axis=0)

            def keep(c, decay, growth, pair_here, before):
                decays[h, c] = decay
                growths[h, c] = growth
                chunk_pairs[h, c] = pair_here
                if c:
                    befores[h, c - 1] = before

            return at(ks, h), at(vs, h), four(b_ref), four(d_ref), keep

        def middle(i):
            if i == 0:
                @pl.when(two == 0)
                def _():
                    greet()

            if i == 3:
                @pl.when((two == 1) & (late == 0))
                def _():
                    scan_group()

        heads = [2 * two, 2 * two + 1]
        for h, result in zip(heads, key_side([head_of(h) for h in heads], masks, middle)):
            items[h] = as_item(result)

            @pl.when(h != mine)
            def _():
                item_copy(h).start()

            @pl.when(h == mine)
            def _():
                group[member] = items[h]

        return 0

    def compute_rows(h):
        q_of, k_of = at(qs, h), at(ks, h)
        for c in range(4):
            rows_q, rows_o = query_side(q_of(c), k_of(c), decays[h, c], growths[h, c], chunk_pairs[h, c],
                                        befores[h, c - 1] if c else None)
            qe[h, c * C : (c + 1) * C, :] = rows_q.astype(BF16)
            own[h, c * C : (c + 1) * C, :] = rows_o

    def scan_group():
        for j in (1, 2, 3):
            other = member ^ j
            copy_to(group.at[other], group.at[other], g_send.at[other], g_recv.at[other],
                    {"seq": base + other}).wait_recv()
        early = join(group[1], from_item(group[0]))
        late = as_item(join(group[3], from_item(group[2])))
        pairs[0] = as_item(join(late, early))
        for j in (2, 1, 3):
            pair_copy(j).start()
        group_maps[0] = group[0]
        group_maps[1] = as_item(early)
        group_maps[2] = as_item(join(group[2], early))

    def scan_pairs():
        for j in (1, 3, 2):
            pair_copy(j).wait_recv()
        at_pair = [pairs[(j + 4 - pair) % 4] for j in range(4)]
        first = from_item(at_pair[0])
        early = join(at_pair[1], first)
        late = as_item(join(at_pair[3], from_item(at_pair[2])))
        rows[line] = as_item(join(late, early))
        for j in (2, 1, 3):
            @pl.when(line + j < 4)
            def _():
                line_copy(j).start()
        eye = jnp.where(
            lax.broadcasted_iota(jnp.int32, (C, 2 * C), 0) == lax.broadcasted_iota(jnp.int32, (C, 2 * C), 1), 1.0, 0.0)
        before = jnp.where(pair == 0, eye, first)
        before = jnp.where(pair > 1, early, before)
        before = jnp.where(pair > 2, join(at_pair[2], early), before)
        for i in range(4):
            here = join(group_maps[i - 1], before) if i else before
            hi, lo = halves(here[:, :C])
            entry_maps[i * C : (i + 1) * C, :C] = hi
            entry_maps[i * C : (i + 1) * C, C:] = lo
            entry_adds[i * C : (i + 1) * C, :] = here[:, C:]

    def scan_lines():
        state[...] = jnp.zeros((C, C), F32)
        for i in range(3):
            @pl.when(line > i)
            def _():
                copy_to(rows.at[i], rows.at[i], x_send.at[line - i], x_recv.at[line - i],
                        {"seq": (seq + 16) % 64}).wait_recv()
                if i == 0:
                    state[...] = rows[0, :, 2 * C :].astype(F32)
                else:
                    state[...] = pass_state(rows[i], state[...])

        row = wide(*halves(state[...]))
        both = dot(entry_maps[...], tall(row, row))
        all_four = (both[:, :C] + both[:, C:] + entry_adds[...]).astype(BF16)
        for i in range(4):
            enters[i] = all_four[i * C : (i + 1) * C]
        for j in (1, 2, 3):
            enter_copy(j).start()
        entering[mine] = enters[member]

    def apply(h):
        @pl.when(mine != h)
        def _():
            copy_to(entering.at[h], entering.at[h], e_send.at[h], e_recv.at[h],
                    {"seq": base + swapped(h)}).wait_recv()
        rows_here = dot(qe[h], entering[h]) + own[h]
        for t in range(4):
            att[t, h] = rows_here[t * C : (t + 1) * C].astype(BF16)
        for j in (2, 1, 3):
            out_copy(h, j).start()

    lax.fori_loop(0, 2, lambda two, _: compute(two), 0)
    go_right(left).wait_recv()
    relay_right(left).start()
    go_left(right).wait_recv()
    relay_left(right).start()
    share(left, 0)
    share(right, 1)
    loads[4].wait()
    qs[...] = q_ref[...].astype(F32).reshape(2048, C)

    def step_out(h, _):
        apply(h)
        return 0

    def step(t, _):
        compute_rows(t)

        @pl.when(t == 3)
        def _():
            lax.fori_loop(0, 2, step_out, 0)

        @pl.when((t == 0) & (late == 1))
        def _():
            scan_group()

        @pl.when(t == late + 1)
        def _():
            scan_pairs()

        @pl.when(t == late + 2)
        def _():
            scan_lines()

        @pl.when(t == 1)
        def _():
            relay_right(across).wait_recv()
            relay_left(across).wait_recv()
            share(across, 2)

        @pl.when(t == 2)
        def _():
            share_x(left, 0)
            share_x(right, 1)

        @pl.when(t == 3)
        def _():
            share_x(across, 2)

        return 0

    lax.fori_loop(0, 4, step, 0)

    lax.fori_loop(2, 4, step_out, 0)

    go_right(head).wait_send()
    go_left(head).wait_send()
    relay_right(left).wait_send()
    relay_left(right).wait_send()
    for j in (1, 2, 3):
        item_copy(swapped(member ^ j)).wait_send()
        pair_copy(j).wait_send()
        enter_copy(j).wait_send()

        @pl.when(line + j < 4)
        def _():
            line_copy(j).wait_send()

    for i, of in enumerate((left, right, across)):
        go_next(of, i).wait_send()
        go_last(of, i).wait_send()
        for k, at_block in ((0, block), (3, block_x)):
            over(of, i + k, at_block).wait_send()
            over(of, i + k, (at_block + 2) % 4).wait_recv()

    def product(heads, cols):
        rows_in = jnp.concatenate(
            [att[head, h] if j == 0 else arrived[j, h] for j in range(4) for h in heads], axis=1)
        rows_w = jnp.concatenate(
            [weight[(head + 4 - j) % 4, h, :, cols] for j in range(4) for h in heads], axis=0)
        return dot(rows_in, rows_w)

    for h in range(3):
        for j in (1, 3, 2):
            out_copy(h, j).wait()
    for n in range(4):
        total[:, n * 512 : (n + 1) * 512] = product((0, 1, 2), slice(n * 512, (n + 1) * 512))
    for j in (1, 3, 2):
        out_copy(3, j).wait()
    for n in range(4):
        cols = slice(n * 512, (n + 1) * 512)
        out_ref[:, cols] = (total[:, cols] + product((3,), cols)).astype(BF16)


def layer(q, k, v, b, d, w):
    vmem = pl.BlockSpec(memory_space=pltpu.VMEM)
    dma = pltpu.SemaphoreType.DMA
    return pl.pallas_call(
        layer_kernel,
        out_shape=jax.ShapeDtypeStruct((128, 2048), BF16),
        in_specs=[pl.BlockSpec(memory_space=pltpu.HBM)] * 6,
        out_specs=vmem,
        scratch_shapes=[pltpu.VMEM((512, 4, C), BF16)] * 3 + [pltpu.VMEM((4, 512), F32)] * 2 + [
            pltpu.VMEM((7, C, C), BF16),
            pltpu.VMEM((2048, C), F32),
            pltpu.VMEM((2048, C), F32),
            pltpu.VMEM((2048, C), F32),
            pltpu.VMEM((4, 4, C, C), F32),
            pltpu.VMEM((4, 4, C, 1), F32),
            pltpu.VMEM((4, 4, C, 2 * C), F32),
            pltpu.VMEM((4, 3, C, 2 * C), F32),
            pltpu.VMEM((4, 512, C), BF16),
            pltpu.VMEM((4, 512, C), F32),
            pltpu.VMEM((4, C, 3 * C), BF16),
            pltpu.VMEM((4, C, 3 * C), BF16),
            pltpu.VMEM((4, C, 3 * C), BF16),
            pltpu.VMEM((4, C, 3 * C), BF16),
            pltpu.VMEM((4, C, C), BF16),
            pltpu.VMEM((4, C, C), BF16),
            pltpu.VMEM((4, 4, C, C), BF16),
            pltpu.VMEM((4, 4, C, C), BF16),
            pltpu.VMEM((4, 4, C, 2048), BF16),
            pltpu.VMEM((C, 2048), F32),
            pltpu.VMEM((3, C, 3 * C), BF16),
            pltpu.VMEM((4 * C, 2 * C), BF16),
            pltpu.VMEM((4 * C, C), F32),
            pltpu.VMEM((C, C), F32),
            dma((5,)), dma, dma((16,)), dma((16,)),
        ] + [dma((4,))] * 8 + [dma((4, 4))] * 2,
        compiler_params=pltpu.CompilerParams(
            collective_id=0, has_side_effects=True, vmem_limit_bytes=40 * 2**20),
    )(q, k, v, b, d, w)


def body(query, key, value, beta, log_decay, out_weight):
    stay = lambda a: pltpu.with_memory_space_constraint(a, pltpu.HBM)
    return layer(stay(query), stay(key), stay(value), stay(beta), stay(log_decay), stay(out_weight.reshape(4, C, 2048)))


def solution(mesh):
    in_specs = (
        P("seq", "head", None),
        P("seq", "head", None),
        P("seq", "head", None),
        P("head", "seq"),
        P("head", "seq"),
        P("head", None),
    )
    out_specs = P(("seq", "head"), None)
    return jax.shard_map(body, mesh=mesh, in_specs=in_specs, out_specs=out_specs, check_vma=False)
```

```python
import jax
import jax.numpy as jnp
from jax import lax
from jax.experimental import pallas as pl
from jax.experimental.pallas import tpu as pltpu
from jax.sharding import PartitionSpec as P

C = 128
LEVELS = (2, 4, 8, 16, 32, 64)
F32, BF16 = jnp.float32, jnp.bfloat16


def dot(a, b):
    return jnp.dot(a, b, preferred_element_type=F32)


def dot_nt(a, b, precision=None):
    return lax.dot_general(a, b, (((1,), (1,)), ((), ())), precision=precision, preferred_element_type=F32)


def halves(a):
    hi = a.astype(BF16)
    return hi, (a - hi.astype(F32)).astype(BF16)


def wide(a, b):
    return jnp.concatenate([a, b], axis=1)


def tall(a, b):
    return jnp.concatenate([a, b], axis=0)


def exact_square(a_halves, b_halves):
    row = wide(*b_halves)
    both = dot(wide(*a_halves), tall(row, row))
    return both[:, :C] + both[:, C:]


def exact_apply(a_halves, b_hi, b_lo):
    return dot(wide(*a_halves), tall(b_hi, b_hi)) + dot(a_halves[0], b_lo)


def fill_masks(masks):
    row = lax.broadcasted_iota(jnp.int32, (C, C), 0)
    col = lax.broadcasted_iota(jnp.int32, (C, C), 1)
    apart = jnp.where(row > col, row ^ col, 0)
    for i, s in enumerate((1,) + LEVELS):
        masks[i] = jnp.where((apart >= s) & (apart < 2 * s), 1.0, 0.0).astype(BF16)


def chunk_start(k, b_col, g_row, g_col):
    row = lax.broadcasted_iota(jnp.int32, (C, C), 0)
    col = lax.broadcasted_iota(jnp.int32, (C, C), 1)
    gram = dot_nt(k, k)
    diagonal = jnp.where(row == col, gram, 0.0)
    rk_row = lax.rsqrt(jnp.sum(diagonal, axis=0, keepdims=True) + 1e-06)
    rk_col = lax.rsqrt(jnp.sum(diagonal, axis=1, keepdims=True) + 1e-06)
    decay = jnp.exp(jnp.where(row >= col, g_col - g_row, -1e30)) * rk_row
    lower = jnp.where(row > col, decay * gram, 0.0) * (b_col * rk_col)
    return lower, decay, rk_row, rk_col


def invert(lowers, masks, middle):
    row = lax.broadcasted_iota(jnp.int32, (C, C), 0)
    col = lax.broadcasted_iota(jnp.int32, (C, C), 1)
    split = [halves(a) for a in lowers]
    first = masks[0].astype(F32)
    xs = [jnp.where(row == col, 1.0, 0.0) - a * first for a in lowers]
    for i in range(len(LEVELS)):
        mask = masks[i + 1]
        xh = [halves(x) for x in xs]
        ys = [exact_square((hi * mask, lo * mask), x) for (hi, lo), x in zip(split, xh)]
        yh = [halves(y) for y in ys]
        zs = [exact_square(x, y) for x, y in zip(xh, yh)]
        xs = [x - z for x, z in zip(xs, zs)]
        middle(i)
    return xs


def chunk_end(x, k, v, b_row, g_row, g_col, rk_row, rk_col):
    row = lax.broadcasted_iota(jnp.int32, (C, C), 0)
    col = lax.broadcasted_iota(jnp.int32, (C, C), 1)
    carried = dot(wide(*halves(x * b_row)), tall(v, v))
    key_factor = dot(wide(*halves(x * (b_row * jnp.exp(g_row) * rk_row))), tall(k, k))
    pair = wide(-key_factor, carried)
    g_end = g_col[C - 1 :, :]
    pair_hi, pair_lo = halves(pair * (jnp.exp(g_end - g_col) * rk_col))
    kt = k.T
    ab = dot(wide(kt, kt), tall(pair_hi, pair_lo))
    step = ab[:, :C] + jnp.where(row == col, jnp.exp(g_end), 0.0)
    return pair, wide(step, ab[:, C:])


def compose(later, earlier):
    return exact_apply(halves(later[:, :C]), *halves(earlier)) + wide(jnp.zeros((C, C), F32), later[:, C:])


def running_sums(beta, decay_log):
    row = lax.broadcasted_iota(jnp.int32, (C, C), 0)
    col = lax.broadcasted_iota(jnp.int32, (C, C), 1)
    sums = jnp.where(row <= col, 1.0, 0.0)
    logs = jnp.maximum(decay_log, -110.0)
    g = jnp.dot(tall(logs, logs), sums, precision=lax.Precision.HIGHEST, preferred_element_type=F32)
    turned = tall(beta, g[:4]).T
    return [(beta[c : c + 1], turned[:, c : c + 1], g[c : c + 1], turned[:, 4 + c : 5 + c]) for c in range(4)]


def key_side(heads, masks, middle):
    rates = [running_sums(beta, logs) for _, _, beta, logs, _ in heads]
    starts = [[chunk_start(head[0](c), *rate[c][1:]) for c in range(4)] for head, rate in zip(heads, rates)]
    xs = invert([start[0] for four in starts for start in four], masks, middle)
    results = []
    for i, (k_of, v_of, _, _, keep) in enumerate(heads):
        ends = [chunk_end(xs[4 * i + c], k_of(c), v_of(c), rates[i][c][0], *rates[i][c][2:], *starts[i][c][2:])
                for c in range(4)]
        maps = [e[1] for e in ends]
        two = compose(maps[1], maps[0])
        other = compose(maps[3], maps[2])
        three = compose(maps[2], two)
        for c, before in enumerate((None, maps[0], two, three)):
            keep(c, starts[i][c][1], jnp.exp(rates[i][c][3]), ends[c][0], before)
        results.append(compose(other, two))
    return results


def query_side(q, k, decay, growth, pair, before):
    qf = q.astype(F32)
    rq_col = lax.rsqrt(jnp.sum(qf * qf, axis=1, keepdims=True) + 1e-06)
    qo = exact_apply(halves(decay * dot_nt(q, k)), *halves(pair))
    rows_q = (qo[:, :C] + growth * qf) * rq_col
    rows_o = qo[:, C:] * rq_col
    if before is None:
        return rows_q, rows_o
    moved = exact_apply(halves(rows_q), *halves(before))
    return moved[:, :C], rows_o + moved[:, C:]


MESH = pl.DeviceIdType.MESH


def as_item(state):
    hi, lo = halves(state[:, :C])
    return jnp.concatenate([hi, lo, state[:, C:].astype(BF16)], axis=1)


def from_item(item):
    return wide(item[:, :C].astype(F32) + item[:, C : 2 * C].astype(F32), item[:, 2 * C :].astype(F32))


def join(later, earlier):
    hi, lo = halves(earlier)
    return exact_apply((later[:, :C], later[:, C : 2 * C]), hi, lo) + wide(
        jnp.zeros((C, C), F32), later[:, 2 * C :].astype(F32))


def pass_state(item, state):
    return exact_square((item[:, :C], item[:, C : 2 * C]), halves(state)) + item[:, 2 * C :].astype(F32)


def swapped(i):
    return (i % 2) * 2 + i // 2


def layer_kernel(q_in, k_in, v_in, b_in, d_in, w_ref, out_ref,
                 q_ref, k_ref, v_ref, b_ref, d_ref, masks, qs, ks, vs, decays, growths, chunk_pairs, befores, qe, own, items, group, pairs, rows, enters, entering, att, arrived, weight,
                 total, group_maps, entry_maps, entry_adds, state,
                 in_load, w_load, w_send, w_recv, g_send, g_recv, p_send, p_recv, x_send, x_recv, e_send, e_recv,
                 y_send, y_recv):
    seq, head = lax.axis_index("seq"), lax.axis_index("head")
    member, pair, line = seq % 4, (seq // 4) % 4, seq // 16
    core = seq % 2
    base = seq - member
    mine = swapped(member)
    late = mine // 2
    right, left, across = (head + 1) % 4, (head + 3) % 4, (head + 2) % 4

    def in_pairs(step):
        return line * 16 + ((pair + step) % 4) * 4 + member

    barrier = pltpu.get_barrier_semaphore()
    friends = [{"seq": base + (member ^ j)} for j in (1, 2, 3)]
    friends += [{"seq": in_pairs(j)} for j in (1, 2, 3)]
    friends += [{"seq": (seq + 16 * j) % 64} for j in (1, 2, 3)]
    friends += [{"head": (head + j) % 4} for j in (1, 2, 3)]
    for friend in friends:
        pl.semaphore_signal(barrier, inc=1, device_id=friend, device_id_type=MESH)
    loads = [pltpu.make_async_copy(source, target, in_load.at[i]) for i, (source, target) in enumerate(
        ((b_in, b_ref), (d_in, d_ref), (k_in, k_ref), (v_in, v_ref), (q_in, q_ref)))]
    for copy in loads:
        copy.start()
    load = pltpu.make_async_copy(w_ref, weight.at[head], w_load)
    load.start()
    fill_masks(masks)
    for copy in loads[:4]:
        copy.wait()
    for source, target in ((k_ref, ks), (v_ref, vs)):
        target[...] = source[...].astype(F32).reshape(2048, C)

    def copy_to(source, target, send_sem, recv_sem, to):
        return pltpu.make_async_remote_copy(source, target, send_sem, recv_sem, device_id=to, device_id_type=MESH)

    sibling = {"seq": seq ^ 1}
    to_right, to_left = {"head": right}, {"head": left}
    to_next, to_last = {"seq": (seq + 16) % 64}, {"seq": (seq + 48) % 64}
    block = 2 * core + line % 2
    block_x = 2 * core + 1 - line % 2
    top, low = pl.ds(0, 64), pl.ds(64, 64)

    def same(ref, i, to):
        return copy_to(ref, ref, w_send.at[i], w_recv.at[i], to)

    def go_right(of):
        return same(weight.at[of, block], 0, to_right)

    def go_left(of):
        return same(weight.at[of, block], 1, to_left)

    def relay_right(of):
        return same(weight.at[of, block, top], 2, to_right)

    def relay_left(of):
        return same(weight.at[of, block, low], 3, to_left)

    def go_next(of, i, at_block=block):
        return same(weight.at[of, at_block, top], 4 + i, to_next)

    def go_last(of, i, at_block=block):
        return same(weight.at[of, at_block, low], 7 + i, to_last)

    def over(of, i, at_block):
        return same(weight.at[of, at_block], 10 + i, sibling)

    def share(of, i):
        go_next(of, i).start()
        go_last(of, i).start()
        over(of, i, block).start()

    def share_x(of, i):
        go_next(of, i, block_x).wait_recv()
        go_last(of, i, block_x).wait_recv()
        over(of, 3 + i, block_x).start()

    def greet():
        load.wait()
        pl.semaphore_wait(barrier, len(friends))
        go_right(head).start()
        go_left(head).start()

    def item_copy(h):
        return copy_to(items.at[h], group.at[member], g_send.at[h], g_recv.at[member], {"seq": base + swapped(h)})

    def pair_copy(j):
        return copy_to(pairs.at[0], pairs.at[4 - j], p_send.at[j], p_recv.at[j], {"seq": in_pairs(j)})

    def line_copy(j):
        return copy_to(rows.at[line], rows.at[line], x_send.at[j], x_recv.at[j], {"seq": (seq + 16 * j) % 64})

    def enter_copy(j):
        other = member ^ j
        return copy_to(enters.at[other], entering.at[mine], e_send.at[other], e_recv.at[mine],
                       {"seq": base + other})

    def out_copy(h, j):
        return copy_to(att.at[(head + j) % 4, h], arrived.at[j, h], y_send.at[j, h], y_recv.at[j, h],
                       {"head": (head + j) % 4})

    def at(ref, h):
        return lambda c: ref[pl.ds(c * 512 + h, C, stride=4), :].astype(BF16)

    def compute(two):
        def head_of(h):
            def four(ref):
                lines = lax.broadcasted_iota(jnp.int32, (4, 512), 0)
                mine = jnp.sum(jnp.where(lines == h, ref[...], 0.0), axis=0, keepdims=True)
                return jnp.concatenate([mine[:, c * C : (c + 1) * C] for c in range(4)], axis=0)

            def keep(c, decay, growth, pair_here, before):
                decays[h, c] = decay
                growths[h, c] = growth
                chunk_pairs[h, c] = pair_here
                if c:
                    befores[h, c - 1] = before

            return at(ks, h), at(vs, h), four(b_ref), four(d_ref), keep

        def middle(i):
            if i == 0:
                @pl.when(two == 0)
                def _():
                    greet()

            if i == 3:
                @pl.when((two == 1) & (late == 0))
                def _():
                    scan_group()

        heads = [2 * two, 2 * two + 1]
        for h, result in zip(heads, key_side([head_of(h) for h in heads], masks, middle)):
            items[h] = as_item(result)

            @pl.when(h != mine)
            def _():
                item_copy(h).start()

            @pl.when(h == mine)
            def _():
                group[member] = items[h]

        return 0

    def compute_rows(h):
        q_of, k_of = at(qs, h), at(ks, h)
        for c in range(4):
            rows_q, rows_o = query_side(q_of(c), k_of(c), decays[h, c], growths[h, c], chunk_pairs[h, c],
                                        befores[h, c - 1] if c else None)
            qe[h, c * C : (c + 1) * C, :] = rows_q.astype(BF16)
            own[h, c * C : (c + 1) * C, :] = rows_o

    def scan_group():
        for j in (1, 2, 3):
            other = member ^ j
            copy_to(group.at[other], group.at[other], g_send.at[other], g_recv.at[other],
                    {"seq": base + other}).wait_recv()
        early = join(group[1], from_item(group[0]))
        late = as_item(join(group[3], from_item(group[2])))
        pairs[0] = as_item(join(late, early))
        for j in (2, 1, 3):
            pair_copy(j).start()
        group_maps[0] = group[0]
        group_maps[1] = as_item(early)
        group_maps[2] = as_item(join(group[2], early))

    def scan_pairs():
        for j in (1, 3, 2):
            pair_copy(j).wait_recv()
        at_pair = [pairs[(j + 4 - pair) % 4] for j in range(4)]
        first = from_item(at_pair[0])
        early = join(at_pair[1], first)
        late = as_item(join(at_pair[3], from_item(at_pair[2])))
        rows[line] = as_item(join(late, early))
        for j in (2, 1, 3):
            @pl.when(line + j < 4)
            def _():
                line_copy(j).start()
        eye = jnp.where(
            lax.broadcasted_iota(jnp.int32, (C, 2 * C), 0) == lax.broadcasted_iota(jnp.int32, (C, 2 * C), 1), 1.0, 0.0)
        before = jnp.where(pair == 0, eye, first)
        before = jnp.where(pair > 1, early, before)
        before = jnp.where(pair > 2, join(at_pair[2], early), before)
        for i in range(4):
            here = join(group_maps[i - 1], before) if i else before
            hi, lo = halves(here[:, :C])
            entry_maps[i * C : (i + 1) * C, :C] = hi
            entry_maps[i * C : (i + 1) * C, C:] = lo
            entry_adds[i * C : (i + 1) * C, :] = here[:, C:]

    def scan_lines():
        state[...] = jnp.zeros((C, C), F32)
        for i in range(3):
            @pl.when(line > i)
            def _():
                copy_to(rows.at[i], rows.at[i], x_send.at[line - i], x_recv.at[line - i],
                        {"seq": (seq + 16) % 64}).wait_recv()
                if i == 0:
                    state[...] = rows[0, :, 2 * C :].astype(F32)
                else:
                    state[...] = pass_state(rows[i], state[...])

        row = wide(*halves(state[...]))
        both = dot(entry_maps[...], tall(row, row))
        all_four = (both[:, :C] + both[:, C:] + entry_adds[...]).astype(BF16)
        for i in range(4):
            enters[i] = all_four[i * C : (i + 1) * C]
        for j in (1, 2, 3):
            enter_copy(j).start()
        entering[mine] = enters[member]

    def apply(h):
        @pl.when(mine != h)
        def _():
            copy_to(entering.at[h], entering.at[h], e_send.at[h], e_recv.at[h],
                    {"seq": base + swapped(h)}).wait_recv()
        rows_here = dot(qe[h], entering[h]) + own[h]
        for t in range(4):
            att[t, h] = rows_here[t * C : (t + 1) * C].astype(BF16)
        for j in (2, 1, 3):
            out_copy(h, j).start()

    lax.fori_loop(0, 2, lambda two, _: compute(two), 0)
    go_right(left).wait_recv()
    relay_right(left).start()
    go_left(right).wait_recv()
    relay_left(right).start()
    share(left, 0)
    share(right, 1)
    loads[4].wait()
    qs[...] = q_ref[...].astype(F32).reshape(2048, C)

    def step_out(h, _):
        apply(h)
        return 0

    def step(t, _):
        compute_rows(t)

        @pl.when(t == 3)
        def _():
            lax.fori_loop(0, 2, step_out, 0)

        @pl.when((t == 0) & (late == 1))
        def _():
            scan_group()

        @pl.when(t == late + 1)
        def _():
            scan_pairs()

        @pl.when(t == late + 2)
        def _():
            scan_lines()

        @pl.when(t == 1)
        def _():
            relay_right(across).wait_recv()
            relay_left(across).wait_recv()
            share(across, 2)

        @pl.when(t == 2)
        def _():
            share_x(left, 0)
            share_x(right, 1)

        return 0

    lax.fori_loop(0, 4, step, 0)

    lax.fori_loop(2, 4, step_out, 0)

    share_x(across, 2)
    go_right(head).wait_send()
    go_left(head).wait_send()
    relay_right(left).wait_send()
    relay_left(right).wait_send()
    for j in (1, 2, 3):
        item_copy(swapped(member ^ j)).wait_send()
        pair_copy(j).wait_send()
        enter_copy(j).wait_send()

        @pl.when(line + j < 4)
        def _():
            line_copy(j).wait_send()

    def settle(of, i):
        go_next(of, i).wait_send()
        go_last(of, i).wait_send()
        for k, at_block in ((0, block), (3, block_x)):
            over(of, i + k, at_block).wait_send()
            over(of, i + k, (at_block + 2) % 4).wait_recv()

    def product(heads, steps, cols):
        rows_in = jnp.concatenate(
            [att[head, h] if j == 0 else arrived[j, h] for j in steps for h in heads], axis=1)
        rows_w = jnp.concatenate(
            [weight[(head + 4 - j) % 4, h, :, cols] for j in steps for h in heads], axis=0)
        return dot(rows_in, rows_w)

    settle(left, 0)
    settle(right, 1)
    for h in range(3):
        for j in (1, 3, 2):
            out_copy(h, j).wait()
    for n in range(4):
        total[:, n * 512 : (n + 1) * 512] = product((0, 1, 2), (0, 1, 3), slice(n * 512, (n + 1) * 512))
    for j in (1, 3, 2):
        out_copy(3, j).wait()
    for n in range(4):
        cols = slice(n * 512, (n + 1) * 512)
        total[:, cols] = total[:, cols] + product((3,), (0, 1, 3), cols)
    settle(across, 2)
    for n in range(4):
        cols = slice(n * 512, (n + 1) * 512)
        out_ref[:, cols] = (total[:, cols] + product((0, 1, 2, 3), (2,), cols)).astype(BF16)


def layer(q, k, v, b, d, w):
    vmem = pl.BlockSpec(memory_space=pltpu.VMEM)
    dma = pltpu.SemaphoreType.DMA
    return pl.pallas_call(
        layer_kernel,
        out_shape=jax.ShapeDtypeStruct((128, 2048), BF16),
        in_specs=[pl.BlockSpec(memory_space=pltpu.HBM)] * 6,
        out_specs=vmem,
        scratch_shapes=[pltpu.VMEM((512, 4, C), BF16)] * 3 + [pltpu.VMEM((4, 512), F32)] * 2 + [
            pltpu.VMEM((7, C, C), BF16),
            pltpu.VMEM((2048, C), F32),
            pltpu.VMEM((2048, C), F32),
            pltpu.VMEM((2048, C), F32),
            pltpu.VMEM((4, 4, C, C), F32),
            pltpu.VMEM((4, 4, C, 1), F32),
            pltpu.VMEM((4, 4, C, 2 * C), F32),
            pltpu.VMEM((4, 3, C, 2 * C), F32),
            pltpu.VMEM((4, 512, C), BF16),
            pltpu.VMEM((4, 512, C), F32),
            pltpu.VMEM((4, C, 3 * C), BF16),
            pltpu.VMEM((4, C, 3 * C), BF16),
            pltpu.VMEM((4, C, 3 * C), BF16),
            pltpu.VMEM((4, C, 3 * C), BF16),
            pltpu.VMEM((4, C, C), BF16),
            pltpu.VMEM((4, C, C), BF16),
            pltpu.VMEM((4, 4, C, C), BF16),
            pltpu.VMEM((4, 4, C, C), BF16),
            pltpu.VMEM((4, 4, C, 2048), BF16),
            pltpu.VMEM((C, 2048), F32),
            pltpu.VMEM((3, C, 3 * C), BF16),
            pltpu.VMEM((4 * C, 2 * C), BF16),
            pltpu.VMEM((4 * C, C), F32),
            pltpu.VMEM((C, C), F32),
            dma((5,)), dma, dma((16,)), dma((16,)),
        ] + [dma((4,))] * 8 + [dma((4, 4))] * 2,
        compiler_params=pltpu.CompilerParams(
            collective_id=0, has_side_effects=True, vmem_limit_bytes=40 * 2**20),
    )(q, k, v, b, d, w)


def body(query, key, value, beta, log_decay, out_weight):
    stay = lambda a: pltpu.with_memory_space_constraint(a, pltpu.HBM)
    return layer(stay(query), stay(key), stay(value), stay(beta), stay(log_decay), stay(out_weight.reshape(4, C, 2048)))


def solution(mesh):
    in_specs = (
        P("seq", "head", None),
        P("seq", "head", None),
        P("seq", "head", None),
        P("head", "seq"),
        P("head", "seq"),
        P("head", None),
    )
    out_specs = P(("seq", "head"), None)
    return jax.shard_map(body, mesh=mesh, in_specs=in_specs, out_specs=out_specs, check_vma=False)
```
